32 devices in a mesh: groups: 2 (over y), lists: 4 (over z), sub: 4 (over x, core).
Axes of the slice: x: 2, y: 2, z: 4, core: 2. Of those that a mesh axis runs over, the one named last changes fastest.
Arguments:
- passages: bfloat16 [4096, 1024], P(('groups', 'lists', 'sub')), parts along dimension 0, may hold values from -6 to 6
- rotation: bfloat16 [1024, 1024], replicated, may hold values from -0.1875 to 0.1875
- centroids: bfloat16 [65536, 1024], P('lists', 'sub'), may hold values from -6 to 6
- list_slot: int32 [131072], P('groups'), parts along dimension 0, may hold values from 0 to 65535, as said below
- list_ids: int32 [4096], P(('groups', 'lists', 'sub')), parts along dimension 0, may hold values from 0 to 65535, as said below
- codes: int32 [4096, 128], P(('groups', 'lists', 'sub')), parts along dimension 0, may hold values from 0 to 255
- codebook: bfloat16 [128, 2048], P('sub'), may hold values from -6 to 6
Outputs:
- recon_error: bfloat16 [4096, 1024], P(('groups', 'lists', 'sub')), parts along dimension 0
- new_codebook: float32 [256, 2048], P(('groups', 'sub'), 'lists'), parts along dimension 0
The draws below stay inside these ranges and needn't reach their ends.
There are 2 independent parts, one for each index of `groups`. The reference program is written for one: setup_inputs(seed, part) draws one part's arguments, and reference() takes and returns one part's arrays. A program takes and returns all parts, laid end to end along the dimension named above; an argument that names none is the same for every part. Nothing has to cross between parts.
Inputs may be any that keep to these rules, and one draw needn't show every extreme that they name: `list_slot`: A permutation: every table row holds exactly one list. The owner of passage r is list_slot[list_ids[r]] // 16384. In each aligned block of 128 passages (the passages of one device) no owner gets more than 64; one owner, the same for every block of a slab, gets exactly 64 in every block, and a second owner, drawn per block, gets exactly 64 too.
All inputs are finite; a program needn't handle non-finite values.
Results may differ from the reference program's by a relative error of at most 0.0046.
Values may be sent and summed in bfloat16 or wider, within the bound.
No kernel may reach another device: no remote copies, remote signals or barrier semaphores. Data moves between devices by JAX's collectives and lax.ppermute only.
A program may use at most 128 MiB of HBM per device.

```python
import jax
import jax.numpy as jnp
from jax import lax

D = 1024
M = 128
K = 256
LISTS = 65536
ROW_DEV = 128
DS = 8
CAP = 64
ROWS = 2048
N_LISTS = 4
N_SUB = 4


def list_layout(key):
    ordering = jax.random.permutation(jax.random.fold_in(key, 101), LISTS).astype(jnp.int32)
    inverse = jnp.argsort(ordering, stable=True).astype(jnp.int32)
    return (ordering, inverse)


def draw_list_slot(key, part):
    ordering, inverse = list_layout(key)
    return ordering


def draw_list_ids(key, part):
    ordering, inverse = list_layout(key)
    key = jax.random.fold_in(key, 7)
    block_count = N_LISTS * N_SUB
    lists_held = LISTS // N_LISTS
    hot_owner = jax.random.randint(jax.random.fold_in(key, 1), (), 0, N_LISTS)
    second = (hot_owner + 1 + jax.random.randint(jax.random.fold_in(key, 2), (block_count,), 0, N_LISTS - 1)) % N_LISTS
    block_keys = jax.random.split(jax.random.fold_in(key, 3), block_count)
    turns = jax.vmap(lambda block_key: jax.random.permutation(block_key, ROW_DEV))(block_keys).astype(jnp.int32)
    spread = jnp.maximum(turns - 2 * CAP, 0) % (N_LISTS - 2)
    lower = jnp.minimum(hot_owner, second)[:, None]
    upper = jnp.maximum(hot_owner, second)[:, None]
    others = spread + (spread >= lower).astype(jnp.int32)
    others = others + (others >= upper).astype(jnp.int32)
    owner_ids = jnp.where(turns < CAP, hot_owner, jnp.where(turns < 2 * CAP, second[:, None], others))
    within = jax.random.randint(jax.random.fold_in(key, 4), (block_count, ROW_DEV), 0, lists_held)
    table_rows = owner_ids * lists_held + within
    return inverse[table_rows].reshape(ROWS).astype(jnp.int32)


def plant(drawn, key, smallest, top_value):
    dims = drawn.shape
    index_at = [jax.random.randint(jax.random.fold_in(key, axis), (), 0, dims[axis]) for axis in range(len(dims))]
    drawn = drawn.at[tuple(index_at)].set(smallest)
    longest = dims.index(max(dims))
    index_at[longest] = (index_at[longest] + 1) % dims[longest]
    return drawn.at[tuple(index_at)].set(top_value)


def level_of(stream_key, extent, pieces, low, high):
    loudness, own = 1.0, jax.random.fold_in(stream_key, 6)
    for axis_at, parts in pieces:
        steps = jnp.exp(jax.random.uniform(jax.random.fold_in(own, axis_at), (parts,), jnp.float32, low / len(pieces), high / len(pieces)))
        loudness = loudness * jnp.repeat(steps, extent[axis_at] // parts).reshape([-1 if axis == axis_at else 1 for axis in range(len(extent))])
    return loudness


def bell_draw(stream_key, extent, width, bound, cuts=(), kind=jnp.bfloat16):
    gain = level_of(stream_key, extent, cuts, -0.22, 0.18) if cuts else 1.0
    result = jax.random.normal(stream_key, extent, jnp.float32) * width * gain
    return jnp.minimum(jnp.maximum(result, -bound), bound).astype(kind)


def setup_inputs(seed: int = 0, part: int = 0) -> dict:
    key_of = jax.random.split(jax.random.key(seed), 8)
    part_keys = jax.random.split(jax.random.fold_in(key_of[7], part), 8)
    return {
        "passages": bell_draw(part_keys[0], (ROWS, D), 1.0, 6.0, ((0, 16),)),
        "rotation": bell_draw(key_of[1], (D, D), D ** -0.5, 0.1875),
        "centroids": bell_draw(key_of[2], (LISTS, D), 1.0, 6.0, ((0, 4), (1, 4))),
        "list_slot": draw_list_slot(jax.random.fold_in(jax.random.fold_in(key_of[7], part), 71), part),
        "list_ids": draw_list_ids(jax.random.fold_in(jax.random.fold_in(key_of[7], part), 71), part),
        "codes": plant(jax.random.randint(part_keys[5], (ROWS, M), 0, K), jax.random.fold_in(part_keys[5], 1), 0, K - 1).astype(jnp.int32),
        "codebook": bell_draw(key_of[6], (M, K * DS), 1.0, 6.0, ((0, 4),)),
    }


def reference(passages, rotation, centroids, list_slot, list_ids, codes, codebook):
    depth_cols = D // M
    rotated = jnp.dot(passages, rotation, preferred_element_type=jnp.float32).astype(jnp.bfloat16)
    table_row = list_slot[list_ids].astype(jnp.int32)
    anchors = centroids[table_row]
    residual = (rotated.astype(jnp.float32) - anchors.astype(jnp.float32)).astype(jnp.bfloat16)

    def one_subspace(subspace):
        slab = lax.dynamic_slice_in_dim(residual, subspace * depth_cols, depth_cols, 1).astype(jnp.float32)
        chosen = lax.dynamic_slice_in_dim(codes, subspace, 1, 1)[:, 0]
        block_sums = jax.ops.segment_sum(slab, chosen, num_segments=K)
        block_count = jax.ops.segment_sum(jnp.ones((ROWS,), jnp.float32), chosen, num_segments=K)
        return block_sums, block_count

    code_sums, code_count = lax.map(one_subspace, jnp.arange(M, dtype=jnp.int32))
    book_words = codebook.astype(jnp.float32).reshape(M, K, depth_cols)
    new_codebook = ((code_sums + book_words) / (code_count[:, :, None] + 1.0)).reshape(M, K * depth_cols)
    picked = book_words[jnp.arange(M, dtype=jnp.int32)[None, :], codes]
    rebuilt = (anchors.astype(jnp.float32) + picked.reshape(ROWS, D)).astype(jnp.bfloat16)
    restored = lax.dot_general(rebuilt, rotation, (((1,), (1,)), ((), ())), preferred_element_type=jnp.float32)
    recon_error = (passages.astype(jnp.float32) - restored).astype(jnp.bfloat16)
    return recon_error, new_codebook
```

```python
import functools

import jax
import jax.numpy as jnp
from jax import lax
from jax.experimental import pallas as pl
from jax.experimental.pallas import tpu as pltpu
from jax.sharding import PartitionSpec as P

BF16 = jnp.bfloat16
F32 = jnp.float32
VMEM_LIMIT = 48 * 1024 * 1024
DIRECT_LISTS = 4


def call(kernel, out_shape, flops, nbytes, *args):
    whole = lambda: pl.BlockSpec(memory_space=pltpu.VMEM)
    return pl.pallas_call(
        kernel,
        out_shape=out_shape,
        in_specs=[whole() for _ in args],
        out_specs=jax.tree.map(lambda _: whole(), out_shape),
        compiler_params=pltpu.CompilerParams(vmem_limit_bytes=VMEM_LIMIT),
        cost_estimate=pl.CostEstimate(flops=flops, bytes_accessed=nbytes, transcendentals=0),
    )(*args)


def strict_before(width):
    row = lax.broadcasted_iota(jnp.int32, (width, width), 0)
    col = lax.broadcasted_iota(jnp.int32, (width, width), 1)
    return (row < col).astype(F32).astype(BF16)


def rotate_kernel(subs, passages_ref, rotation_ref, codes_ref, out_ref):
    rows, model = passages_ref.shape
    width = model // subs
    spaces = codes_ref.shape[1] // subs
    halves = width // rows
    tail = spaces // halves
    codes_t = jnp.transpose(codes_ref[...].astype(F32)).astype(BF16)
    for at in range(subs):
        out_ref[at, :rows, :] = jnp.dot(
            passages_ref[...],
            rotation_ref[:, at * width : (at + 1) * width],
            preferred_element_type=F32,
        ).astype(BF16)
        for half in range(halves):
            start = at * spaces + half * tail
            out_ref[at, rows:, half * rows : (half + 1) * rows] = codes_t[start : start + tail]


def slots_kernel(held, lists, direct, rows_ref, *outs):
    blocks, rows = rows_ref.shape
    me = lax.axis_index("lists")
    subs = blocks // lists
    cap = outs[0].shape[1]
    local = rows_ref[...] - me * held
    mine = jnp.logical_and(local >= 0, local < held)
    flags = mine.astype(F32)
    rank = jnp.dot(flags.astype(BF16), strict_before(rows), preferred_element_type=F32)
    rank = jnp.where(mine, rank, -1.0)
    local = jnp.where(mine, local, 0)
    high = (local // 128).astype(F32)
    low = (local % 128).astype(F32)
    slot = lax.broadcasted_iota(jnp.int32, (cap, rows), 0).astype(F32)
    for block in range(blocks):
        chosen = (slot == rank[block : block + 1, :]).astype(F32).astype(BF16)
        pair = jnp.concatenate(
            [
                jnp.broadcast_to(high[block : block + 1, :], (8, rows)),
                jnp.broadcast_to(low[block : block + 1, :], (8, rows)),
            ],
            axis=0,
        ).astype(BF16)
        found = lax.dot_general(
            pair, chosen, (((1,), (1,)), ((), ())), preferred_element_type=F32
        )
        row = (found[0:1, :] * 128.0 + found[8:9, :]).astype(jnp.int32)
        if direct:
            place = (block // subs) ^ me
            for step in range(lists):

                @pl.when(place == step)
                def _():
                    outs[step][block % subs : block % subs + 1, :] = row
        else:
            outs[0][block : block + 1, :] = row


def lookup_kernel(held, lists, direct, cap, rows_ref, message_ref, words_ref, picked_ref, slot_ref, codes_ref, tally_ref):
    subs, _, width = message_ref.shape
    rows = rows_ref.shape[1]
    spaces = codes_ref.shape[0]
    depth = width // spaces
    words = words_ref.shape[1]
    halves = width // rows
    tail = spaces // halves
    me = lax.axis_index("lists")
    tables = rows_ref[pl.ds(pl.multiple_of(me * subs, subs), subs), :]
    owners = tables // held
    rank = jnp.zeros((subs, rows), F32)
    flags = [(owners == at).astype(F32) for at in range(lists)]
    stacked = jnp.concatenate(flags, axis=0)
    before = jnp.dot(stacked.astype(BF16), strict_before(rows), preferred_element_type=F32)
    for at in range(lists):
        rank = rank + flags[at] * before[at * subs : (at + 1) * subs]
    place = (owners ^ me) if direct else owners
    slot = place.astype(F32) * cap + rank
    slot_ref[...] = jnp.transpose(jnp.concatenate([slot] * (rows // subs), axis=0))
    for at in range(subs):
        for half in range(halves):
            codes_ref[half * tail : (half + 1) * tail, at * rows : (at + 1) * rows] = message_ref[
                at, rows:, half * rows : (half + 1) * rows
            ].astype(F32)
    parts = []
    for space in range(spaces):
        line = codes_ref[space : space + 1, :].astype(jnp.int32)
        table = words_ref[space * depth : (space + 1) * depth, :]
        cells = []
        for at in range(subs):
            index = jnp.broadcast_to(line[:, at * rows : (at + 1) * rows], (depth, rows))
            value = None
            for piece in range(words // 128):
                got = jnp.take_along_axis(
                    table[:, piece * 128 : (piece + 1) * 128], index & 127, axis=1
                )
                value = got if value is None else jnp.where(index >= piece * 128, got, value)
            cells.append(value)
        parts.append(jnp.concatenate(cells, axis=1))
    picked_ref[...] = jnp.transpose(jnp.concatenate(parts, axis=0)).astype(BF16)
    tally = jnp.zeros((words, 128), F32)
    word = lax.broadcasted_iota(jnp.int32, (words, subs * rows), 0).astype(F32)
    lane = lax.broadcasted_iota(jnp.int32, (subs * rows, 128), 1)
    for space in range(spaces):
        hot = (word == codes_ref[space : space + 1, :]).astype(F32).astype(BF16)
        tally = tally + jnp.dot(
            hot, (lane == space).astype(F32).astype(BF16), preferred_element_type=F32
        )
    tally_ref[...] = tally.astype(BF16)


def place_kernel(own, slot_ref, message_ref, picked_ref, *refs):
    pieces, (rebuilt_ref, residual_ref) = refs[:-2], refs[-2:]
    subs, _, width = message_ref.shape
    rows = slot_ref.shape[0]
    total = sum(piece.shape[1] for piece in pieces)
    column = lax.broadcasted_iota(jnp.int32, (rows, total), 1).astype(F32)
    for at in range(subs):
        chosen = (column == slot_ref[:, at : at + 1]).astype(F32).astype(BF16)
        centre = jnp.zeros((rows, width), F32)
        start = 0
        stacked = jnp.concatenate([piece[at] for piece in pieces], axis=0)
        centre = jnp.dot(chosen, stacked, preferred_element_type=F32)
        span = slice(at * rows, (at + 1) * rows)
        rebuilt_ref[at] = (centre + picked_ref[span, :].astype(F32)).astype(BF16)
        residual_ref[span, :] = (message_ref[at, :rows, :].astype(F32) - centre).astype(BF16)


def sums_kernel(lists, codes_ref, residual_ref, tally_ref, out_ref):
    spaces, rows = codes_ref.shape
    width = residual_ref.shape[1]
    words = tally_ref.shape[0]
    depth = width // spaces
    share = words // lists
    word = lax.broadcasted_iota(jnp.int32, (words, rows), 0).astype(F32)
    owner = lax.broadcasted_iota(jnp.int32, (rows, width), 1) // depth
    residual = residual_ref[...]
    total = jnp.zeros((words, width), F32)
    for space in range(spaces):
        hot = (word == codes_ref[space : space + 1, :]).astype(F32).astype(BF16)
        part = jnp.where(owner == space, residual, jnp.zeros_like(residual))
        total = total + jnp.dot(hot, part, preferred_element_type=F32)
    total = total.astype(BF16)
    tally = tally_ref[...]
    for at in range(lists):
        out_ref[at, :, :width] = total[at * share : (at + 1) * share]
        out_ref[at, :, width:] = tally[at * share : (at + 1) * share]


def refine_kernel(spaces, direct, codebook_ref, *refs):
    pieces, (out_ref, turned_ref) = refs[:-2], refs[-2:]
    total = None
    for piece in pieces:
        if direct:
            value = piece[...].astype(F32)
        else:
            value = jnp.sum(piece[...].astype(F32), axis=0)
        total = value if total is None else total + value
    share = total.shape[0]
    width = total.shape[1] - 128
    depth = width // spaces
    span = share * depth
    turned = jnp.transpose(total)
    turned_ref[...] = turned[:width, :]
    tally = turned[width : width + spaces, :]
    word = lax.broadcasted_iota(jnp.int32, (share, span), 0)
    cell = lax.broadcasted_iota(jnp.int32, (share, span), 1)

    def spread(value, table):
        high = value.astype(BF16)
        rest = value - high.astype(F32)
        low = rest.astype(BF16)
        return jnp.dot(high, table, preferred_element_type=F32) + jnp.dot(
            low, table, preferred_element_type=F32
        )

    sums = jnp.zeros((spaces, span), F32)
    for at in range(depth):
        table = (cell == word * depth + at).astype(F32).astype(BF16)
        sums = sums + spread(turned_ref[pl.ds(at, spaces, stride=depth), :], table)
    counts = spread(tally, (cell // depth == word).astype(F32).astype(BF16))
    me = lax.axis_index("lists")
    if span % 128 == 0:
        prior = codebook_ref[:, pl.ds(pl.multiple_of(me * span, span), span)].astype(F32)
    else:
        prior = jnp.zeros((spaces, span), F32)
        for at in range(codebook_ref.shape[1] // span):
            block = codebook_ref[:, at * span : (at + 1) * span].astype(F32)
            prior = prior + jnp.where(me == at, block, 0.0)
    out_ref[...] = (sums + prior) / (counts + 1.0)


def restore_kernel(direct, passages_ref, rotation_ref, *refs):
    pieces, out_ref = refs[:-1], refs[-1]
    me = lax.axis_index("sub")
    if direct:
        blocks = [piece[...] for piece in pieces]
    else:
        blocks = [pieces[0][at] for at in range(pieces[0].shape[0])]
    width = blocks[0].shape[1]
    total = None
    for at, block in enumerate(blocks):
        start = (me ^ at) * width if direct else at * width
        if direct:
            start = pl.multiple_of(start, width)
        value = lax.dot_general(
            block,
            rotation_ref[:, pl.ds(start, width)],
            (((1,), (1,)), ((), ())),
            preferred_element_type=F32,
        )
        total = value if total is None else total + value
    out_ref[...] = (passages_ref[...].astype(F32) - total).astype(BF16)


def swap(value, axis, step):
    count = lax.axis_size(axis)
    return lax.ppermute(value, axis, [(at, at ^ step) for at in range(count)])


def pick(value, index):
    return lax.dynamic_index_in_dim(value, index, 0, keepdims=False)


def body(passages, rotation, centroids, list_slot, list_ids, codes, codebook):
    lists = lax.axis_size("lists")
    subs = lax.axis_size("sub")
    rows, model = passages.shape
    held, width = centroids.shape
    cap = 2 * rows // lists
    spaces = codebook.shape[0]
    depth = width // spaces
    words = codebook.shape[1] // depth
    share = words // lists
    direct = lists <= DIRECT_LISTS
    me_list = lax.axis_index("lists")
    me_sub = lax.axis_index("sub")
    shape = jax.ShapeDtypeStruct

    tables = list_slot.at[list_ids].get(mode="promise_in_bounds")
    tables = lax.all_to_all(
        jnp.broadcast_to(tables[None, None, :], (lists * subs, 1, rows)),
        ("lists", "sub"),
        split_axis=0,
        concat_axis=0,
        tiled=True,
    ).reshape(lists * subs, rows)

    halves = width // rows
    message = call(
        functools.partial(rotate_kernel, subs),
        shape((subs, rows + spaces // halves, width), BF16),
        2 * rows * model * model,
        2 * model * model + 4 * rows * model,
        passages,
        rotation,
        codes,
    )
    message = lax.all_to_all(message, "sub", split_axis=0, concat_axis=0, tiled=True)

    idx = call(
        functools.partial(slots_kernel, held, lists, direct),
        [shape((subs, cap), jnp.int32)] * lists if direct else [shape((lists * subs, cap), jnp.int32)],
        10_000_000,
        100_000,
        tables,
    )
    fetch = lambda at: centroids.at[at].get(mode="promise_in_bounds")
    if direct:
        pieces = [fetch(idx[0])] + [
            swap(fetch(idx[step]), "lists", step) for step in range(1, lists)
        ]
    else:
        found = lax.all_to_all(
            fetch(idx[0]).reshape(lists, subs * cap, width), "lists", 0, 0, tiled=True
        )
        found = found.reshape(lists, subs, cap, width)
        pieces = [jnp.swapaxes(found, 0, 1).reshape(subs, lists * cap, width)]

    word_table = (
        codebook.astype(F32).reshape(spaces, words, depth).transpose(0, 2, 1).reshape(width, words)
    )
    picked, slot, codes_t, tally = call(
        functools.partial(lookup_kernel, held, lists, direct, cap),
        [
            shape((subs * rows, width), BF16),
            shape((rows, rows), F32),
            shape((spaces, subs * rows), F32),
            shape((words, 128), BF16),
        ],
        1_000_000_000,
        2_000_000,
        tables,
        message,
        word_table,
    )
    rebuilt, residual = call(
        functools.partial(place_kernel, me_list),
        [shape((subs, rows, width), BF16), shape((subs * rows, width), BF16)],
        300_000_000,
        2_000_000,
        slot,
        message,
        picked,
        *pieces,
    )
    if subs <= DIRECT_LISTS:
        rebuilt = [pick(rebuilt, me_sub)] + [
            swap(pick(rebuilt, me_sub ^ step), "sub", step) for step in range(1, subs)
        ]
    else:
        rebuilt = [lax.all_to_all(rebuilt, "sub", 0, 0, tiled=True)]
    sums = call(
        functools.partial(sums_kernel, lists),
        shape((lists, share, width + 128), BF16),
        2_000_000_000,
        1_000_000,
        codes_t,
        residual,
        tally,
    )
    if direct:
        sums = [pick(sums, me_list)] + [
            swap(pick(sums, me_list ^ step), "lists", step) for step in range(1, lists)
        ]
    else:
        sums = [lax.all_to_all(sums, "lists", 0, 0, tiled=True)]
    recon_error = call(
        functools.partial(restore_kernel, subs <= DIRECT_LISTS),
        shape((rows, model), BF16),
        2 * rows * model * model,
        2 * model * model + 4 * rows * model,
        passages,
        rotation,
        *rebuilt,
    )
    new_codebook = pl.pallas_call(
        functools.partial(refine_kernel, spaces, direct),
        out_shape=shape((spaces, share * depth), F32),
        in_specs=[pl.BlockSpec(memory_space=pltpu.VMEM)] * (1 + len(sums)),
        out_specs=pl.BlockSpec(memory_space=pltpu.VMEM),
        scratch_shapes=[pltpu.VMEM((width, share), F32)],
        compiler_params=pltpu.CompilerParams(vmem_limit_bytes=VMEM_LIMIT),
        cost_estimate=pl.CostEstimate(flops=100_000_000, bytes_accessed=500_000, transcendentals=0),
    )(codebook, *sums)
    return (recon_error, new_codebook)


def solution(mesh):
    return jax.shard_map(
        body,
        mesh=mesh,
        in_specs=(
            P(("groups", "lists", "sub"), None),
            P(),
            P("lists", "sub"),
            P("groups"),
            P(("groups", "lists", "sub")),
            P(("groups", "lists", "sub"), None),
            P("sub", None),
        ),
        out_specs=(P(("groups", "lists", "sub"), None), P(("groups", "sub"), "lists")),
        check_vma=False,
    )
```

```python
import functools

import jax
import jax.numpy as jnp
from jax import lax
from jax.experimental import pallas as pl
from jax.experimental.pallas import tpu as pltpu
from jax.sharding import PartitionSpec as P

BF16 = jnp.bfloat16
F32 = jnp.float32
VMEM_LIMIT = 32 * 1024 * 1024
DIRECT = 4


def call(kernel, out_shape, flops, nbytes, *args, scratch=()):
    whole = lambda: pl.BlockSpec(memory_space=pltpu.VMEM)
    return pl.pallas_call(
        kernel,
        out_shape=out_shape,
        in_specs=[whole() for _ in args],
        out_specs=jax.tree.map(lambda _: whole(), out_shape),
        scratch_shapes=list(scratch),
        compiler_params=pltpu.CompilerParams(vmem_limit_bytes=VMEM_LIMIT),
        cost_estimate=pl.CostEstimate(flops=flops, bytes_accessed=nbytes, transcendentals=0),
    )(*args)


def strict_before(width):
    row = lax.broadcasted_iota(jnp.int32, (width, width), 0)
    col = lax.broadcasted_iota(jnp.int32, (width, width), 1)
    return (row < col).astype(F32).astype(BF16)


def rotate_kernel(subs, direct, passages_ref, rotation_ref, codes_ref, *refs):
    outs, turned_ref = refs[:-1], refs[-1]
    rows, model = passages_ref.shape
    width = model // subs
    spaces = codes_ref.shape[1] // subs
    halves = width // rows
    tail = spaces // halves
    me = lax.axis_index("sub")
    turned_ref[...] = jnp.transpose(codes_ref[...].astype(F32))
    for step in range(subs):
        at = (me ^ step) if direct else step
        out = outs[step] if direct else outs[0].at[step]
        columns = pl.ds(pl.multiple_of(at * width, width), width)
        out[:rows, :] = jnp.dot(
            passages_ref[...], rotation_ref[:, columns], preferred_element_type=F32
        ).astype(BF16)
        for half in range(halves):
            start = pl.multiple_of(at * spaces + half * tail, tail)
            out[rows:, half * rows : (half + 1) * rows] = turned_ref[pl.ds(start, tail), :].astype(
                BF16
            )


def fetch_kernel(held, lists, count, *refs):
    rows_refs, centroids_ref, outs = refs[:count], refs[count], refs[count + 1 : -3]
    index_ref, scalar_ref, sem = refs[-3:]
    blocks, cap = index_ref.shape
    rows = rows_refs[0].shape[1]
    group = min(cap, 16)
    me = lax.axis_index("lists")
    local = jnp.concatenate([ref[...] for ref in rows_refs], axis=0) - me * held
    mine = jnp.logical_and(local >= 0, local < held)
    flags = mine.astype(F32)
    rank = jnp.dot(flags.astype(BF16), strict_before(rows), preferred_element_type=F32)
    rank = jnp.where(mine, rank, -1.0)
    local = jnp.where(mine, local, 0)
    high = (local // 128).astype(F32)
    low = (local % 128).astype(F32)
    slot = lax.broadcasted_iota(jnp.int32, (cap, rows), 0).astype(F32)
    for block in range(blocks):
        chosen = (slot == rank[block : block + 1, :]).astype(F32).astype(BF16)
        pair = jnp.concatenate(
            [
                jnp.broadcast_to(high[block : block + 1, :], (8, rows)),
                jnp.broadcast_to(low[block : block + 1, :], (8, rows)),
            ],
            axis=0,
        ).astype(BF16)
        found = lax.dot_general(
            pair, chosen, (((1,), (1,)), ((), ())), preferred_element_type=F32
        )
        row = (found[0:1, :] * 128.0 + found[8:9, :]).astype(jnp.int32)
        index_ref[block : block + 1, :] = row
    move = pltpu.make_async_copy(index_ref, scalar_ref, sem)
    move.start()
    within = lax.broadcasted_iota(jnp.int32, (blocks, cap), 1) % group
    spot = (within * 16 + index_ref[...] % 16).astype(F32)
    pad = max(128 // blocks, 1)
    spot = jnp.transpose(jnp.concatenate([spot] * pad, axis=0))
    lane = lax.broadcasted_iota(jnp.int32, (cap, group * 16), 1).astype(F32)
    move.wait()
    for block in range(blocks):
        chosen = (lane == spot[:, block : block + 1]).astype(F32).astype(BF16)
        for start in range(0, cap, group):
            tiles = []
            for at in range(start, start + group):
                base = pl.multiple_of((scalar_ref[block, at] // 16) * 16, 16)
                tiles.append(centroids_ref[pl.ds(base, 16), :])
            value = jnp.dot(
                chosen[start : start + group],
                jnp.concatenate(tiles, axis=0),
                preferred_element_type=F32,
            ).astype(BF16)
            per = blocks // len(outs)
            outs[block // per][block % per, start : start + group, :] = value


def lookup_kernel(held, lists, direct, cap, count, rows_ref, words_ref, *refs):
    messages, (picked_ref, slot_ref, codes_ref, tally_ref) = refs[:count], refs[count:]
    if not direct:
        messages = [messages[0].at[at] for at in range(messages[0].shape[0])]
    subs = len(messages)
    width = messages[0].shape[1]
    rows = rows_ref.shape[1]
    spaces = codes_ref.shape[0]
    depth = width // spaces
    words = words_ref.shape[1]
    halves = width // rows
    tail = spaces // halves
    me = lax.axis_index("lists")
    if direct:
        tables = rows_ref[...]
    else:
        tables = rows_ref[pl.ds(pl.multiple_of(me * subs, subs), subs), :]
    owners = tables // held
    rank = jnp.zeros((subs, rows), F32)
    flags = [(owners == at).astype(F32) for at in range(lists)]
    stacked = jnp.concatenate(flags, axis=0)
    before = jnp.dot(stacked.astype(BF16), strict_before(rows), preferred_element_type=F32)
    for at in range(lists):
        rank = rank + flags[at] * before[at * subs : (at + 1) * subs]
    place = (owners ^ me) if direct else owners
    slot = place.astype(F32) * cap + rank
    slot_ref[...] = jnp.transpose(jnp.concatenate([slot] * (rows // subs), axis=0))
    for at in range(subs):
        for half in range(halves):
            codes_ref[half * tail : (half + 1) * tail, at * rows : (at + 1) * rows] = messages[at][
                rows:, half * rows : (half + 1) * rows
            ].astype(F32)
    parts = []
    for space in range(spaces):
        line = codes_ref[space : space + 1, :].astype(jnp.int32)
        table = words_ref[space * depth : (space + 1) * depth, :]
        cells = []
        for at in range(subs):
            index = jnp.broadcast_to(line[:, at * rows : (at + 1) * rows], (depth, rows))
            value = None
            for piece in range(words // 128):
                got = jnp.take_along_axis(
                    table[:, piece * 128 : (piece + 1) * 128], index & 127, axis=1
                )
                value = got if value is None else jnp.where(index >= piece * 128, got, value)
            cells.append(value)
        parts.append(jnp.concatenate(cells, axis=1))
    picked_ref[...] = jnp.transpose(jnp.concatenate(parts, axis=0)).astype(BF16)
    tally = jnp.zeros((words, 128), F32)
    word = lax.broadcasted_iota(jnp.int32, (words, subs * rows), 0).astype(F32)
    lane = lax.broadcasted_iota(jnp.int32, (subs * rows, 128), 1)
    for space in range(spaces):
        hot = (word == codes_ref[space : space + 1, :]).astype(F32).astype(BF16)
        tally = tally + jnp.dot(
            hot, (lane == space).astype(F32).astype(BF16), preferred_element_type=F32
        )
    tally_ref[...] = tally


def place_kernel(direct, count, slot_ref, picked_ref, *refs):
    messages, refs = refs[:count], refs[count:]
    if not direct:
        messages = [messages[0].at[at] for at in range(messages[0].shape[0])]
    subs = len(messages)
    spread = subs if direct else 1
    pieces, rebuilt, residual_ref = refs[: -1 - spread], refs[-1 - spread : -1], refs[-1]
    rows = slot_ref.shape[0]
    total = sum(piece.shape[1] for piece in pieces)
    column = lax.broadcasted_iota(jnp.int32, (rows, total), 1).astype(F32)
    for at in range(subs):
        chosen = (column == slot_ref[:, at : at + 1]).astype(F32).astype(BF16)
        stacked = jnp.concatenate([piece[at] for piece in pieces], axis=0)
        centre = jnp.dot(chosen, stacked, preferred_element_type=F32)
        span = slice(at * rows, (at + 1) * rows)
        out = rebuilt[at] if direct else rebuilt[0].at[at]
        out[...] = (centre + picked_ref[span, :].astype(F32)).astype(BF16)
        residual_ref[span, :] = (messages[at][:rows, :].astype(F32) - centre).astype(BF16)


def sums_kernel(lists, direct, codes_ref, residual_ref, tally_ref, *refs):
    outs, total_ref = refs[:-1], refs[-1]
    spaces, rows = codes_ref.shape
    width = residual_ref.shape[1]
    words = tally_ref.shape[0]
    depth = width // spaces
    share = words // lists
    word = lax.broadcasted_iota(jnp.int32, (words, rows), 0).astype(F32)
    owner = lax.broadcasted_iota(jnp.int32, (rows, width), 1) // depth
    residual = residual_ref[...]
    total = jnp.zeros((words, width), F32)
    for space in range(spaces):
        hot = (word == codes_ref[space : space + 1, :]).astype(F32).astype(BF16)
        part = jnp.where(owner == space, residual, jnp.zeros_like(residual))
        total = total + jnp.dot(hot, part, preferred_element_type=F32)
    total_ref[...] = total
    me = lax.axis_index("lists")
    for step in range(lists):
        out = outs[step] if direct else outs[0].at[step]
        at = (me ^ step) if direct else step
        span = pl.ds(pl.multiple_of(at * share, share), share)
        out[:, :width] = total_ref[span, :].astype(BF16)
        out[:, width:] = tally_ref[span, :].astype(BF16)


def refine_kernel(spaces, direct, codebook_ref, *refs):
    pieces, (out_ref, turned_ref) = refs[:-2], refs[-2:]
    total = None
    for piece in pieces:
        if direct:
            value = piece[...].astype(F32)
        else:
            value = jnp.sum(piece[...].astype(F32), axis=0)
        total = value if total is None else total + value
    share = total.shape[0]
    width = total.shape[1] - 128
    depth = width // spaces
    span = share * depth
    turned = jnp.transpose(total)
    turned_ref[...] = turned[:width, :]
    tally = turned[width : width + spaces, :]
    word = lax.broadcasted_iota(jnp.int32, (share, span), 0)
    cell = lax.broadcasted_iota(jnp.int32, (share, span), 1)

    def spread(value, table):
        high = value.astype(BF16)
        rest = value - high.astype(F32)
        low = rest.astype(BF16)
        return jnp.dot(high, table, preferred_element_type=F32) + jnp.dot(
            low, table, preferred_element_type=F32
        )

    sums = jnp.zeros((spaces, span), F32)
    for at in range(depth):
        table = (cell == word * depth + at).astype(F32).astype(BF16)
        sums = sums + spread(turned_ref[pl.ds(at, spaces, stride=depth), :], table)
    counts = spread(tally, (cell // depth == word).astype(F32).astype(BF16))
    me = lax.axis_index("lists")
    if span % 128 == 0:
        prior = codebook_ref[:, pl.ds(pl.multiple_of(me * span, span), span)].astype(F32)
    else:
        prior = jnp.zeros((spaces, span), F32)
        for at in range(codebook_ref.shape[1] // span):
            block = codebook_ref[:, at * span : (at + 1) * span].astype(F32)
            prior = prior + jnp.where(me == at, block, 0.0)
    out_ref[...] = (sums + prior) / (counts + 1.0)


def restore_kernel(direct, passages_ref, rotation_ref, *refs):
    pieces, out_ref = refs[:-1], refs[-1]
    me = lax.axis_index("sub")
    if direct:
        blocks = [piece[...] for piece in pieces]
    else:
        blocks = [pieces[0][at] for at in range(pieces[0].shape[0])]
    width = blocks[0].shape[1]
    total = None
    for at, block in enumerate(blocks):
        start = (me ^ at) * width if direct else at * width
        if direct:
            start = pl.multiple_of(start, width)
        value = lax.dot_general(
            block,
            rotation_ref[:, pl.ds(start, width)],
            (((1,), (1,)), ((), ())),
            preferred_element_type=F32,
        )
        total = value if total is None else total + value
    out_ref[...] = (passages_ref[...].astype(F32) - total).astype(BF16)


def swap(value, axis, step):
    count = lax.axis_size(axis)
    return lax.ppermute(value, axis, [(at, at ^ step) for at in range(count)])


def gather_rows(table, at):
    return lax.gather(
        table,
        at[:, None],
        lax.GatherDimensionNumbers(offset_dims=(), collapsed_slice_dims=(0,), start_index_map=(0,)),
        slice_sizes=(1,),
        mode=lax.GatherScatterMode.PROMISE_IN_BOUNDS,
    )


def exchange(values, axis):
    return [values[0]] + [swap(values[step], axis, step) for step in range(1, len(values))]


def all_swap(value, axis):
    return lax.all_to_all(value, axis, split_axis=0, concat_axis=0, tiled=True)


def body(passages, rotation, centroids, list_slot, list_ids, codes, codebook):
    lists = lax.axis_size("lists")
    subs = lax.axis_size("sub")
    rows, model = passages.shape
    held, width = centroids.shape
    cap = 2 * rows // lists
    spaces = codebook.shape[0]
    depth = width // spaces
    words = codebook.shape[1] // depth
    share = words // lists
    direct = max(lists, subs) <= DIRECT
    shape = jax.ShapeDtypeStruct

    tables = gather_rows(list_slot, list_ids)
    if direct:
        tables = tables.reshape(1, rows)
        tables = jnp.concatenate(exchange([tables] * subs, "sub"), axis=0)
        tables = exchange([tables] * lists, "lists")
    else:
        tables = jnp.broadcast_to(tables[None, None, :], (lists * subs, 1, rows))
        tables = [all_swap(tables, ("lists", "sub")).reshape(lists * subs, rows)]

    pieces = call(
        functools.partial(fetch_kernel, held, lists, len(tables)),
        [shape((subs, cap, width), BF16)] * lists
        if direct
        else [shape((lists * subs, cap, width), BF16)],
        600_000_000,
        held * width * 2,
        *tables,
        centroids,
        scratch=[
            pltpu.VMEM((lists * subs, cap), jnp.int32),
            pltpu.SMEM((lists * subs, cap), jnp.int32),
            pltpu.SemaphoreType.DMA,
        ],
    )
    if direct:
        pieces = exchange(pieces, "lists")
    else:
        found = all_swap(pieces[0].reshape(lists, subs * cap, width), "lists")
        found = found.reshape(lists, subs, cap, width)
        pieces = [jnp.swapaxes(found, 0, 1).reshape(subs, lists * cap, width)]

    long = rows + spaces // (width // rows)
    messages = call(
        functools.partial(rotate_kernel, subs, direct),
        [shape((long, width), BF16)] * subs if direct else [shape((subs, long, width), BF16)],
        2 * rows * model * model,
        2 * model * model + 4 * rows * model,
        passages,
        rotation,
        codes,
        scratch=[pltpu.VMEM((codes.shape[1], rows), F32)],
    )
    messages = exchange(messages, "sub") if direct else [all_swap(messages[0], "sub")]

    word_table = (
        codebook.astype(F32).reshape(spaces, words, depth).transpose(0, 2, 1).reshape(width, words)
    )
    picked, slot, codes_t, tally = call(
        functools.partial(lookup_kernel, held, lists, direct, cap, len(messages)),
        [
            shape((subs * rows, width), BF16),
            shape((rows, rows), F32),
            shape((spaces, subs * rows), F32),
            shape((words, 128), F32),
        ],
        1_000_000_000,
        2_000_000,
        tables[0],
        word_table,
        *messages,
    )
    *rebuilt, residual = call(
        functools.partial(place_kernel, direct, len(messages)),
        ([shape((rows, width), BF16)] * subs if direct else [shape((subs, rows, width), BF16)])
        + [shape((subs * rows, width), BF16)],
        300_000_000,
        2_000_000,
        slot,
        picked,
        *messages,
        *pieces,
    )
    rebuilt = exchange(rebuilt, "sub") if direct else [all_swap(rebuilt[0], "sub")]
    sums = call(
        functools.partial(sums_kernel, lists, direct),
        [shape((share, width + 128), BF16)] * lists
        if direct
        else [shape((lists, share, width + 128), BF16)],
        2_000_000_000,
        1_000_000,
        codes_t,
        residual,
        tally,
        scratch=[pltpu.VMEM((words, width), F32)],
    )
    sums = exchange(sums, "lists") if direct else [all_swap(sums[0], "lists")]
    recon_error = call(
        functools.partial(restore_kernel, direct),
        shape((rows, model), BF16),
        2 * rows * model * model,
        2 * model * model + 4 * rows * model,
        passages,
        rotation,
        *rebuilt,
    )
    new_codebook = call(
        functools.partial(refine_kernel, spaces, direct),
        shape((spaces, share * depth), F32),
        100_000_000,
        500_000,
        codebook,
        *sums,
        scratch=[pltpu.VMEM((width, share), F32)],
    )
    return (recon_error, new_codebook)


def solution(mesh):
    return jax.shard_map(
        body,
        mesh=mesh,
        in_specs=(
            P(("groups", "lists", "sub"), None),
            P(),
            P("lists", "sub"),
            P("groups"),
            P(("groups", "lists", "sub")),
            P(("groups", "lists", "sub"), None),
            P("sub", None),
        ),
        out_specs=(P(("groups", "lists", "sub"), None), P(("groups", "sub"), "lists")),
        check_vma=False,
    )
```

```python
import functools

import jax
import jax.numpy as jnp
from jax import lax
from jax.experimental import pallas as pl
from jax.experimental.pallas import tpu as pltpu
from jax.sharding import PartitionSpec as P

BF16 = jnp.bfloat16
F32 = jnp.float32
VMEM_LIMIT = 32 * 1024 * 1024
DIRECT = 4


def call(kernel, out_shape, flops, nbytes, *args, scratch=(), loose=0):
    whole = lambda: pl.BlockSpec(memory_space=pltpu.VMEM)
    return pl.pallas_call(
        kernel,
        out_shape=out_shape,
        in_specs=[whole() for _ in args[: len(args) - loose]]
        + [pl.BlockSpec(memory_space=pl.ANY)] * loose,
        out_specs=jax.tree.map(lambda _: whole(), out_shape),
        scratch_shapes=list(scratch),
        compiler_params=pltpu.CompilerParams(vmem_limit_bytes=VMEM_LIMIT),
        cost_estimate=pl.CostEstimate(flops=flops, bytes_accessed=nbytes, transcendentals=0),
    )(*args)


def strict_before(width):
    row = lax.broadcasted_iota(jnp.int32, (width, width), 0)
    col = lax.broadcasted_iota(jnp.int32, (width, width), 1)
    return (row < col).astype(F32).astype(BF16)


def tables_kernel(ids_ref, slots_ref, out_ref):
    rows = ids_ref.shape[1]
    lines = slots_ref.shape[0]
    ids = jnp.transpose(jnp.concatenate([ids_ref[...].astype(F32)] * 128, axis=0))[:, :1]
    ids = ids.astype(jnp.int32)
    line = lax.broadcasted_iota(jnp.int32, (rows, lines), 1)
    chosen = (line == (ids >> 7)).astype(F32).astype(BF16)
    table = slots_ref[...]
    high = (table >> 8).astype(F32).astype(BF16)
    low = (table & 255).astype(F32).astype(BF16)
    found = jnp.dot(chosen, high, preferred_element_type=F32) * 256.0 + jnp.dot(
        chosen, low, preferred_element_type=F32
    )
    lane = lax.broadcasted_iota(jnp.int32, (rows, 128), 1)
    found = jnp.transpose(jnp.where(lane == (ids & 127), found, 0.0))
    out_ref[...] = jnp.sum(found, axis=0, keepdims=True).astype(jnp.int32)


def rotate_kernel(subs, direct, passages_ref, rotation_ref, codes_ref, after_ref, *refs):
    outs, turned_ref = refs[:-1], refs[-1]
    rows, model = passages_ref.shape
    width = model // subs
    spaces = codes_ref.shape[1] // subs
    halves = width // rows
    tail = spaces // halves
    me = lax.axis_index("sub")
    turned_ref[...] = jnp.transpose(codes_ref[...].astype(F32))
    for step in range(subs):
        at = (me ^ step) if direct else step
        out = outs[step] if direct else outs[0].at[step]
        columns = pl.ds(pl.multiple_of(at * width, width), width)
        out[:rows, :] = jnp.dot(
            passages_ref[...], rotation_ref[:, columns], preferred_element_type=F32
        ).astype(BF16)
        for half in range(halves):
            start = pl.multiple_of(at * spaces + half * tail, tail)
            out[rows:, half * rows : (half + 1) * rows] = turned_ref[pl.ds(start, tail), :].astype(
                BF16
            )


def fetch_kernel(held, lists, count, *refs):
    rows_refs, centroids_ref, outs = refs[:count], refs[count], refs[count + 1 : -3]
    index_ref, scalar_ref, sem = refs[-3:]
    blocks, cap = index_ref.shape
    rows = rows_refs[0].shape[1]
    group = min(cap, 16)
    me = lax.axis_index("lists")
    local = jnp.concatenate([ref[...] for ref in rows_refs], axis=0) - me * held
    mine = jnp.logical_and(local >= 0, local < held)
    flags = mine.astype(F32)
    rank = jnp.dot(flags.astype(BF16), strict_before(rows), preferred_element_type=F32)
    rank = jnp.where(mine, rank, -1.0)
    local = jnp.where(mine, local, 0)
    pad = max(128 // blocks, 1)
    rank = jnp.transpose(jnp.concatenate([rank] * pad, axis=0))
    local = jnp.transpose(jnp.concatenate([local.astype(F32)] * pad, axis=0))
    slot = lax.broadcasted_iota(jnp.int32, (rows, cap), 1).astype(F32)
    index = []
    for block in range(blocks):
        chosen = slot == rank[:, block : block + 1]
        index.append(
            jnp.sum(jnp.where(chosen, local[:, block : block + 1], 0.0), axis=0, keepdims=True)
        )
    index = jnp.concatenate(index, axis=0).astype(jnp.int32)
    index_ref[...] = index & -16
    move = pltpu.make_async_copy(index_ref, scalar_ref, sem)
    move.start()
    within = lax.broadcasted_iota(jnp.int32, (blocks, cap), 1) & (group - 1)
    spot = (within * 16 + (index & 15)).astype(F32)
    spot = jnp.transpose(jnp.concatenate([spot] * pad, axis=0))
    lane = lax.broadcasted_iota(jnp.int32, (cap, group * 16), 1).astype(F32)
    move.wait()
    for block in range(blocks):
        chosen = (lane == spot[:, block : block + 1]).astype(F32).astype(BF16)
        for start in range(0, cap, group):
            tiles = []
            for at in range(start, start + group):
                base = pl.multiple_of(scalar_ref[block, at], 16)
                tiles.append(centroids_ref[pl.ds(base, 16), :])
            value = jnp.dot(
                chosen[start : start + group],
                jnp.concatenate(tiles, axis=0),
                preferred_element_type=F32,
            ).astype(BF16)
            per = blocks // len(outs)
            outs[block // per][block % per, start : start + group, :] = value


def lookup_kernel(held, lists, direct, cap, count, rows_ref, codebook_ref, *refs):
    messages, refs = refs[:count], refs[count:]
    picked_ref, slot_ref, codes_ref, tally_ref, turned_ref, words_ref = refs
    if not direct:
        messages = [messages[0].at[at] for at in range(messages[0].shape[0])]
    subs = len(messages)
    width = messages[0].shape[1]
    rows = rows_ref.shape[1]
    spaces = codes_ref.shape[0]
    depth = width // spaces
    words = words_ref.shape[0] * 128
    halves = width // rows
    tail = spaces // halves
    me = lax.axis_index("lists")
    if direct:
        tables = rows_ref[...]
    else:
        tables = rows_ref[pl.ds(pl.multiple_of(me * subs, subs), subs), :]
    owners = tables // held
    rank = jnp.zeros((subs, rows), F32)
    flags = [(owners == at).astype(F32) for at in range(lists)]
    stacked = jnp.concatenate(flags, axis=0)
    before = jnp.dot(stacked.astype(BF16), strict_before(rows), preferred_element_type=F32)
    for at in range(lists):
        rank = rank + flags[at] * before[at * subs : (at + 1) * subs]
    place = (owners ^ me) if direct else owners
    slot = place.astype(F32) * cap + rank
    slot_ref[...] = jnp.transpose(jnp.concatenate([slot] * (rows // subs), axis=0))
    for at in range(subs):
        for half in range(halves):
            codes_ref[half * tail : (half + 1) * tail, at * rows : (at + 1) * rows] = messages[at][
                rows:, half * rows : (half + 1) * rows
            ].astype(F32)
    for at in range(0, words * depth, 128):
        block = jnp.concatenate(
            [codebook_ref[:, at : at + 128].astype(F32)] * (128 // spaces), axis=0
        )
        turned_ref[at : at + 128, :] = jnp.transpose(block)
    for at in range(depth):
        block = jnp.transpose(turned_ref[pl.ds(at, words, stride=depth), :])
        for piece in range(words // 128):
            words_ref[piece, pl.ds(at, spaces, stride=depth), :] = block[
                :spaces, piece * 128 : (piece + 1) * 128
            ]
    parts = []
    for space in range(spaces):
        line = codes_ref[space : space + 1, :].astype(jnp.int32)
        cells = []
        for at in range(subs):
            index = jnp.broadcast_to(line[:, at * rows : (at + 1) * rows], (depth, rows))
            value = None
            for piece in range(words // 128):
                got = jnp.take_along_axis(
                    words_ref[piece, space * depth : (space + 1) * depth, :], index & 127, axis=1
                )
                value = got if value is None else jnp.where(index >= piece * 128, got, value)
            cells.append(value)
        parts.append(jnp.concatenate(cells, axis=1))
    picked_ref[...] = jnp.transpose(jnp.concatenate(parts, axis=0)).astype(BF16)
    tally = jnp.zeros((words, 128), F32)
    word = lax.broadcasted_iota(jnp.int32, (words, subs * rows), 0).astype(F32)
    lane = lax.broadcasted_iota(jnp.int32, (subs * rows, 128), 1)
    for space in range(spaces):
        hot = (word == codes_ref[space : space + 1, :]).astype(F32).astype(BF16)
        tally = tally + jnp.dot(
            hot, (lane == space).astype(F32).astype(BF16), preferred_element_type=F32
        )
    tally_ref[...] = tally


def place_kernel(direct, count, slot_ref, picked_ref, *refs):
    messages, refs = refs[:count], refs[count:]
    if not direct:
        messages = [messages[0].at[at] for at in range(messages[0].shape[0])]
    subs = len(messages)
    spread = subs if direct else 1
    pieces, rebuilt, residual_ref = refs[: -1 - spread], refs[-1 - spread : -1], refs[-1]
    rows = slot_ref.shape[0]
    total = sum(piece.shape[1] for piece in pieces)
    column = lax.broadcasted_iota(jnp.int32, (rows, total), 1).astype(F32)
    for at in range(subs):
        chosen = (column == slot_ref[:, at : at + 1]).astype(F32).astype(BF16)
        stacked = jnp.concatenate([piece[at] for piece in pieces], axis=0)
        centre = jnp.dot(chosen, stacked, preferred_element_type=F32)
        span = slice(at * rows, (at + 1) * rows)
        out = rebuilt[at] if direct else rebuilt[0].at[at]
        out[...] = (centre + picked_ref[span, :].astype(F32)).astype(BF16)
        residual_ref[span, :] = (messages[at][:rows, :].astype(F32) - centre).astype(BF16)


def sums_kernel(lists, direct, codes_ref, residual_ref, tally_ref, *refs):
    outs, total_ref = refs[:-1], refs[-1]
    spaces, rows = codes_ref.shape
    width = residual_ref.shape[1]
    words = tally_ref.shape[0]
    depth = width // spaces
    share = words // lists
    word = lax.broadcasted_iota(jnp.int32, (words, rows), 0).astype(F32)
    owner = lax.broadcasted_iota(jnp.int32, (rows, width), 1) // depth
    residual = residual_ref[...]
    total = jnp.zeros((words, width), F32)
    for space in range(spaces):
        hot = (word == codes_ref[space : space + 1, :]).astype(F32).astype(BF16)
        part = jnp.where(owner == space, residual, jnp.zeros_like(residual))
        total = total + jnp.dot(hot, part, preferred_element_type=F32)
    total_ref[...] = total
    me = lax.axis_index("lists")
    for step in range(lists):
        out = outs[step] if direct else outs[0].at[step]
        at = (me ^ step) if direct else step
        span = pl.ds(pl.multiple_of(at * share, share), share)
        out[:, :width] = total_ref[span, :].astype(BF16)
        out[:, width:] = tally_ref[span, :].astype(BF16)


def refine_kernel(spaces, direct, codebook_ref, *refs):
    pieces, (out_ref, turned_ref) = refs[:-2], refs[-2:]
    total = None
    for piece in pieces:
        if direct:
            value = piece[...].astype(F32)
        else:
            value = jnp.sum(piece[...].astype(F32), axis=0)
        total = value if total is None else total + value
    share = total.shape[0]
    width = total.shape[1] - 128
    depth = width // spaces
    span = share * depth
    turned = jnp.transpose(total)
    turned_ref[...] = turned[:width, :]
    tally = turned[width : width + spaces, :]
    word = lax.broadcasted_iota(jnp.int32, (share, span), 0)
    cell = lax.broadcasted_iota(jnp.int32, (share, span), 1)

    def spread(value, table):
        high = value.astype(BF16)
        rest = value - high.astype(F32)
        low = rest.astype(BF16)
        return jnp.dot(high, table, preferred_element_type=F32) + jnp.dot(
            low, table, preferred_element_type=F32
        )

    sums = jnp.zeros((spaces, span), F32)
    for at in range(depth):
        table = (cell == word * depth + at).astype(F32).astype(BF16)
        sums = sums + spread(turned_ref[pl.ds(at, spaces, stride=depth), :], table)
    counts = spread(tally, (cell // depth == word).astype(F32).astype(BF16))
    me = lax.axis_index("lists")
    if span % 128 == 0:
        prior = codebook_ref[:, pl.ds(pl.multiple_of(me * span, span), span)].astype(F32)
    else:
        prior = jnp.zeros((spaces, span), F32)
        for at in range(codebook_ref.shape[1] // span):
            block = codebook_ref[:, at * span : (at + 1) * span].astype(F32)
            prior = prior + jnp.where(me == at, block, 0.0)
    out_ref[...] = (sums + prior) / (counts + 1.0)


def restore_kernel(direct, passages_ref, rotation_ref, *refs):
    pieces, out_ref = refs[:-1], refs[-1]
    me = lax.axis_index("sub")
    if direct:
        blocks = [piece[...] for piece in pieces]
    else:
        blocks = [pieces[0][at] for at in range(pieces[0].shape[0])]
    width = blocks[0].shape[1]
    total = None
    for at, block in enumerate(blocks):
        start = (me ^ at) * width if direct else at * width
        if direct:
            start = pl.multiple_of(start, width)
        value = lax.dot_general(
            block,
            rotation_ref[:, pl.ds(start, width)],
            (((1,), (1,)), ((), ())),
            preferred_element_type=F32,
        )
        total = value if total is None else total + value
    out_ref[...] = (passages_ref[...].astype(F32) - total).astype(BF16)


def swap(value, axis, step):
    count = lax.axis_size(axis)
    return lax.ppermute(value, axis, [(at, at ^ step) for at in range(count)])


def exchange(values, axis):
    return [values[0]] + [swap(values[step], axis, step) for step in range(1, len(values))]


def all_swap(value, axis):
    return lax.all_to_all(value, axis, split_axis=0, concat_axis=0, tiled=True)


def body(passages, rotation, centroids, list_slot, list_ids, codes, codebook):
    lists = lax.axis_size("lists")
    subs = lax.axis_size("sub")
    rows, model = passages.shape
    held, width = centroids.shape
    cap = 2 * rows // lists
    spaces = codebook.shape[0]
    depth = width // spaces
    words = codebook.shape[1] // depth
    share = words // lists
    direct = max(lists, subs) <= DIRECT
    shape = jax.ShapeDtypeStruct

    tables = call(
        tables_kernel,
        shape((1, rows), jnp.int32),
        40_000_000,
        4 * list_slot.shape[0],
        list_ids.reshape(1, rows),
        list_slot.reshape(-1, 128),
    )
    if direct:
        tables = jnp.concatenate(exchange([tables] * subs, "sub"), axis=0)
        tables = exchange([tables] * lists, "lists")
    else:
        tables = jnp.broadcast_to(tables[None], (lists * subs, 1, rows))
        tables = [all_swap(tables, ("lists", "sub")).reshape(lists * subs, rows)]

    pieces = call(
        functools.partial(fetch_kernel, held, lists, len(tables)),
        [shape((subs, cap, width), BF16)] * lists
        if direct
        else [shape((lists * subs, cap, width), BF16)],
        600_000_000,
        held * width * 2,
        *tables,
        centroids,
        scratch=[
            pltpu.VMEM((lists * subs, cap), jnp.int32),
            pltpu.SMEM((lists * subs, cap), jnp.int32),
            pltpu.SemaphoreType.DMA,
        ],
    )
    fetched = pieces[0]
    if direct:
        pieces = exchange(pieces, "lists")
    else:
        found = all_swap(pieces[0].reshape(lists, subs * cap, width), "lists")
        found = found.reshape(lists, subs, cap, width)
        pieces = [jnp.swapaxes(found, 0, 1).reshape(subs, lists * cap, width)]

    long = rows + spaces // (width // rows)
    messages = call(
        functools.partial(rotate_kernel, subs, direct),
        [shape((long, width), BF16)] * subs if direct else [shape((subs, long, width), BF16)],
        2 * rows * model * model,
        2 * model * model + 4 * rows * model,
        passages,
        rotation,
        codes,
        fetched,
        loose=1,
        scratch=[pltpu.VMEM((codes.shape[1], rows), F32)],
    )
    messages = exchange(messages, "sub") if direct else [all_swap(messages[0], "sub")]

    picked, slot, codes_t, tally = call(
        functools.partial(lookup_kernel, held, lists, direct, cap, len(messages)),
        [
            shape((subs * rows, width), BF16),
            shape((rows, rows), F32),
            shape((spaces, subs * rows), F32),
            shape((words, 128), F32),
        ],
        1_000_000_000,
        2_000_000,
        tables[0],
        codebook,
        *messages,
        scratch=[pltpu.VMEM((words * depth, 128), F32), pltpu.VMEM((words // 128, width, 128), F32)],
    )
    *rebuilt, residual = call(
        functools.partial(place_kernel, direct, len(messages)),
        ([shape((rows, width), BF16)] * subs if direct else [shape((subs, rows, width), BF16)])
        + [shape((subs * rows, width), BF16)],
        300_000_000,
        2_000_000,
        slot,
        picked,
        *messages,
        *pieces,
    )
    rebuilt = exchange(rebuilt, "sub") if direct else [all_swap(rebuilt[0], "sub")]
    sums = call(
        functools.partial(sums_kernel, lists, direct),
        [shape((share, width + 128), BF16)] * lists
        if direct
        else [shape((lists, share, width + 128), BF16)],
        2_000_000_000,
        1_000_000,
        codes_t,
        residual,
        tally,
        scratch=[pltpu.VMEM((words, width), F32)],
    )
    sums = exchange(sums, "lists") if direct else [all_swap(sums[0], "lists")]
    recon_error = call(
        functools.partial(restore_kernel, direct),
        shape((rows, model), BF16),
        2 * rows * model * model,
        2 * model * model + 4 * rows * model,
        passages,
        rotation,
        *rebuilt,
    )
    new_codebook = call(
        functools.partial(refine_kernel, spaces, direct),
        shape((spaces, share * depth), F32),
        100_000_000,
        500_000,
        codebook,
        *sums,
        scratch=[pltpu.VMEM((width, share), F32)],
    )
    return (recon_error, new_codebook)


def solution(mesh):
    return jax.shard_map(
        body,
        mesh=mesh,
        in_specs=(
            P(("groups", "lists", "sub"), None),
            P(),
            P("lists", "sub"),
            P("groups"),
            P(("groups", "lists", "sub")),
            P(("groups", "lists", "sub"), None),
            P("sub", None),
        ),
        out_specs=(P(("groups", "lists", "sub"), None), P(("groups", "sub"), "lists")),
        check_vma=False,
    )
```

```python
import functools

import jax
import jax.numpy as jnp
from jax import lax
from jax.experimental import pallas as pl
from jax.experimental.pallas import tpu as pltpu
from jax.sharding import PartitionSpec as P

BF16 = jnp.bfloat16
F32 = jnp.float32
VMEM_LIMIT = 32 * 1024 * 1024
MERGE_FLOPS = 6_000_000_000
DIRECT = 4


def call(kernel, out_shape, flops, nbytes, *args, scratch=(), loose=0, limit=VMEM_LIMIT):
    whole = lambda: pl.BlockSpec(memory_space=pltpu.VMEM)
    return pl.pallas_call(
        kernel,
        out_shape=out_shape,
        in_specs=[whole() for _ in args[: len(args) - loose]]
        + [pl.BlockSpec(memory_space=pl.ANY)] * loose,
        out_specs=jax.tree.map(lambda _: whole(), out_shape),
        scratch_shapes=list(scratch),
        compiler_params=pltpu.CompilerParams(vmem_limit_bytes=limit),
        cost_estimate=pl.CostEstimate(flops=flops, bytes_accessed=nbytes, transcendentals=0),
    )(*args)


def strict_before(width):
    row = lax.broadcasted_iota(jnp.int32, (width, width), 0)
    col = lax.broadcasted_iota(jnp.int32, (width, width), 1)
    return (row < col).astype(F32).astype(BF16)


def tables_kernel(ids_ref, slots_ref, out_ref):
    rows = ids_ref.shape[1]
    lines = slots_ref.shape[0]
    ids = jnp.transpose(jnp.concatenate([ids_ref[...].astype(F32)] * 128, axis=0))[:, :1]
    ids = ids.astype(jnp.int32)
    line = lax.broadcasted_iota(jnp.int32, (rows, lines), 1)
    chosen = (line == (ids >> 7)).astype(F32).astype(BF16)
    table = slots_ref[...]
    high = (table >> 8).astype(F32).astype(BF16)
    low = (table & 255).astype(F32).astype(BF16)
    found = jnp.dot(chosen, high, preferred_element_type=F32) * 256.0 + jnp.dot(
        chosen, low, preferred_element_type=F32
    )
    lane = lax.broadcasted_iota(jnp.int32, (rows, 128), 1)
    found = jnp.transpose(jnp.where(lane == (ids & 127), found, 0.0))
    out_ref[...] = jnp.sum(found, axis=0, keepdims=True).astype(jnp.int32)


def merge_kernel(*refs):
    for at, ref in enumerate(refs[:-1]):
        refs[-1][at : at + 1, :] = ref[...]


def rotate_kernel(subs, direct, passages_ref, rotation_ref, codes_ref, after_ref, *refs):
    outs, turned_ref = refs[:-1], refs[-1]
    rows, model = passages_ref.shape
    width = model // subs
    spaces = codes_ref.shape[1] // subs
    halves = width // rows
    tail = spaces // halves
    me = lax.axis_index("sub")
    turned_ref[...] = jnp.transpose(codes_ref[...].astype(F32))
    for step in range(subs):
        at = (me ^ step) if direct else step
        out = outs[step] if direct else outs[0].at[step]
        columns = pl.ds(pl.multiple_of(at * width, width), width)
        out[:rows, :] = jnp.dot(
            passages_ref[...], rotation_ref[:, columns], preferred_element_type=F32
        ).astype(BF16)
        for half in range(halves):
            start = pl.multiple_of(at * spaces + half * tail, tail)
            out[rows:, half * rows : (half + 1) * rows] = turned_ref[pl.ds(start, tail), :].astype(
                BF16
            )


def fetch_kernel(held, lists, count, *refs):
    rows_refs, centroids_ref, outs = refs[:count], refs[count], refs[count + 1 : -3]
    index_ref, scalar_ref, sem = refs[-3:]
    blocks, cap = index_ref.shape
    rows = rows_refs[0].shape[1]
    group = min(cap, 16)
    me = lax.axis_index("lists")
    local = jnp.concatenate([ref[...] for ref in rows_refs], axis=0) - me * held
    mine = jnp.logical_and(local >= 0, local < held)
    flags = mine.astype(F32)
    rank = jnp.dot(flags.astype(BF16), strict_before(rows), preferred_element_type=F32)
    rank = jnp.where(mine, rank, -1.0)
    local = jnp.where(mine, local, 0)
    pad = max(128 // blocks, 1)
    rank = jnp.transpose(jnp.concatenate([rank] * pad, axis=0))
    local = jnp.transpose(jnp.concatenate([local.astype(F32)] * pad, axis=0))
    slot = lax.broadcasted_iota(jnp.int32, (rows, cap), 1).astype(F32)
    index = []
    for block in range(blocks):
        chosen = slot == rank[:, block : block + 1]
        index.append(
            jnp.sum(jnp.where(chosen, local[:, block : block + 1], 0.0), axis=0, keepdims=True)
        )
    index = jnp.concatenate(index, axis=0).astype(jnp.int32)
    index_ref[...] = index & -16
    move = pltpu.make_async_copy(index_ref, scalar_ref, sem)
    move.start()
    within = lax.broadcasted_iota(jnp.int32, (blocks, cap), 1) & (group - 1)
    spot = (within * 16 + (index & 15)).astype(F32)
    spot = jnp.transpose(jnp.concatenate([spot] * pad, axis=0))
    lane = lax.broadcasted_iota(jnp.int32, (cap, group * 16), 1).astype(F32)
    move.wait()
    for block in range(blocks):
        chosen = (lane == spot[:, block : block + 1]).astype(F32).astype(BF16)
        for start in range(0, cap, group):
            tiles = []
            for at in range(start, start + group):
                base = pl.multiple_of(scalar_ref[block, at], 16)
                tiles.append(centroids_ref[pl.ds(base, 16), :])
            value = jnp.dot(
                chosen[start : start + group],
                jnp.concatenate(tiles, axis=0),
                preferred_element_type=F32,
            ).astype(BF16)
            per = blocks // len(outs)
            outs[block // per][block % per, start : start + group, :] = value


def lookup_kernel(held, lists, direct, cap, count, rows_ref, codebook_ref, *refs):
    messages, refs = refs[:count], refs[count:]
    picked_ref, slot_ref, codes_ref, tally_ref, turned_ref, words_ref = refs
    if not direct:
        messages = [messages[0].at[at] for at in range(messages[0].shape[0])]
    subs = len(messages)
    width = messages[0].shape[1]
    rows = rows_ref.shape[1]
    spaces = codes_ref.shape[0]
    depth = width // spaces
    words = words_ref.shape[0] * 128
    halves = width // rows
    tail = spaces // halves
    me = lax.axis_index("lists")
    if direct:
        tables = rows_ref[...]
    else:
        tables = rows_ref[pl.ds(pl.multiple_of(me * subs, subs), subs), :]
    owners = tables // held
    rank = jnp.zeros((subs, rows), F32)
    flags = [(owners == at).astype(F32) for at in range(lists)]
    stacked = jnp.concatenate(flags, axis=0)
    before = jnp.dot(stacked.astype(BF16), strict_before(rows), preferred_element_type=F32)
    for at in range(lists):
        rank = rank + flags[at] * before[at * subs : (at + 1) * subs]
    place = (owners ^ me) if direct else owners
    slot = place.astype(F32) * cap + rank
    slot_ref[...] = jnp.transpose(jnp.concatenate([slot] * (rows // subs), axis=0))
    for at in range(subs):
        for half in range(halves):
            codes_ref[half * tail : (half + 1) * tail, at * rows : (at + 1) * rows] = messages[at][
                rows:, half * rows : (half + 1) * rows
            ].astype(F32)
    for at in range(0, words * depth, 128):
        block = jnp.concatenate(
            [codebook_ref[:, at : at + 128].astype(F32)] * (128 // spaces), axis=0
        )
        turned_ref[at : at + 128, :] = jnp.transpose(block)
    for at in range(depth):
        block = jnp.transpose(turned_ref[pl.ds(at, words, stride=depth), :])
        for piece in range(words // 128):
            words_ref[piece, pl.ds(at, spaces, stride=depth), :] = block[
                :spaces, piece * 128 : (piece + 1) * 128
            ]
    parts = []
    for space in range(spaces):
        line = codes_ref[space : space + 1, :].astype(jnp.int32)
        cells = []
        for at in range(subs):
            index = jnp.broadcast_to(line[:, at * rows : (at + 1) * rows], (depth, rows))
            value = None
            for piece in range(words // 128):
                got = jnp.take_along_axis(
                    words_ref[piece, space * depth : (space + 1) * depth, :], index & 127, axis=1
                )
                value = got if value is None else jnp.where(index >= piece * 128, got, value)
            cells.append(value)
        parts.append(jnp.concatenate(cells, axis=1))
    picked_ref[...] = jnp.transpose(jnp.concatenate(parts, axis=0)).astype(BF16)
    tally = jnp.zeros((words, 128), F32)
    word = lax.broadcasted_iota(jnp.int32, (words, subs * rows), 0).astype(F32)
    lane = lax.broadcasted_iota(jnp.int32, (subs * rows, 128), 1)
    for space in range(spaces):
        hot = (word == codes_ref[space : space + 1, :]).astype(F32).astype(BF16)
        tally = tally + jnp.dot(
            hot, (lane == space).astype(F32).astype(BF16), preferred_element_type=F32
        )
    tally_ref[...] = tally


def place_kernel(direct, count, slot_ref, picked_ref, *refs):
    messages, refs = refs[:count], refs[count:]
    if not direct:
        messages = [messages[0].at[at] for at in range(messages[0].shape[0])]
    subs = len(messages)
    spread = subs if direct else 1
    pieces, rebuilt, residual_ref = refs[: -1 - spread], refs[-1 - spread : -1], refs[-1]
    rows = slot_ref.shape[0]
    total = sum(piece.shape[1] for piece in pieces)
    column = lax.broadcasted_iota(jnp.int32, (rows, total), 1).astype(F32)
    for at in range(subs):
        chosen = (column == slot_ref[:, at : at + 1]).astype(F32).astype(BF16)
        stacked = jnp.concatenate([piece[at] for piece in pieces], axis=0)
        centre = jnp.dot(chosen, stacked, preferred_element_type=F32)
        span = slice(at * rows, (at + 1) * rows)
        out = rebuilt[at] if direct else rebuilt[0].at[at]
        out[...] = (centre + picked_ref[span, :].astype(F32)).astype(BF16)
        residual_ref[span, :] = (messages[at][:rows, :].astype(F32) - centre).astype(BF16)


def sums_kernel(lists, direct, codes_ref, residual_ref, tally_ref, after_ref, *refs):
    outs, total_ref = refs[:-1], refs[-1]
    spaces, rows = codes_ref.shape
    width = residual_ref.shape[1]
    words = tally_ref.shape[0]
    depth = width // spaces
    share = words // lists
    word = lax.broadcasted_iota(jnp.int32, (words, rows), 0).astype(F32)
    owner = lax.broadcasted_iota(jnp.int32, (rows, width), 1) // depth
    residual = residual_ref[...]
    total = jnp.zeros((words, width), F32)
    for space in range(spaces):
        hot = (word == codes_ref[space : space + 1, :]).astype(F32).astype(BF16)
        part = jnp.where(owner == space, residual, jnp.zeros_like(residual))
        total = total + jnp.dot(hot, part, preferred_element_type=F32)
    total_ref[...] = total
    me = lax.axis_index("lists")
    for step in range(lists):
        out = outs[step] if direct else outs[0].at[step]
        at = (me ^ step) if direct else step
        span = pl.ds(pl.multiple_of(at * share, share), share)
        out[:, :width] = total_ref[span, :].astype(BF16)
        out[:, width:] = tally_ref[span, :].astype(BF16)


def refine_kernel(spaces, direct, codebook_ref, *refs):
    pieces, (out_ref, turned_ref) = refs[:-2], refs[-2:]
    total = None
    for piece in pieces:
        if direct:
            value = piece[...].astype(F32)
        else:
            value = jnp.sum(piece[...].astype(F32), axis=0)
        total = value if total is None else total + value
    share = total.shape[0]
    width = total.shape[1] - 128
    depth = width // spaces
    span = share * depth
    turned = jnp.transpose(total)
    turned_ref[...] = turned[:width, :]
    tally = turned[width : width + spaces, :]
    word = lax.broadcasted_iota(jnp.int32, (share, span), 0)
    cell = lax.broadcasted_iota(jnp.int32, (share, span), 1)

    def spread(value, table):
        high = value.astype(BF16)
        rest = value - high.astype(F32)
        low = rest.astype(BF16)
        return jnp.dot(high, table, preferred_element_type=F32) + jnp.dot(
            low, table, preferred_element_type=F32
        )

    sums = jnp.zeros((spaces, span), F32)
    for at in range(depth):
        table = (cell == word * depth + at).astype(F32).astype(BF16)
        sums = sums + spread(turned_ref[pl.ds(at, spaces, stride=depth), :], table)
    counts = spread(tally, (cell // depth == word).astype(F32).astype(BF16))
    me = lax.axis_index("lists")
    if span % 128 == 0:
        prior = codebook_ref[:, pl.ds(pl.multiple_of(me * span, span), span)].astype(F32)
    else:
        prior = jnp.zeros((spaces, span), F32)
        for at in range(codebook_ref.shape[1] // span):
            block = codebook_ref[:, at * span : (at + 1) * span].astype(F32)
            prior = prior + jnp.where(me == at, block, 0.0)
    out_ref[...] = (sums + prior) / (counts + 1.0)


def restore_kernel(direct, passages_ref, rotation_ref, *refs):
    pieces, out_ref = refs[:-2], refs[-1]
    me = lax.axis_index("sub")
    if direct:
        blocks = [piece[...] for piece in pieces]
    else:
        blocks = [pieces[0][at] for at in range(pieces[0].shape[0])]
    width = blocks[0].shape[1]
    total = None
    for at, block in enumerate(blocks):
        start = (me ^ at) * width if direct else at * width
        if direct:
            start = pl.multiple_of(start, width)
        value = lax.dot_general(
            block,
            rotation_ref[:, pl.ds(start, width)],
            (((1,), (1,)), ((), ())),
            preferred_element_type=F32,
        )
        total = value if total is None else total + value
    out_ref[...] = (passages_ref[...].astype(F32) - total).astype(BF16)


def swap(value, axis, step):
    count = lax.axis_size(axis)
    return lax.ppermute(value, axis, [(at, at ^ step) for at in range(count)])


def exchange(values, axis):
    return [values[0]] + [swap(values[step], axis, step) for step in range(1, len(values))]


def spread(value, axis):
    values, step = [value], 1
    while step < lax.axis_size(axis):
        values += [swap(one, axis, step) for one in values]
        step *= 2
    return values


def all_swap(value, axis):
    return lax.all_to_all(value, axis, split_axis=0, concat_axis=0, tiled=True)


def body(passages, rotation, centroids, list_slot, list_ids, codes, codebook):
    lists = lax.axis_size("lists")
    subs = lax.axis_size("sub")
    rows, model = passages.shape
    held, width = centroids.shape
    cap = 2 * rows // lists
    spaces = codebook.shape[0]
    depth = width // spaces
    words = codebook.shape[1] // depth
    share = words // lists
    direct = max(lists, subs) <= DIRECT
    shape = jax.ShapeDtypeStruct

    tables = call(
        tables_kernel,
        shape((1, rows), jnp.int32),
        1_000,
        0,
        list_ids.reshape(1, rows),
        list_slot.reshape(-1, 128),
    )
    if direct:
        tables = call(
            merge_kernel,
            shape((subs, rows), jnp.int32),
            MERGE_FLOPS,
            4 * subs * rows,
            *spread(tables, "sub"),
        )
        tables = spread(tables, "lists")
    else:
        tables = jnp.broadcast_to(tables[None], (lists * subs, 1, rows))
        tables = [all_swap(tables, ("lists", "sub")).reshape(lists * subs, rows)]

    pieces = call(
        functools.partial(fetch_kernel, held, lists, len(tables)),
        [shape((subs, cap, width), BF16)] * lists
        if direct
        else [shape((lists * subs, cap, width), BF16)],
        600_000_000,
        held * width * 2,
        *tables,
        centroids,
        scratch=[
            pltpu.VMEM((lists * subs, cap), jnp.int32),
            pltpu.SMEM((lists * subs, cap), jnp.int32),
            pltpu.SemaphoreType.DMA,
        ],
    )
    if direct:
        pieces = exchange(pieces, "lists")
    else:
        found = all_swap(pieces[0].reshape(lists, subs * cap, width), "lists")
        found = found.reshape(lists, subs, cap, width)
        pieces = [jnp.swapaxes(found, 0, 1).reshape(subs, lists * cap, width)]

    long = rows + spaces // (width // rows)
    messages = call(
        functools.partial(rotate_kernel, subs, direct),
        [shape((long, width), BF16)] * subs if direct else [shape((subs, long, width), BF16)],
        1_000_000,
        1_000,
        passages,
        rotation,
        codes,
        pieces[1] if direct else tables[0],
        loose=1,
        scratch=[pltpu.VMEM((codes.shape[1], rows), F32)],
    )
    messages = exchange(messages, "sub") if direct else [all_swap(messages[0], "sub")]

    picked, slot, codes_t, tally = call(
        functools.partial(lookup_kernel, held, lists, direct, cap, len(messages)),
        [
            shape((subs * rows, width), BF16),
            shape((rows, rows), F32),
            shape((spaces, subs * rows), F32),
            shape((words, 128), F32),
        ],
        1_000_000,
        1_000,
        tables[0],
        codebook,
        *messages,
        scratch=[pltpu.VMEM((words * depth, 128), F32), pltpu.VMEM((words // 128, width, 128), F32)],
    )
    *rebuilt, residual = call(
        functools.partial(place_kernel, direct, len(messages)),
        ([shape((rows, width), BF16)] * subs if direct else [shape((subs, rows, width), BF16)])
        + [shape((subs * rows, width), BF16)],
        300_000_000,
        2_000_000,
        slot,
        picked,
        *messages,
        *pieces,
    )
    rebuilt = exchange(rebuilt, "sub") if direct else [all_swap(rebuilt[0], "sub")]
    sums = call(
        functools.partial(sums_kernel, lists, direct),
        [shape((share, width + 128), BF16)] * lists
        if direct
        else [shape((lists, share, width + 128), BF16)],
        2_000_000_000,
        1_000_000,
        codes_t,
        residual,
        tally,
        rebuilt[1] if direct else residual,
        loose=1,
        scratch=[pltpu.VMEM((words, width), F32)],
    )
    sums = exchange(sums, "lists") if direct else [all_swap(sums[0], "lists")]
    recon_error = call(
        functools.partial(restore_kernel, direct),
        shape((rows, model), BF16),
        2 * rows * model * model,
        2 * model * model + 4 * rows * model,
        passages,
        rotation,
        *rebuilt,
        sums[1] if direct else sums[0],
        loose=1,
    )
    new_codebook = call(
        functools.partial(refine_kernel, spaces, direct),
        shape((spaces, share * depth), F32),
        100_000_000,
        500_000,
        codebook,
        *sums,
        scratch=[pltpu.VMEM((width, share), F32)],
    )
    return (recon_error, new_codebook)


def solution(mesh):
    return jax.shard_map(
        body,
        mesh=mesh,
        in_specs=(
            P(("groups", "lists", "sub"), None),
            P(),
            P("lists", "sub"),
            P("groups"),
            P(("groups", "lists", "sub")),
            P(("groups", "lists", "sub"), None),
            P("sub", None),
        ),
        out_specs=(P(("groups", "lists", "sub"), None), P(("groups", "sub"), "lists")),
        check_vma=False,
    )
```

```python
import functools

import jax
import jax.numpy as jnp
from jax import lax
from jax.experimental import pallas as pl
from jax.experimental.pallas import tpu as pltpu
from jax.sharding import PartitionSpec as P

BF16 = jnp.bfloat16
F32 = jnp.float32
VMEM_LIMIT = 32 * 1024 * 1024
TABLES_FLOPS = 8_000_000_000
DIRECT = 4


def call(kernel, out_shape, flops, nbytes, *args, scratch=(), loose=0, limit=VMEM_LIMIT):
    whole = lambda: pl.BlockSpec(memory_space=pltpu.VMEM)
    return pl.pallas_call(
        kernel,
        out_shape=out_shape,
        in_specs=[whole() for _ in args[: len(args) - loose]]
        + [pl.BlockSpec(memory_space=pl.ANY)] * loose,
        out_specs=jax.tree.map(lambda _: whole(), out_shape),
        scratch_shapes=list(scratch),
        compiler_params=pltpu.CompilerParams(vmem_limit_bytes=limit),
        cost_estimate=pl.CostEstimate(flops=flops, bytes_accessed=nbytes, transcendentals=0),
    )(*args)


def strict_before(width):
    row = lax.broadcasted_iota(jnp.int32, (width, width), 0)
    col = lax.broadcasted_iota(jnp.int32, (width, width), 1)
    return (row < col).astype(F32).astype(BF16)


def tables_kernel(ids_ref, slots_ref, out_ref):
    rows = ids_ref.shape[1]
    lines = slots_ref.shape[0]
    ids = jnp.transpose(jnp.concatenate([ids_ref[...].astype(F32)] * 128, axis=0))[:, :1]
    ids = ids.astype(jnp.int32)
    line = lax.broadcasted_iota(jnp.int32, (rows, lines), 1)
    chosen = (line == (ids >> 7)).astype(F32).astype(BF16)
    table = slots_ref[...]
    high = (table >> 8).astype(F32).astype(BF16)
    low = (table & 255).astype(F32).astype(BF16)
    found = jnp.dot(chosen, high, preferred_element_type=F32) * 256.0 + jnp.dot(
        chosen, low, preferred_element_type=F32
    )
    lane = lax.broadcasted_iota(jnp.int32, (rows, 128), 1)
    found = jnp.transpose(jnp.where(lane == (ids & 127), found, 0.0))
    line = jnp.sum(found, axis=0, keepdims=True).astype(jnp.int32)
    out_ref[...] = jnp.broadcast_to(line, out_ref.shape)


def rotate_kernel(subs, direct, passages_ref, rotation_ref, codes_ref, after_ref, *refs):
    outs, turned_ref = refs[:-1], refs[-1]
    rows, model = passages_ref.shape
    width = model // subs
    spaces = codes_ref.shape[1] // subs
    halves = width // rows
    tail = spaces // halves
    me = lax.axis_index("sub")
    turned_ref[...] = jnp.transpose(codes_ref[...].astype(F32))
    for step in range(subs):
        at = (me ^ step) if direct else step
        out = outs[step] if direct else outs[0].at[step]
        columns = pl.ds(pl.multiple_of(at * width, width), width)
        out[:rows, :] = jnp.dot(
            passages_ref[...], rotation_ref[:, columns], preferred_element_type=F32
        ).astype(BF16)
        for half in range(halves):
            start = pl.multiple_of(at * spaces + half * tail, tail)
            out[rows:, half * rows : (half + 1) * rows] = turned_ref[pl.ds(start, tail), :].astype(
                BF16
            )


def near_rows(rows_ref, owner, subs):
    me = lax.axis_index("sub")
    return jnp.concatenate(
        [rows_ref[pl.ds(owner * subs + (me ^ step), 1), :] for step in range(subs)], axis=0
    )


def fetch_kernel(held, lists, direct, rows_ref, centroids_ref, *refs):
    outs = refs[:-3]
    index_ref, scalar_ref, sem = refs[-3:]
    blocks, cap = index_ref.shape
    rows = rows_ref.shape[1]
    group = min(cap, 16)
    me = lax.axis_index("lists")
    if direct:
        tables = jnp.concatenate(
            [near_rows(rows_ref, me ^ step, blocks // lists) for step in range(lists)], axis=0
        )
    else:
        tables = rows_ref[...]
    local = tables - me * held
    mine = jnp.logical_and(local >= 0, local < held)
    flags = mine.astype(F32)
    rank = jnp.dot(flags.astype(BF16), strict_before(rows), preferred_element_type=F32)
    rank = jnp.where(mine, rank, -1.0)
    local = jnp.where(mine, local, 0)
    pad = max(128 // blocks, 1)
    rank = jnp.transpose(jnp.concatenate([rank] * pad, axis=0))
    local = jnp.transpose(jnp.concatenate([local.astype(F32)] * pad, axis=0))
    slot = lax.broadcasted_iota(jnp.int32, (rows, cap), 1).astype(F32)
    index = []
    for block in range(blocks):
        chosen = slot == rank[:, block : block + 1]
        index.append(
            jnp.sum(jnp.where(chosen, local[:, block : block + 1], 0.0), axis=0, keepdims=True)
        )
    index = jnp.concatenate(index, axis=0).astype(jnp.int32)
    index_ref[...] = index & -16
    move = pltpu.make_async_copy(index_ref, scalar_ref, sem)
    move.start()
    within = lax.broadcasted_iota(jnp.int32, (blocks, cap), 1) & (group - 1)
    spot = (within * 16 + (index & 15)).astype(F32)
    spot = jnp.transpose(jnp.concatenate([spot] * pad, axis=0))
    lane = lax.broadcasted_iota(jnp.int32, (cap, group * 16), 1).astype(F32)
    move.wait()
    for block in range(blocks):
        chosen = (lane == spot[:, block : block + 1]).astype(F32).astype(BF16)
        for start in range(0, cap, group):
            tiles = []
            for at in range(start, start + group):
                base = pl.multiple_of(scalar_ref[block, at], 16)
                tiles.append(centroids_ref[pl.ds(base, 16), :])
            value = jnp.dot(
                chosen[start : start + group],
                jnp.concatenate(tiles, axis=0),
                preferred_element_type=F32,
            ).astype(BF16)
            per = blocks // len(outs)
            outs[block // per][block % per, start : start + group, :] = value


def lookup_kernel(held, lists, direct, cap, count, rows_ref, codebook_ref, *refs):
    messages, refs = refs[:count], refs[count:]
    picked_ref, slot_ref, codes_ref, tally_ref, turned_ref, words_ref = refs
    if not direct:
        messages = [messages[0].at[at] for at in range(messages[0].shape[0])]
    subs = len(messages)
    width = messages[0].shape[1]
    rows = rows_ref.shape[1]
    spaces = codes_ref.shape[0]
    depth = width // spaces
    words = words_ref.shape[0] * 128
    halves = width // rows
    tail = spaces // halves
    me = lax.axis_index("lists")
    if direct:
        tables = near_rows(rows_ref, me, subs)
    else:
        tables = rows_ref[pl.ds(pl.multiple_of(me * subs, subs), subs), :]
    owners = tables // held
    rank = jnp.zeros((subs, rows), F32)
    flags = [(owners == at).astype(F32) for at in range(lists)]
    stacked = jnp.concatenate(flags, axis=0)
    before = jnp.dot(stacked.astype(BF16), strict_before(rows), preferred_element_type=F32)
    for at in range(lists):
        rank = rank + flags[at] * before[at * subs : (at + 1) * subs]
    place = (owners ^ me) if direct else owners
    slot = place.astype(F32) * cap + rank
    slot_ref[...] = jnp.transpose(jnp.concatenate([slot] * (rows // subs), axis=0))
    for at in range(subs):
        for half in range(halves):
            codes_ref[half * tail : (half + 1) * tail, at * rows : (at + 1) * rows] = messages[at][
                rows:, half * rows : (half + 1) * rows
            ].astype(F32)
    for at in range(0, words * depth, 128):
        block = jnp.concatenate(
            [codebook_ref[:, at : at + 128].astype(F32)] * (128 // spaces), axis=0
        )
        turned_ref[at : at + 128, :] = jnp.transpose(block)
    for at in range(depth):
        block = jnp.transpose(turned_ref[pl.ds(at, words, stride=depth), :])
        for piece in range(words // 128):
            words_ref[piece, pl.ds(at, spaces, stride=depth), :] = block[
                :spaces, piece * 128 : (piece + 1) * 128
            ]
    parts = []
    for space in range(spaces):
        line = codes_ref[space : space + 1, :].astype(jnp.int32)
        cells = []
        for at in range(subs):
            index = jnp.broadcast_to(line[:, at * rows : (at + 1) * rows], (depth, rows))
            value = None
            for piece in range(words // 128):
                got = jnp.take_along_axis(
                    words_ref[piece, space * depth : (space + 1) * depth, :], index & 127, axis=1
                )
                value = got if value is None else jnp.where(index >= piece * 128, got, value)
            cells.append(value)
        parts.append(jnp.concatenate(cells, axis=1))
    picked_ref[...] = jnp.transpose(jnp.concatenate(parts, axis=0)).astype(BF16)
    tally = jnp.zeros((words, 128), F32)
    word = lax.broadcasted_iota(jnp.int32, (words, subs * rows), 0).astype(F32)
    lane = lax.broadcasted_iota(jnp.int32, (subs * rows, 128), 1)
    for space in range(spaces):
        hot = (word == codes_ref[space : space + 1, :]).astype(F32).astype(BF16)
        tally = tally + jnp.dot(
            hot, (lane == space).astype(F32).astype(BF16), preferred_element_type=F32
        )
    tally_ref[...] = tally


def place_kernel(direct, count, slot_ref, picked_ref, *refs):
    messages, refs = refs[:count], refs[count:]
    if not direct:
        messages = [messages[0].at[at] for at in range(messages[0].shape[0])]
    subs = len(messages)
    spread = subs if direct else 1
    pieces, rebuilt, residual_ref = refs[: -1 - spread], refs[-1 - spread : -1], refs[-1]
    rows = slot_ref.shape[0]
    total = sum(piece.shape[1] for piece in pieces)
    column = lax.broadcasted_iota(jnp.int32, (rows, total), 1).astype(F32)
    for at in range(subs):
        chosen = (column == slot_ref[:, at : at + 1]).astype(F32).astype(BF16)
        stacked = jnp.concatenate([piece[at] for piece in pieces], axis=0)
        centre = jnp.dot(chosen, stacked, preferred_element_type=F32)
        span = slice(at * rows, (at + 1) * rows)
        out = rebuilt[at] if direct else rebuilt[0].at[at]
        out[...] = (centre + picked_ref[span, :].astype(F32)).astype(BF16)
        residual_ref[span, :] = (messages[at][:rows, :].astype(F32) - centre).astype(BF16)


def sums_kernel(lists, direct, codes_ref, residual_ref, tally_ref, after_ref, *refs):
    outs, total_ref = refs[:-1], refs[-1]
    spaces, rows = codes_ref.shape
    width = residual_ref.shape[1]
    words = tally_ref.shape[0]
    depth = width // spaces
    share = words // lists
    word = lax.broadcasted_iota(jnp.int32, (words, rows), 0).astype(F32)
    owner = lax.broadcasted_iota(jnp.int32, (rows, width), 1) // depth
    residual = residual_ref[...]
    total = jnp.zeros((words, width), F32)
    for space in range(spaces):
        hot = (word == codes_ref[space : space + 1, :]).astype(F32).astype(BF16)
        part = jnp.where(owner == space, residual, jnp.zeros_like(residual))
        total = total + jnp.dot(hot, part, preferred_element_type=F32)
    total_ref[...] = total
    me = lax.axis_index("lists")
    for step in range(lists):
        out = outs[step] if direct else outs[0].at[step]
        at = (me ^ step) if direct else step
        span = pl.ds(pl.multiple_of(at * share, share), share)
        if direct:
            halves = width // 128
            for half in range(halves):
                out[half * share : (half + 1) * share, :] = total_ref[
                    span, half * 128 : (half + 1) * 128
                ].astype(BF16)
            counts = tally_ref[span, :]
            fold = 128 // spaces
            lines = share // fold
            out[halves * share :, :] = jnp.concatenate(
                [counts[at * lines : (at + 1) * lines, :spaces] for at in range(fold)], axis=1
            ).astype(BF16)
        else:
            out[:, :width] = total_ref[span, :].astype(BF16)
            out[:, width:] = tally_ref[span, :].astype(BF16)


def refine_kernel(spaces, direct, codebook_ref, *refs):
    pieces, (out_ref, turned_ref) = refs[:-3], refs[-2:]
    total = None
    for piece in pieces:
        if direct:
            value = piece[...].astype(F32)
        else:
            value = jnp.sum(piece[...].astype(F32), axis=0)
        total = value if total is None else total + value
    share, width = turned_ref.shape[1], turned_ref.shape[0]
    depth = width // spaces
    span = share * depth
    if direct:
        halves = width // 128
        fold = 128 // spaces
        for half in range(halves):
            turned_ref[half * 128 : (half + 1) * 128, :] = jnp.transpose(
                total[half * share : (half + 1) * share]
            )
        packed = jnp.transpose(total[halves * share :])
        tally = jnp.concatenate(
            [packed[at * spaces : (at + 1) * spaces] for at in range(fold)], axis=1
        )
    else:
        turned = jnp.transpose(total)
        turned_ref[...] = turned[:width, :]
        tally = turned[width : width + spaces, :]
    word = lax.broadcasted_iota(jnp.int32, (share, span), 0)
    cell = lax.broadcasted_iota(jnp.int32, (share, span), 1)

    def spread(value, table):
        high = value.astype(BF16)
        rest = value - high.astype(F32)
        low = rest.astype(BF16)
        return jnp.dot(high, table, preferred_element_type=F32) + jnp.dot(
            low, table, preferred_element_type=F32
        )

    sums = jnp.zeros((spaces, span), F32)
    for at in range(depth):
        table = (cell == word * depth + at).astype(F32).astype(BF16)
        sums = sums + spread(turned_ref[pl.ds(at, spaces, stride=depth), :], table)
    counts = spread(tally, (cell // depth == word).astype(F32).astype(BF16))
    me = lax.axis_index("lists")
    if span % 128 == 0:
        prior = codebook_ref[:, pl.ds(pl.multiple_of(me * span, span), span)].astype(F32)
    else:
        prior = jnp.zeros((spaces, span), F32)
        for at in range(codebook_ref.shape[1] // span):
            block = codebook_ref[:, at * span : (at + 1) * span].astype(F32)
            prior = prior + jnp.where(me == at, block, 0.0)
    out_ref[...] = (sums + prior) / (counts + 1.0)


def restore_kernel(direct, passages_ref, rotation_ref, *refs):
    pieces, (out_ref, token_ref) = refs[:-3], refs[-2:]
    token_ref[...] = jnp.zeros(token_ref.shape, F32)
    me = lax.axis_index("sub")
    if direct:
        blocks = [piece[...] for piece in pieces]
    else:
        blocks = [pieces[0][at] for at in range(pieces[0].shape[0])]
    width = blocks[0].shape[1]
    total = None
    for at, block in enumerate(blocks):
        start = (me ^ at) * width if direct else at * width
        if direct:
            start = pl.multiple_of(start, width)
        value = lax.dot_general(
            block,
            rotation_ref[:, pl.ds(start, width)],
            (((1,), (1,)), ((), ())),
            preferred_element_type=F32,
        )
        total = value if total is None else total + value
    out_ref[...] = (passages_ref[...].astype(F32) - total).astype(BF16)


def swap(value, axis, step):
    count = lax.axis_size(axis)
    return lax.ppermute(value, axis, [(at, at ^ step) for at in range(count)])


def exchange(values, axis, order=None):
    came = {0: values[0]}
    for step in order or range(1, len(values)):
        came[step] = swap(values[step], axis, step)
    return [came[step] for step in range(len(values))]


def all_swap(value, axis):
    return lax.all_to_all(value, axis, split_axis=0, concat_axis=0, tiled=True)


def body(passages, rotation, centroids, list_slot, list_ids, codes, codebook):
    lists = lax.axis_size("lists")
    subs = lax.axis_size("sub")
    rows, model = passages.shape
    held, width = centroids.shape
    cap = 2 * rows // lists
    spaces = codebook.shape[0]
    depth = width // spaces
    words = codebook.shape[1] // depth
    share = words // lists
    direct = max(lists, subs) <= DIRECT
    shape = jax.ShapeDtypeStruct

    tables = call(
        tables_kernel,
        shape((lists * subs, rows), jnp.int32),
        TABLES_FLOPS,
        0,
        list_ids.reshape(1, rows),
        list_slot.reshape(-1, 128),
    )
    own_tables = tables
    tables = all_swap(tables.reshape(lists * subs, 1, rows), ("lists", "sub"))
    tables = tables.reshape(lists * subs, rows)

    pieces = call(
        functools.partial(fetch_kernel, held, lists, direct),
        [shape((subs, cap, width), BF16)] * lists
        if direct
        else [shape((lists * subs, cap, width), BF16)],
        600_000_000,
        held * width * 2,
        tables,
        centroids,
        scratch=[
            pltpu.VMEM((lists * subs, cap), jnp.int32),
            pltpu.SMEM((lists * subs, cap), jnp.int32),
            pltpu.SemaphoreType.DMA,
        ],
    )
    fetched = pieces[0]
    if direct:
        pieces = exchange(pieces, "lists")
    else:
        found = all_swap(pieces[0].reshape(lists, subs * cap, width), "lists")
        found = found.reshape(lists, subs, cap, width)
        pieces = [jnp.swapaxes(found, 0, 1).reshape(subs, lists * cap, width)]

    long = rows + spaces // (width // rows)
    messages = call(
        functools.partial(rotate_kernel, subs, direct),
        [shape((long, width), BF16)] * subs if direct else [shape((subs, long, width), BF16)],
        1_000,
        1_000,
        passages,
        rotation,
        codes,
        fetched,
        loose=1,
        scratch=[pltpu.VMEM((codes.shape[1], rows), F32)],
    )
    messages = exchange(messages, "sub") if direct else [all_swap(messages[0], "sub")]

    picked, slot, codes_t, tally = call(
        functools.partial(lookup_kernel, held, lists, direct, cap, len(messages)),
        [
            shape((subs * rows, width), BF16),
            shape((rows, rows), F32),
            shape((spaces, subs * rows), F32),
            shape((words, 128), F32),
        ],
        1_000_000,
        1_000,
        tables,
        codebook,
        *messages,
        scratch=[pltpu.VMEM((words * depth, 128), F32), pltpu.VMEM((words // 128, width, 128), F32)],
    )
    *rebuilt, residual = call(
        functools.partial(place_kernel, direct, len(messages)),
        ([shape((rows, width), BF16)] * subs if direct else [shape((subs, rows, width), BF16)])
        + [shape((subs * rows, width), BF16)],
        300_000_000,
        2_000_000,
        slot,
        picked,
        *messages,
        *pieces,
    )
    rebuilt = exchange(rebuilt, "sub") if direct else [all_swap(rebuilt[0], "sub")]
    sums = call(
        functools.partial(sums_kernel, lists, direct),
        [shape((width // 128 * share + share * spaces // 128, 128), BF16)] * lists
        if direct
        else [shape((lists, share, width + 128), BF16)],
        2_000_000_000,
        1_000_000,
        codes_t,
        residual,
        tally,
        rebuilt[1] if direct else residual,
        loose=1,
        scratch=[pltpu.VMEM((words, width), F32)],
    )
    sums = exchange(sums, "lists", (3, 2, 1)) if direct else [all_swap(sums[0], "lists")]
    recon_error, token = call(
        functools.partial(restore_kernel, direct),
        [shape((rows, model), BF16), shape((8, 128), F32)],
        1_000,
        1_000,
        passages,
        rotation,
        *rebuilt,
        sums[3] if direct else sums[0],
        loose=1,
    )
    new_codebook = call(
        functools.partial(refine_kernel, spaces, direct),
        shape((spaces, share * depth), F32),
        100_000_000,
        500_000,
        codebook,
        *sums,
        token,
        loose=1,
        scratch=[pltpu.VMEM((width, share), F32)],
    )
    return (recon_error, new_codebook)


def solution(mesh):
    return jax.shard_map(
        body,
        mesh=mesh,
        in_specs=(
            P(("groups", "lists", "sub"), None),
            P(),
            P("lists", "sub"),
            P("groups"),
            P(("groups", "lists", "sub")),
            P(("groups", "lists", "sub"), None),
            P("sub", None),
        ),
        out_specs=(P(("groups", "lists", "sub"), None), P(("groups", "sub"), "lists")),
        check_vma=False,
    )
```

```python
import functools

import jax
import jax.numpy as jnp
from jax import lax
from jax.experimental import pallas as pl
from jax.experimental.pallas import tpu as pltpu
from jax.sharding import PartitionSpec as P

BF16 = jnp.bfloat16
F32 = jnp.float32
VMEM_LIMIT = 32 * 1024 * 1024
FETCH_FLOPS = 600_000_000
ORDER_FLOPS = 3_000_000_000
ORDER_REST_FLOPS = 12_000_000_000
TABLES_FLOPS = 8_000_000_000
DIRECT = 4


def call(kernel, out_shape, flops, nbytes, *args, scratch=(), loose=0, limit=VMEM_LIMIT):
    whole = lambda: pl.BlockSpec(memory_space=pltpu.VMEM)
    return pl.pallas_call(
        kernel,
        out_shape=out_shape,
        in_specs=[whole() for _ in args[: len(args) - loose]]
        + [pl.BlockSpec(memory_space=pl.ANY)] * loose,
        out_specs=jax.tree.map(lambda _: whole(), out_shape),
        scratch_shapes=list(scratch),
        compiler_params=pltpu.CompilerParams(vmem_limit_bytes=limit),
        cost_estimate=pl.CostEstimate(flops=flops, bytes_accessed=nbytes, transcendentals=0),
    )(*args)


def strict_before(width):
    row = lax.broadcasted_iota(jnp.int32, (width, width), 0)
    col = lax.broadcasted_iota(jnp.int32, (width, width), 1)
    return (row < col).astype(F32).astype(BF16)


def tables_kernel(ids_ref, slots_ref, out_ref):
    rows = ids_ref.shape[1]
    lines = slots_ref.shape[0]
    ids = jnp.transpose(jnp.concatenate([ids_ref[...].astype(F32)] * 128, axis=0))[:, :1]
    ids = ids.astype(jnp.int32)
    line = lax.broadcasted_iota(jnp.int32, (rows, lines), 1)
    chosen = (line == (ids >> 7)).astype(F32).astype(BF16)
    table = slots_ref[...]
    high = (table >> 8).astype(F32).astype(BF16)
    low = (table & 255).astype(F32).astype(BF16)
    found = jnp.dot(chosen, high, preferred_element_type=F32) * 256.0 + jnp.dot(
        chosen, low, preferred_element_type=F32
    )
    lane = lax.broadcasted_iota(jnp.int32, (rows, 128), 1)
    found = jnp.transpose(jnp.where(lane == (ids & 127), found, 0.0))
    line = jnp.sum(found, axis=0, keepdims=True).astype(jnp.int32)
    out_ref[...] = jnp.broadcast_to(line, out_ref.shape)


def rotate_kernel(subs, direct, passages_ref, rotation_ref, codes_ref, after_ref, *refs):
    outs, turned_ref = refs[:-1], refs[-1]
    rows, model = passages_ref.shape
    width = model // subs
    spaces = codes_ref.shape[1] // subs
    halves = width // rows
    tail = spaces // halves
    me = lax.axis_index("sub")
    turned_ref[...] = jnp.transpose(codes_ref[...].astype(F32))
    for step in range(subs):
        at = (me ^ step) if direct else step
        out = outs[step] if direct else outs[0].at[step]
        columns = pl.ds(pl.multiple_of(at * width, width), width)
        out[:rows, :] = jnp.dot(
            passages_ref[...], rotation_ref[:, columns], preferred_element_type=F32
        ).astype(BF16)
        for half in range(halves):
            start = pl.multiple_of(at * spaces + half * tail, tail)
            out[rows:, half * rows : (half + 1) * rows] = turned_ref[pl.ds(start, tail), :].astype(
                BF16
            )


def near_rows(rows_ref, owner, subs):
    me = lax.axis_index("sub")
    return jnp.concatenate(
        [rows_ref[pl.ds(owner * subs + (me ^ step), 1), :] for step in range(subs)], axis=0
    )


def index_slots(held, rows_refs, index_ref, spot_ref):
    blocks, cap = index_ref.shape
    rows = rows_refs[0].shape[1]
    group = min(cap, 16)
    me = lax.axis_index("lists")
    local = jnp.concatenate([ref[...] for ref in rows_refs], axis=0) - me * held
    mine = jnp.logical_and(local >= 0, local < held)
    flags = mine.astype(F32)
    rank = jnp.dot(flags.astype(BF16), strict_before(rows), preferred_element_type=F32)
    rank = jnp.where(mine, rank, -1.0)
    local = jnp.where(mine, local, 0)
    pad = max(128 // blocks, 1)
    rank = jnp.transpose(jnp.concatenate([rank] * pad, axis=0))
    local = jnp.transpose(jnp.concatenate([local.astype(F32)] * pad, axis=0))
    slot = lax.broadcasted_iota(jnp.int32, (rows, cap), 1).astype(F32)
    index = []
    for block in range(blocks):
        chosen = slot == rank[:, block : block + 1]
        index.append(
            jnp.sum(jnp.where(chosen, local[:, block : block + 1], 0.0), axis=0, keepdims=True)
        )
    index = jnp.concatenate(index, axis=0).astype(jnp.int32)
    index_ref[...] = index & -16
    within = lax.broadcasted_iota(jnp.int32, (blocks, cap), 1) & (group - 1)
    spot = (within * 16 + (index & 15)).astype(F32)
    spot_ref[...] = jnp.transpose(jnp.concatenate([spot] * pad, axis=0))


def fetch_blocks(first, spot_ref, scalar_ref, centroids_ref, out_ref):
    blocks, cap = out_ref.shape[0], out_ref.shape[1]
    group = min(cap, 16)
    lane = lax.broadcasted_iota(jnp.int32, (cap, group * 16), 1).astype(F32)
    for at in range(blocks):
        block = first + at
        chosen = (lane == spot_ref[:, block : block + 1]).astype(F32).astype(BF16)
        for start in range(0, cap, group):
            tiles = [
                centroids_ref[pl.ds(pl.multiple_of(scalar_ref[block, slot], 16), 16), :]
                for slot in range(start, start + group)
            ]
            out_ref[at, start : start + group, :] = jnp.dot(
                chosen[start : start + group],
                jnp.concatenate(tiles, axis=0),
                preferred_element_type=F32,
            ).astype(BF16)


def fetch_kernel(held, direct, rows_ref, centroids_ref, *refs):
    outs = refs[:-4]
    index_ref, spot_ref, scalar_ref, sem = refs[-4:]
    blocks = index_ref.shape[0]
    me = lax.axis_index("lists")
    if direct:
        lists = rows_ref.shape[0] // outs[0].shape[0]
        near = [near_rows(rows_ref, me ^ step, blocks // lists) for step in range(lists)]
        index_slots(held, near, index_ref, spot_ref)
    else:
        index_slots(held, [rows_ref], index_ref, spot_ref)
    move = pltpu.make_async_copy(index_ref, scalar_ref, sem)
    move.start()
    move.wait()
    for at, out in enumerate(outs):
        first = (at + 1) * out.shape[0] if direct else 0
        fetch_blocks(first, spot_ref, scalar_ref, centroids_ref, out)


def fetch_rest_kernel(steps, index_ref, spot_ref, centroids_ref, *refs):
    outs, (scalar_ref, sem) = refs[:-2], refs[-2:]
    move = pltpu.make_async_copy(index_ref, scalar_ref, sem)
    move.start()
    move.wait()
    for step, out in zip(steps, outs):
        fetch_blocks(step * out.shape[0], spot_ref, scalar_ref, centroids_ref, out)


def lookup_kernel(direct, count, codebook_ref, *refs):
    messages, refs = refs[:count], refs[count:]
    picked_ref, codes_ref, tally_ref, turned_ref, words_ref = refs
    if not direct:
        messages = [messages[0].at[at] for at in range(messages[0].shape[0])]
    subs = len(messages)
    width = messages[0].shape[1]
    spaces = codes_ref.shape[0]
    rows = codes_ref.shape[1] // subs
    depth = width // spaces
    words = words_ref.shape[0] * 128
    halves = width // rows
    tail = spaces // halves
    for at in range(subs):
        for half in range(halves):
            codes_ref[half * tail : (half + 1) * tail, at * rows : (at + 1) * rows] = messages[at][
                rows:, half * rows : (half + 1) * rows
            ].astype(F32)
    for at in range(0, words * depth, 128):
        block = jnp.concatenate(
            [codebook_ref[:, at : at + 128].astype(F32)] * (128 // spaces), axis=0
        )
        turned_ref[at : at + 128, :] = jnp.transpose(block)
    for at in range(depth):
        block = jnp.transpose(turned_ref[pl.ds(at, words, stride=depth), :])
        for piece in range(words // 128):
            words_ref[piece, pl.ds(at, spaces, stride=depth), :] = block[
                :spaces, piece * 128 : (piece + 1) * 128
            ]
    parts = []
    for space in range(spaces):
        line = codes_ref[space : space + 1, :].astype(jnp.int32)
        cells = []
        for at in range(subs):
            index = jnp.broadcast_to(line[:, at * rows : (at + 1) * rows], (depth, rows))
            value = None
            for piece in range(words // 128):
                got = jnp.take_along_axis(
                    words_ref[piece, space * depth : (space + 1) * depth, :], index & 127, axis=1
                )
                value = got if value is None else jnp.where(index >= piece * 128, got, value)
            cells.append(value)
        parts.append(jnp.concatenate(cells, axis=1))
    picked_ref[...] = jnp.transpose(jnp.concatenate(parts, axis=0)).astype(BF16)
    if direct:
        low_words = words * spaces // tally_ref.shape[1]
        codes = codes_ref[...].astype(jnp.int32)
        high, low = codes // low_words, codes % low_words
        highs = [(high == at).astype(F32).astype(BF16) for at in range(words // low_words)]
        lows = [(low == at).astype(F32).astype(BF16) for at in range(low_words)]
        pairs = lax.dot_general(
            jnp.concatenate(lows, axis=0),
            jnp.concatenate(highs, axis=0),
            (((1,), (1,)), ((), ())),
            preferred_element_type=F32,
        )
        first = lax.broadcasted_iota(jnp.int32, pairs.shape, 0) % spaces
        second = lax.broadcasted_iota(jnp.int32, pairs.shape, 1) % spaces
        pairs = jnp.where(first == second, pairs, 0.0)
        tally_ref[...] = jnp.sum(pairs.reshape(low_words, spaces, pairs.shape[1]), axis=1)
        return
    tally = jnp.zeros((words, 128), F32)
    word = lax.broadcasted_iota(jnp.int32, (words, subs * rows), 0).astype(F32)
    lane = lax.broadcasted_iota(jnp.int32, (subs * rows, 128), 1)
    for space in range(spaces):
        hot = (word == codes_ref[space : space + 1, :]).astype(F32).astype(BF16)
        tally = tally + jnp.dot(
            hot, (lane == space).astype(F32).astype(BF16), preferred_element_type=F32
        )
    tally_ref[...] = tally


def in_order(slot_ref, at, start, pieces):
    rows = slot_ref.shape[0]
    total = sum(piece.shape[1] for piece in pieces)
    column = start + lax.broadcasted_iota(jnp.int32, (rows, total), 1).astype(F32)
    chosen = (column == slot_ref[:, at : at + 1]).astype(F32).astype(BF16)
    stacked = jnp.concatenate([piece[at] for piece in pieces], axis=0)
    return jnp.dot(chosen, stacked, preferred_element_type=F32)


def order_kernel(held, lists, direct, cap, rows_ref, *refs):
    pieces, (slot_ref, centre_ref) = refs[:-2], refs[-2:]
    rows = rows_ref.shape[1]
    subs = pieces[0].shape[0]
    me = lax.axis_index("lists")
    if direct:
        tables = near_rows(rows_ref, me, subs)
    else:
        tables = rows_ref[pl.ds(pl.multiple_of(me * subs, subs), subs), :]
    owners = tables // held
    rank = jnp.zeros((subs, rows), F32)
    flags = [(owners == at).astype(F32) for at in range(lists)]
    stacked = jnp.concatenate(flags, axis=0)
    before = jnp.dot(stacked.astype(BF16), strict_before(rows), preferred_element_type=F32)
    for at in range(lists):
        rank = rank + flags[at] * before[at * subs : (at + 1) * subs]
    place = (owners ^ me) if direct else owners
    slot = place.astype(F32) * cap + rank
    slot_ref[...] = jnp.transpose(jnp.concatenate([slot] * (rows // subs), axis=0))
    for at in range(subs):
        centre_ref[at * rows : (at + 1) * rows, :] = in_order(slot_ref, at, 0.0, pieces).astype(BF16)


def order_rest_kernel(start, slot_ref, part_ref, piece_ref, centre_ref):
    rows = slot_ref.shape[0]
    for at in range(piece_ref.shape[0]):
        span = slice(at * rows, (at + 1) * rows)
        rest = in_order(slot_ref, at, start, [piece_ref])
        centre_ref[span, :] = (part_ref[span, :].astype(F32) + rest).astype(BF16)


def place_kernel(direct, count, centre_ref, picked_ref, *refs):
    messages, refs = refs[:count], refs[count:]
    if not direct:
        messages = [messages[0].at[at] for at in range(messages[0].shape[0])]
    subs = len(messages)
    rebuilt, residual_ref = refs[:-1], refs[-1]
    rows = centre_ref.shape[0] // subs
    for at in range(subs):
        span = slice(at * rows, (at + 1) * rows)
        centre = centre_ref[span, :].astype(F32)
        out = rebuilt[at] if direct else rebuilt[0].at[at]
        out[...] = (centre + picked_ref[span, :].astype(F32)).astype(BF16)
        residual_ref[span, :] = (messages[at][:rows, :].astype(F32) - centre).astype(BF16)


def sums_kernel(lists, direct, codes_ref, residual_ref, tally_ref, after_ref, *refs):
    outs, total_ref = refs[:-1], refs[-1]
    spaces, rows = codes_ref.shape
    width = residual_ref.shape[1]
    words = total_ref.shape[0]
    depth = width // spaces
    share = words // lists
    word = lax.broadcasted_iota(jnp.int32, (words, rows), 0).astype(F32)
    owner = lax.broadcasted_iota(jnp.int32, (rows, width), 1) // depth
    residual = residual_ref[...]
    total = jnp.zeros((words, width), F32)
    for space in range(spaces):
        hot = (word == codes_ref[space : space + 1, :]).astype(F32).astype(BF16)
        part = jnp.where(owner == space, residual, jnp.zeros_like(residual))
        total = total + jnp.dot(hot, part, preferred_element_type=F32)
    total_ref[...] = total
    me = lax.axis_index("lists")
    for step in range(lists):
        out = outs[step] if direct else outs[0].at[step]
        at = (me ^ step) if direct else step
        span = pl.ds(pl.multiple_of(at * share, share), share)
        if direct:
            halves = width // 128
            for half in range(halves):
                out[half * share : (half + 1) * share, :] = total_ref[
                    span, half * 128 : (half + 1) * 128
                ].astype(BF16)
            lanes = pl.ds(pl.multiple_of(at * 128, 128), 128)
            out[halves * share :, :] = tally_ref[:, lanes].astype(BF16)
        else:
            out[:, :width] = total_ref[span, :].astype(BF16)
            out[:, width:] = tally_ref[span, :].astype(BF16)


def refine_kernel(spaces, direct, codebook_ref, *refs):
    pieces, (out_ref, turned_ref) = refs[:-3], refs[-2:]
    total = None
    for piece in pieces:
        if direct:
            value = piece[...].astype(F32)
        else:
            value = jnp.sum(piece[...].astype(F32), axis=0)
        total = value if total is None else total + value
    share, width = turned_ref.shape[1], turned_ref.shape[0]
    depth = width // spaces
    span = share * depth
    if direct:
        halves = width // 128
        fold = 128 // spaces
        for half in range(halves):
            turned_ref[half * 128 : (half + 1) * 128, :] = jnp.transpose(
                total[half * share : (half + 1) * share]
            )
        packed = jnp.transpose(total[halves * share :])
        tally = jnp.concatenate(
            [packed[at * spaces : (at + 1) * spaces] for at in range(fold)], axis=1
        )
    else:
        turned = jnp.transpose(total)
        turned_ref[...] = turned[:width, :]
        tally = turned[width : width + spaces, :]
    word = lax.broadcasted_iota(jnp.int32, (share, span), 0)
    cell = lax.broadcasted_iota(jnp.int32, (share, span), 1)

    def spread(value, table):
        high = value.astype(BF16)
        rest = value - high.astype(F32)
        low = rest.astype(BF16)
        return jnp.dot(high, table, preferred_element_type=F32) + jnp.dot(
            low, table, preferred_element_type=F32
        )

    sums = jnp.zeros((spaces, span), F32)
    for at in range(depth):
        table = (cell == word * depth + at).astype(F32).astype(BF16)
        sums = sums + spread(turned_ref[pl.ds(at, spaces, stride=depth), :], table)
    counts = spread(tally, (cell // depth == word).astype(F32).astype(BF16))
    me = lax.axis_index("lists")
    if span % 128 == 0:
        prior = codebook_ref[:, pl.ds(pl.multiple_of(me * span, span), span)].astype(F32)
    else:
        prior = jnp.zeros((spaces, span), F32)
        for at in range(codebook_ref.shape[1] // span):
            block = codebook_ref[:, at * span : (at + 1) * span].astype(F32)
            prior = prior + jnp.where(me == at, block, 0.0)
    out_ref[...] = (sums + prior) / (counts + 1.0)


def restore_kernel(direct, passages_ref, rotation_ref, *refs):
    pieces, (out_ref, token_ref) = refs[:-3], refs[-2:]
    token_ref[...] = jnp.zeros(token_ref.shape, F32)
    me = lax.axis_index("sub")
    if direct:
        blocks = [piece[...] for piece in pieces]
    else:
        blocks = [pieces[0][at] for at in range(pieces[0].shape[0])]
    width = blocks[0].shape[1]
    total = None
    for at, block in enumerate(blocks):
        start = (me ^ at) * width if direct else at * width
        if direct:
            start = pl.multiple_of(start, width)
        value = lax.dot_general(
            block,
            rotation_ref[:, pl.ds(start, width)],
            (((1,), (1,)), ((), ())),
            preferred_element_type=F32,
        )
        total = value if total is None else total + value
    out_ref[...] = (passages_ref[...].astype(F32) - total).astype(BF16)


def swap(value, axis, step):
    count = lax.axis_size(axis)
    return lax.ppermute(value, axis, [(at, at ^ step) for at in range(count)])


def exchange(values, axis, order=None):
    came = {0: values[0]}
    for step in order or range(1, len(values)):
        came[step] = swap(values[step], axis, step)
    return [came[step] for step in range(len(values))]


def all_swap(value, axis):
    return lax.all_to_all(value, axis, split_axis=0, concat_axis=0, tiled=True)


def body(passages, rotation, centroids, list_slot, list_ids, codes, codebook):
    lists = lax.axis_size("lists")
    subs = lax.axis_size("sub")
    rows, model = passages.shape
    held, width = centroids.shape
    cap = 2 * rows // lists
    spaces = codebook.shape[0]
    depth = width // spaces
    words = codebook.shape[1] // depth
    share = words // lists
    direct = max(lists, subs) <= DIRECT
    shape = jax.ShapeDtypeStruct

    tables = call(
        tables_kernel,
        shape((lists * subs, rows), jnp.int32),
        TABLES_FLOPS,
        0,
        list_ids.reshape(1, rows),
        list_slot.reshape(-1, 128),
    )
    own_tables = tables
    tables = all_swap(tables.reshape(lists * subs, 1, rows), ("lists", "sub"))
    tables = tables.reshape(lists * subs, rows)

    blocks = lists * subs
    scalars = [pltpu.SMEM((blocks, cap), jnp.int32), pltpu.SemaphoreType.DMA]
    early = lists // 2 if direct else 1
    *pieces, index, spot = call(
        functools.partial(fetch_kernel, held, direct),
        [shape((subs if direct else blocks, cap, width), BF16)] * early
        + [shape((blocks, cap), jnp.int32), shape((cap, max(blocks, 128)), F32)],
        FETCH_FLOPS,
        held * width * 2,
        tables,
        centroids,
        scratch=scalars,
    )
    fetched = pieces[0]
    if direct:
        late = list(range(early + 1, lists)) + [0]
        rest = call(
            functools.partial(fetch_rest_kernel, late),
            [shape((subs, cap, width), BF16)] * len(late),
            0,
            0,
            index,
            spot,
            centroids,
            scratch=scalars,
        )
        fetched = rest[-1]
        pieces = exchange([fetched] + list(pieces) + list(rest[:-1]), "lists")
    else:
        found = all_swap(pieces[0].reshape(lists, subs * cap, width), "lists")
        found = found.reshape(lists, subs, cap, width)
        pieces = [jnp.swapaxes(found, 0, 1).reshape(subs, lists * cap, width)]

    long = rows + spaces // (width // rows)
    messages = call(
        functools.partial(rotate_kernel, subs, direct),
        [shape((long, width), BF16)] * subs if direct else [shape((subs, long, width), BF16)],
        0,
        0,
        passages,
        rotation,
        codes,
        fetched,
        loose=1,
        scratch=[pltpu.VMEM((codes.shape[1], rows), F32)],
    )
    messages = exchange(messages, "sub") if direct else [all_swap(messages[0], "sub")]

    picked, codes_t, tally = call(
        functools.partial(lookup_kernel, direct, len(messages)),
        [
            shape((subs * rows, width), BF16),
            shape((spaces, subs * rows), F32),
            shape((share * spaces // 128, lists * 128) if direct else (words, 128), F32),
        ],
        0,
        0,
        codebook,
        *messages,
        scratch=[
            pltpu.VMEM((words * depth, 128), F32),
            pltpu.VMEM((words // 128, width, 128), F32),
        ],
    )
    first = pieces[:-1] if direct else pieces
    slot, centre = call(
        functools.partial(order_kernel, held, lists, direct, cap),
        [shape((rows, rows), F32), shape((subs * rows, width), BF16)],
        ORDER_FLOPS,
        0,
        tables,
        *first,
    )
    if direct:
        centre = call(
            functools.partial(order_rest_kernel, float((lists - 1) * cap)),
            shape((subs * rows, width), BF16),
            ORDER_REST_FLOPS,
            0,
            slot,
            centre,
            pieces[-1],
        )
    *rebuilt, residual = call(
        functools.partial(place_kernel, direct, len(messages)),
        ([shape((rows, width), BF16)] * subs if direct else [shape((subs, rows, width), BF16)])
        + [shape((subs * rows, width), BF16)],
        0,
        0,
        centre,
        picked,
        *messages,
    )
    rebuilt = exchange(rebuilt, "sub") if direct else [all_swap(rebuilt[0], "sub")]
    sums = call(
        functools.partial(sums_kernel, lists, direct),
        [shape((width // 128 * share + share * spaces // 128, 128), BF16)] * lists
        if direct
        else [shape((lists, share, width + 128), BF16)],
        2_000_000_000,
        1_000_000,
        codes_t,
        residual,
        tally,
        rebuilt[1] if direct else residual,
        loose=1,
        scratch=[pltpu.VMEM((words, width), F32)],
    )
    sums = exchange(sums, "lists", (3, 2, 1)) if direct else [all_swap(sums[0], "lists")]
    recon_error, token = call(
        functools.partial(restore_kernel, direct),
        [shape((rows, model), BF16), shape((8, 128), F32)],
        1_000,
        1_000,
        passages,
        rotation,
        *rebuilt,
        sums[3] if direct else sums[0],
        loose=1,
    )
    new_codebook = call(
        functools.partial(refine_kernel, spaces, direct),
        shape((spaces, share * depth), F32),
        100_000_000,
        500_000,
        codebook,
        *sums,
        token,
        loose=1,
        scratch=[pltpu.VMEM((width, share), F32)],
    )
    return (recon_error, new_codebook)


def solution(mesh):
    return jax.shard_map(
        body,
        mesh=mesh,
        in_specs=(
            P(("groups", "lists", "sub"), None),
            P(),
            P("lists", "sub"),
            P("groups"),
            P(("groups", "lists", "sub")),
            P(("groups", "lists", "sub"), None),
            P("sub", None),
        ),
        out_specs=(P(("groups", "lists", "sub"), None), P(("groups", "sub"), "lists")),
        check_vma=False,
    )
```

```python
import functools

import jax
import jax.numpy as jnp
from jax import lax
from jax.experimental import pallas as pl
from jax.experimental.pallas import tpu as pltpu
from jax.sharding import PartitionSpec as P

BF16 = jnp.bfloat16
F32 = jnp.float32
VMEM_LIMIT = 32 * 1024 * 1024
FETCH_FLOPS = 600_000_000
ORDER_FLOPS = 3_000_000_000
ORDER_REST_FLOPS = 12_000_000_000
TABLES_FLOPS = 8_000_000_000
DIRECT = 4


def call(kernel, out_shape, flops, nbytes, *args, scratch=(), loose=0, limit=VMEM_LIMIT):
    whole = lambda: pl.BlockSpec(memory_space=pltpu.VMEM)
    return pl.pallas_call(
        kernel,
        out_shape=out_shape,
        in_specs=[whole() for _ in args[: len(args) - loose]]
        + [pl.BlockSpec(memory_space=pl.ANY)] * loose,
        out_specs=jax.tree.map(lambda _: whole(), out_shape),
        scratch_shapes=list(scratch),
        compiler_params=pltpu.CompilerParams(vmem_limit_bytes=limit),
        cost_estimate=pl.CostEstimate(flops=flops, bytes_accessed=nbytes, transcendentals=0),
    )(*args)


def strict_before(width):
    row = lax.broadcasted_iota(jnp.int32, (width, width), 0)
    col = lax.broadcasted_iota(jnp.int32, (width, width), 1)
    return (row < col).astype(F32).astype(BF16)


def tables_kernel(ids_ref, slots_ref, out_ref):
    rows = ids_ref.shape[1]
    lines = slots_ref.shape[0]
    ids = jnp.transpose(jnp.concatenate([ids_ref[...].astype(F32)] * 128, axis=0))[:, :1]
    ids = ids.astype(jnp.int32)
    line = lax.broadcasted_iota(jnp.int32, (rows, lines), 1)
    chosen = (line == (ids >> 7)).astype(F32).astype(BF16)
    table = slots_ref[...]
    high = (table >> 8).astype(F32).astype(BF16)
    low = (table & 255).astype(F32).astype(BF16)
    found = jnp.dot(chosen, high, preferred_element_type=F32) * 256.0 + jnp.dot(
        chosen, low, preferred_element_type=F32
    )
    lane = lax.broadcasted_iota(jnp.int32, (rows, 128), 1)
    found = jnp.transpose(jnp.where(lane == (ids & 127), found, 0.0))
    line = jnp.sum(found, axis=0, keepdims=True).astype(jnp.int32)
    out_ref[...] = jnp.broadcast_to(line, out_ref.shape)


def rotate_kernel(subs, direct, passages_ref, rotation_ref, codes_ref, after_ref, *refs):
    outs, turned_ref = refs[:-1], refs[-1]
    rows, model = passages_ref.shape
    width = model // subs
    spaces = codes_ref.shape[1] // subs
    halves = width // rows
    tail = spaces // halves
    me = lax.axis_index("sub")
    turned_ref[...] = jnp.transpose(codes_ref[...].astype(F32))
    for step in range(subs):
        at = (me ^ step) if direct else step
        out = outs[step] if direct else outs[0].at[step]
        columns = pl.ds(pl.multiple_of(at * width, width), width)
        out[:rows, :] = jnp.dot(
            passages_ref[...], rotation_ref[:, columns], preferred_element_type=F32
        ).astype(BF16)
        for half in range(halves):
            start = pl.multiple_of(at * spaces + half * tail, tail)
            out[rows:, half * rows : (half + 1) * rows] = turned_ref[pl.ds(start, tail), :].astype(
                BF16
            )


def near_rows(rows_ref, owner, subs):
    me = lax.axis_index("sub")
    return jnp.concatenate(
        [rows_ref[pl.ds(owner * subs + (me ^ step), 1), :] for step in range(subs)], axis=0
    )


def index_slots(held, rows_refs, index_ref, spot_ref, move):
    blocks, cap = index_ref.shape
    rows = rows_refs[0].shape[1]
    group = min(cap, 16)
    me = lax.axis_index("lists")
    local = jnp.concatenate([ref[...] for ref in rows_refs], axis=0) - me * held
    mine = jnp.logical_and(local >= 0, local < held)
    flags = mine.astype(F32)
    rank = jnp.dot(flags.astype(BF16), strict_before(rows), preferred_element_type=F32)
    rank = jnp.where(mine, rank, -1.0)
    local = jnp.where(mine, local, 0)
    pad = max(128 // blocks, 1)
    rank = jnp.transpose(jnp.concatenate([rank] * pad, axis=0))
    local = jnp.transpose(jnp.concatenate([local.astype(F32)] * pad, axis=0))
    slot = lax.broadcasted_iota(jnp.int32, (rows, cap), 1).astype(F32)
    index = []
    for block in range(blocks):
        chosen = slot == rank[:, block : block + 1]
        index.append(
            jnp.sum(jnp.where(chosen, local[:, block : block + 1], 0.0), axis=0, keepdims=True)
        )
    index = jnp.concatenate(index, axis=0).astype(jnp.int32)
    index_ref[...] = index & -16
    move.start()
    within = lax.broadcasted_iota(jnp.int32, (blocks, cap), 1) & (group - 1)
    spot = (within * 16 + (index & 15)).astype(F32)
    spot_ref[...] = jnp.transpose(jnp.concatenate([spot] * pad, axis=0))


def fetch_blocks(first, spot_ref, scalar_ref, centroids_ref, out_ref):
    blocks, cap = out_ref.shape[0], out_ref.shape[1]
    group = min(cap, 16)
    lane = lax.broadcasted_iota(jnp.int32, (cap, group * 16), 1).astype(F32)
    for at in range(blocks):
        block = first + at
        chosen = (lane == spot_ref[:, block : block + 1]).astype(F32).astype(BF16)
        for start in range(0, cap, group):
            tiles = [
                centroids_ref[pl.ds(pl.multiple_of(scalar_ref[block, slot], 16), 16), :]
                for slot in range(start, start + group)
            ]
            out_ref[at, start : start + group, :] = jnp.dot(
                chosen[start : start + group],
                jnp.concatenate(tiles, axis=0),
                preferred_element_type=F32,
            ).astype(BF16)


def fetch_kernel(held, direct, rows_ref, centroids_ref, *refs):
    outs = refs[:-4]
    index_ref, spot_ref, scalar_ref, sem = refs[-4:]
    blocks = index_ref.shape[0]
    me = lax.axis_index("lists")
    if direct:
        lists = rows_ref.shape[0] // outs[0].shape[0]
        near = [near_rows(rows_ref, me ^ step, blocks // lists) for step in range(lists)]
    else:
        near = [rows_ref]
    move = pltpu.make_async_copy(index_ref, scalar_ref, sem)
    index_slots(held, near, index_ref, spot_ref, move)
    move.wait()
    for at, out in enumerate(outs):
        first = (at + 1) * out.shape[0] if direct else 0
        fetch_blocks(first, spot_ref, scalar_ref, centroids_ref, out)


def fetch_rest_kernel(steps, index_ref, spot_ref, centroids_ref, *refs):
    outs, (scalar_ref, sem) = refs[:-2], refs[-2:]
    move = pltpu.make_async_copy(index_ref, scalar_ref, sem)
    move.start()
    move.wait()
    for step, out in zip(steps, outs):
        fetch_blocks(step * out.shape[0], spot_ref, scalar_ref, centroids_ref, out)


def lookup_kernel(direct, count, codebook_ref, *refs):
    messages, refs = refs[:count], refs[count:]
    picked_ref, codes_ref, tally_ref, turned_ref, words_ref = refs
    if not direct:
        messages = [messages[0].at[at] for at in range(messages[0].shape[0])]
    subs = len(messages)
    width = messages[0].shape[1]
    spaces = codes_ref.shape[0]
    rows = codes_ref.shape[1] // subs
    depth = width // spaces
    words = words_ref.shape[0] * 128
    halves = width // rows
    tail = spaces // halves
    for at in range(subs):
        for half in range(halves):
            codes_ref[half * tail : (half + 1) * tail, at * rows : (at + 1) * rows] = messages[at][
                rows:, half * rows : (half + 1) * rows
            ].astype(F32)
    for at in range(0, words * depth, 128):
        block = jnp.concatenate(
            [codebook_ref[:, at : at + 128].astype(F32)] * (128 // spaces), axis=0
        )
        turned_ref[at : at + 128, :] = jnp.transpose(block)
    for at in range(depth):
        block = jnp.transpose(turned_ref[pl.ds(at, words, stride=depth), :])
        for piece in range(words // 128):
            words_ref[piece, pl.ds(at, spaces, stride=depth), :] = block[
                :spaces, piece * 128 : (piece + 1) * 128
            ]
    parts = []
    for space in range(spaces):
        line = codes_ref[space : space + 1, :].astype(jnp.int32)
        cells = []
        for at in range(subs):
            index = jnp.broadcast_to(line[:, at * rows : (at + 1) * rows], (depth, rows))
            value = None
            for piece in range(words // 128):
                got = jnp.take_along_axis(
                    words_ref[piece, space * depth : (space + 1) * depth, :], index & 127, axis=1
                )
                value = got if value is None else jnp.where(index >= piece * 128, got, value)
            cells.append(value)
        parts.append(jnp.concatenate(cells, axis=1))
    picked_ref[...] = jnp.transpose(jnp.concatenate(parts, axis=0)).astype(BF16)
    if direct:
        low_words = words * spaces // tally_ref.shape[1]
        codes = codes_ref[...].astype(jnp.int32)
        high, low = codes // low_words, codes % low_words
        highs = [(high == at).astype(F32).astype(BF16) for at in range(words // low_words)]
        lows = [(low == at).astype(F32).astype(BF16) for at in range(low_words)]
        pairs = lax.dot_general(
            jnp.concatenate(lows, axis=0),
            jnp.concatenate(highs, axis=0),
            (((1,), (1,)), ((), ())),
            preferred_element_type=F32,
        )
        first = lax.broadcasted_iota(jnp.int32, pairs.shape, 0) % spaces
        second = lax.broadcasted_iota(jnp.int32, pairs.shape, 1) % spaces
        pairs = jnp.where(first == second, pairs, 0.0)
        tally_ref[...] = jnp.sum(pairs.reshape(low_words, spaces, pairs.shape[1]), axis=1)
        return
    tally = jnp.zeros((words, 128), F32)
    word = lax.broadcasted_iota(jnp.int32, (words, subs * rows), 0).astype(F32)
    lane = lax.broadcasted_iota(jnp.int32, (subs * rows, 128), 1)
    for space in range(spaces):
        hot = (word == codes_ref[space : space + 1, :]).astype(F32).astype(BF16)
        tally = tally + jnp.dot(
            hot, (lane == space).astype(F32).astype(BF16), preferred_element_type=F32
        )
    tally_ref[...] = tally


def in_order(slot_ref, at, start, pieces):
    rows = slot_ref.shape[0]
    total = sum(piece.shape[1] for piece in pieces)
    column = start + lax.broadcasted_iota(jnp.int32, (rows, total), 1).astype(F32)
    chosen = (column == slot_ref[:, at : at + 1]).astype(F32).astype(BF16)
    stacked = jnp.concatenate([piece[at] for piece in pieces], axis=0)
    return jnp.dot(chosen, stacked, preferred_element_type=F32)


def order_kernel(held, lists, direct, cap, rows_ref, *refs):
    pieces, (slot_ref, centre_ref) = refs[:-2], refs[-2:]
    rows = rows_ref.shape[1]
    subs = pieces[0].shape[0]
    me = lax.axis_index("lists")
    if direct:
        tables = near_rows(rows_ref, me, subs)
    else:
        tables = rows_ref[pl.ds(pl.multiple_of(me * subs, subs), subs), :]
    owners = tables // held
    rank = jnp.zeros((subs, rows), F32)
    flags = [(owners == at).astype(F32) for at in range(lists)]
    stacked = jnp.concatenate(flags, axis=0)
    before = jnp.dot(stacked.astype(BF16), strict_before(rows), preferred_element_type=F32)
    for at in range(lists):
        rank = rank + flags[at] * before[at * subs : (at + 1) * subs]
    place = (owners ^ me) if direct else owners
    slot = place.astype(F32) * cap + rank
    slot_ref[...] = jnp.transpose(jnp.concatenate([slot] * (rows // subs), axis=0))
    for at in range(subs):
        centre_ref[at * rows : (at + 1) * rows, :] = in_order(slot_ref, at, 0.0, pieces).astype(BF16)


def order_rest_kernel(start, slot_ref, part_ref, piece_ref, after_ref, centre_ref):
    rows = slot_ref.shape[0]
    for at in range(piece_ref.shape[0]):
        span = slice(at * rows, (at + 1) * rows)
        rest = in_order(slot_ref, at, start, [piece_ref])
        centre_ref[span, :] = (part_ref[span, :].astype(F32) + rest).astype(BF16)


def place_kernel(direct, count, centre_ref, picked_ref, *refs):
    messages, refs = refs[:count], refs[count:]
    if not direct:
        messages = [messages[0].at[at] for at in range(messages[0].shape[0])]
    subs = len(messages)
    rebuilt, residual_ref = (refs, None) if direct else (refs[:-1], refs[-1])
    rows = centre_ref.shape[0] // subs
    for at in range(subs):
        span = slice(at * rows, (at + 1) * rows)
        centre = centre_ref[span, :].astype(F32)
        out = rebuilt[at] if direct else rebuilt[0].at[at]
        out[...] = (centre + picked_ref[span, :].astype(F32)).astype(BF16)
        if not direct:
            residual_ref[span, :] = (messages[at][:rows, :].astype(F32) - centre).astype(BF16)


def add_words(total, codes, residual):
    spaces, rows = codes.shape
    words, width = total.shape
    depth = width // spaces
    word = lax.broadcasted_iota(jnp.int32, (words, rows), 0).astype(F32)
    owner = lax.broadcasted_iota(jnp.int32, (rows, width), 1) // depth
    for space in range(spaces):
        hot = (word == codes[space : space + 1, :]).astype(F32).astype(BF16)
        part = jnp.where(owner == space, residual, jnp.zeros_like(residual))
        total = total + jnp.dot(hot, part, preferred_element_type=F32)
    return total


def early_sums_kernel(limit, codes_ref, slot_ref, centre_ref, *refs):
    messages, out_ref = refs[:-1], refs[-1]
    rows = slot_ref.shape[0]
    residual = []
    for at, message in enumerate(messages):
        centre = centre_ref[at * rows : (at + 1) * rows, :].astype(F32)
        value = message[:rows, :].astype(F32) - centre
        residual.append(jnp.where(slot_ref[:, at : at + 1] < limit, value, 0.0).astype(BF16))
    total = jnp.zeros(out_ref.shape, F32)
    out_ref[...] = add_words(total, codes_ref[...], jnp.concatenate(residual, axis=0))


def late_sums_kernel(limit, codes_ref, slot_ref, piece_ref, early_ref, tally_ref, *refs):
    messages, outs, total_ref = refs[: piece_ref.shape[0]], refs[piece_ref.shape[0] + 1 : -1], refs[-1]
    rows = slot_ref.shape[0]
    subs, cap, width = piece_ref.shape
    column = limit + lax.broadcasted_iota(jnp.int32, (rows, cap), 1).astype(F32)
    residual, codes = [], []
    for at, message in enumerate(messages):
        chosen = (column == slot_ref[:, at : at + 1]).astype(F32)
        turned = jnp.transpose(chosen)
        used = jnp.sum(turned, axis=1, keepdims=True) > 0.0
        rotated = jnp.dot(turned.astype(BF16), message[:rows, :], preferred_element_type=F32)
        value = rotated - piece_ref[at].astype(F32)
        residual.append(jnp.where(used, value, 0.0).astype(BF16))
        own = codes_ref[:, at * rows : (at + 1) * rows].astype(BF16)
        codes.append(jnp.dot(own, chosen.astype(BF16), preferred_element_type=F32))
    residual = jnp.concatenate(residual, axis=0)
    total_ref[...] = add_words(early_ref[...], jnp.concatenate(codes, axis=1), residual)
    send_sums(True, total_ref, tally_ref, outs)


def sums_kernel(codes_ref, residual_ref, tally_ref, *refs):
    outs, total_ref = refs[:-1], refs[-1]
    total = jnp.zeros(total_ref.shape, F32)
    total_ref[...] = add_words(total, codes_ref[...], residual_ref[...])
    send_sums(False, total_ref, tally_ref, outs)


def send_sums(direct, total_ref, tally_ref, outs):
    words, width = total_ref.shape
    lists = lax.axis_size("lists")
    share = words // lists
    me = lax.axis_index("lists")
    for step in range(lists):
        out = outs[step] if direct else outs[0].at[step]
        at = (me ^ step) if direct else step
        span = pl.ds(pl.multiple_of(at * share, share), share)
        if direct:
            halves = width // 128
            for half in range(halves):
                out[half * share : (half + 1) * share, :] = total_ref[
                    span, half * 128 : (half + 1) * 128
                ].astype(BF16)
            lanes = pl.ds(pl.multiple_of(at * 128, 128), 128)
            out[halves * share :, :] = tally_ref[:, lanes].astype(BF16)
        else:
            out[:, :width] = total_ref[span, :].astype(BF16)
            out[:, width:] = tally_ref[span, :].astype(BF16)


def refine_kernel(spaces, direct, codebook_ref, *refs):
    pieces, (out_ref, turned_ref) = refs[:-3], refs[-2:]
    total = None
    for piece in pieces:
        if direct:
            value = piece[...].astype(F32)
        else:
            value = jnp.sum(piece[...].astype(F32), axis=0)
        total = value if total is None else total + value
    share, width = turned_ref.shape[1], turned_ref.shape[0]
    depth = width // spaces
    span = share * depth
    if direct:
        halves = width // 128
        fold = 128 // spaces
        for half in range(halves):
            turned_ref[half * 128 : (half + 1) * 128, :] = jnp.transpose(
                total[half * share : (half + 1) * share]
            )
        packed = jnp.transpose(total[halves * share :])
        tally = jnp.concatenate(
            [packed[at * spaces : (at + 1) * spaces] for at in range(fold)], axis=1
        )
    else:
        turned = jnp.transpose(total)
        turned_ref[...] = turned[:width, :]
        tally = turned[width : width + spaces, :]
    word = lax.broadcasted_iota(jnp.int32, (share, span), 0)
    cell = lax.broadcasted_iota(jnp.int32, (share, span), 1)

    def spread(value, table):
        high = value.astype(BF16)
        rest = value - high.astype(F32)
        low = rest.astype(BF16)
        return jnp.dot(high, table, preferred_element_type=F32) + jnp.dot(
            low, table, preferred_element_type=F32
        )

    sums = jnp.zeros((spaces, span), F32)
    for at in range(depth):
        table = (cell == word * depth + at).astype(F32).astype(BF16)
        sums = sums + spread(turned_ref[pl.ds(at, spaces, stride=depth), :], table)
    counts = spread(tally, (cell // depth == word).astype(F32).astype(BF16))
    me = lax.axis_index("lists")
    if span % 128 == 0:
        prior = codebook_ref[:, pl.ds(pl.multiple_of(me * span, span), span)].astype(F32)
    else:
        prior = jnp.zeros((spaces, span), F32)
        for at in range(codebook_ref.shape[1] // span):
            block = codebook_ref[:, at * span : (at + 1) * span].astype(F32)
            prior = prior + jnp.where(me == at, block, 0.0)
    out_ref[...] = (sums + prior) / (counts + 1.0)


def restore_kernel(direct, passages_ref, rotation_ref, *refs):
    pieces, (out_ref, token_ref) = refs[:-3], refs[-2:]
    token_ref[...] = jnp.zeros(token_ref.shape, F32)
    me = lax.axis_index("sub")
    if direct:
        blocks = [piece[...] for piece in pieces]
    else:
        blocks = [pieces[0][at] for at in range(pieces[0].shape[0])]
    width = blocks[0].shape[1]
    total = None
    for at, block in enumerate(blocks):
        start = (me ^ at) * width if direct else at * width
        if direct:
            start = pl.multiple_of(start, width)
        value = lax.dot_general(
            block,
            rotation_ref[:, pl.ds(start, width)],
            (((1,), (1,)), ((), ())),
            preferred_element_type=F32,
        )
        total = value if total is None else total + value
    out_ref[...] = (passages_ref[...].astype(F32) - total).astype(BF16)


def swap(value, axis, step):
    count = lax.axis_size(axis)
    return lax.ppermute(value, axis, [(at, at ^ step) for at in range(count)])


def exchange(values, axis, order=None):
    came = {0: values[0]}
    for step in order or range(1, len(values)):
        came[step] = swap(values[step], axis, step)
    return [came[step] for step in range(len(values))]


def all_swap(value, axis):
    return lax.all_to_all(value, axis, split_axis=0, concat_axis=0, tiled=True)


def body(passages, rotation, centroids, list_slot, list_ids, codes, codebook):
    lists = lax.axis_size("lists")
    subs = lax.axis_size("sub")
    rows, model = passages.shape
    held, width = centroids.shape
    cap = 2 * rows // lists
    spaces = codebook.shape[0]
    depth = width // spaces
    words = codebook.shape[1] // depth
    share = words // lists
    direct = max(lists, subs) <= DIRECT
    shape = jax.ShapeDtypeStruct

    tables = call(
        tables_kernel,
        shape((lists * subs, rows), jnp.int32),
        TABLES_FLOPS,
        0,
        list_ids.reshape(1, rows),
        list_slot.reshape(-1, 128),
    )
    own_tables = tables
    tables = all_swap(tables.reshape(lists * subs, 1, rows), ("lists", "sub"))
    tables = tables.reshape(lists * subs, rows)

    blocks = lists * subs
    scalars = [pltpu.SMEM((blocks, cap), jnp.int32), pltpu.SemaphoreType.DMA]
    early = lists // 2 if direct else 1
    *pieces, index, spot = call(
        functools.partial(fetch_kernel, held, direct),
        [shape((subs if direct else blocks, cap, width), BF16)] * early
        + [shape((blocks, cap), jnp.int32), shape((cap, max(blocks, 128)), F32)],
        FETCH_FLOPS,
        held * width * 2,
        tables,
        centroids,
        scratch=scalars,
    )
    fetched = pieces[0]
    if direct:
        late = list(range(early + 1, lists)) + [0]
        rest = call(
            functools.partial(fetch_rest_kernel, late),
            [shape((subs, cap, width), BF16)] * len(late),
            0,
            0,
            index,
            spot,
            centroids,
            scratch=scalars,
        )
        fetched = rest[-1]
        pieces = exchange([fetched] + list(pieces) + list(rest[:-1]), "lists")
    else:
        found = all_swap(pieces[0].reshape(lists, subs * cap, width), "lists")
        found = found.reshape(lists, subs, cap, width)
        pieces = [jnp.swapaxes(found, 0, 1).reshape(subs, lists * cap, width)]

    long = rows + spaces // (width // rows)
    messages = call(
        functools.partial(rotate_kernel, subs, direct),
        [shape((long, width), BF16)] * subs if direct else [shape((subs, long, width), BF16)],
        0,
        0,
        passages,
        rotation,
        codes,
        fetched,
        loose=1,
        scratch=[pltpu.VMEM((codes.shape[1], rows), F32)],
    )
    messages = exchange(messages, "sub") if direct else [all_swap(messages[0], "sub")]

    picked, codes_t, tally = call(
        functools.partial(lookup_kernel, direct, len(messages)),
        [
            shape((subs * rows, width), BF16),
            shape((spaces, subs * rows), F32),
            shape((share * spaces // 128, lists * 128) if direct else (words, 128), F32),
        ],
        0,
        0,
        codebook,
        *messages,
        scratch=[
            pltpu.VMEM((words * depth, 128), F32),
            pltpu.VMEM((words // 128, width, 128), F32),
        ],
    )
    first = pieces[:-1] if direct else pieces
    slot, part = call(
        functools.partial(order_kernel, held, lists, direct, cap),
        [shape((rows, rows), F32), shape((subs * rows, width), BF16)],
        ORDER_FLOPS,
        0,
        tables,
        *first,
    )
    centre = part
    if direct:
        early_sums = call(
            functools.partial(early_sums_kernel, float((lists - 1) * cap)),
            shape((words, width), F32),
            2_000_000_000,
            0,
            codes_t,
            slot,
            part,
            *messages,
        )
        centre = call(
            functools.partial(order_rest_kernel, float((lists - 1) * cap)),
            shape((subs * rows, width), BF16),
            ORDER_REST_FLOPS,
            0,
            slot,
            part,
            pieces[-1],
            early_sums,
            loose=1,
        )
    rebuilt = call(
        functools.partial(place_kernel, direct, len(messages)),
        [shape((rows, width), BF16)] * subs
        if direct
        else [shape((subs, rows, width), BF16), shape((subs * rows, width), BF16)],
        0,
        0,
        centre,
        picked,
        *messages,
    )
    if not direct:
        rebuilt, residual = rebuilt[:1], rebuilt[1]
    rebuilt = exchange(rebuilt, "sub") if direct else [all_swap(rebuilt[0], "sub")]
    if direct:
        sums = call(
            functools.partial(late_sums_kernel, float((lists - 1) * cap)),
            [shape((width // 128 * share + share * spaces // 128, 128), BF16)] * lists,
            1_000_000_000,
            1_000_000,
            codes_t,
            slot,
            pieces[-1],
            early_sums,
            tally,
            *messages,
            rebuilt[1],
            loose=1,
            scratch=[pltpu.VMEM((words, width), F32)],
        )
    else:
        sums = call(
            sums_kernel,
            [shape((lists, share, width + 128), BF16)],
            2_000_000_000,
            1_000_000,
            codes_t,
            residual,
            tally,
            scratch=[pltpu.VMEM((words, width), F32)],
        )
    sums = exchange(sums, "lists", (3, 2, 1)) if direct else [all_swap(sums[0], "lists")]
    recon_error, token = call(
        functools.partial(restore_kernel, direct),
        [shape((rows, model), BF16), shape((8, 128), F32)],
        1_000,
        1_000,
        passages,
        rotation,
        *rebuilt,
        sums[3] if direct else sums[0],
        loose=1,
    )
    new_codebook = call(
        functools.partial(refine_kernel, spaces, direct),
        shape((spaces, share * depth), F32),
        100_000_000,
        500_000,
        codebook,
        *sums,
        token,
        loose=1,
        scratch=[pltpu.VMEM((width, share), F32)],
    )
    return (recon_error, new_codebook)


def solution(mesh):
    return jax.shard_map(
        body,
        mesh=mesh,
        in_specs=(
            P(("groups", "lists", "sub"), None),
            P(),
            P("lists", "sub"),
            P("groups"),
            P(("groups", "lists", "sub")),
            P(("groups", "lists", "sub"), None),
            P("sub", None),
        ),
        out_specs=(P(("groups", "lists", "sub"), None), P(("groups", "sub"), "lists")),
        check_vma=False,
    )
```

```python
import functools

import jax
import jax.numpy as jnp
from jax import lax
from jax.experimental import pallas as pl
from jax.experimental.pallas import tpu as pltpu
from jax.sharding import PartitionSpec as P

BF16 = jnp.bfloat16
F32 = jnp.float32
VMEM_LIMIT = 32 * 1024 * 1024
FETCH_FLOPS = 600_000_000
ORDER_FLOPS = 3_000_000_000
ORDER_REST_FLOPS = 12_000_000_000
TABLES_FLOPS = 8_000_000_000
DIRECT = 4


def call(kernel, out_shape, flops, nbytes, *args, scratch=(), loose=0, space=pl.ANY):
    whole = lambda: pl.BlockSpec(memory_space=pltpu.VMEM)
    return pl.pallas_call(
        kernel,
        out_shape=out_shape,
        in_specs=[whole() for _ in args[: len(args) - loose]]
        + [pl.BlockSpec(memory_space=space)] * loose,
        out_specs=jax.tree.map(lambda _: whole(), out_shape),
        scratch_shapes=list(scratch),
        compiler_params=pltpu.CompilerParams(vmem_limit_bytes=VMEM_LIMIT),
        cost_estimate=pl.CostEstimate(flops=flops, bytes_accessed=nbytes, transcendentals=0),
    )(*args)


def strict_before(width):
    row = lax.broadcasted_iota(jnp.int32, (width, width), 0)
    col = lax.broadcasted_iota(jnp.int32, (width, width), 1)
    return (row < col).astype(F32).astype(BF16)


def tables_kernel(ids_ref, slots_ref, out_ref):
    rows = ids_ref.shape[1]
    lines = slots_ref.shape[0]
    ids = jnp.transpose(jnp.concatenate([ids_ref[...].astype(F32)] * 128, axis=0))[:, :1]
    ids = ids.astype(jnp.int32)
    line = lax.broadcasted_iota(jnp.int32, (rows, lines), 1)
    chosen = (line == (ids >> 7)).astype(F32).astype(BF16)
    table = slots_ref[...]
    high = (table >> 8).astype(F32).astype(BF16)
    low = (table & 255).astype(F32).astype(BF16)
    found = jnp.dot(chosen, high, preferred_element_type=F32) * 256.0 + jnp.dot(
        chosen, low, preferred_element_type=F32
    )
    lane = lax.broadcasted_iota(jnp.int32, (rows, 128), 1)
    found = jnp.transpose(jnp.where(lane == (ids & 127), found, 0.0))
    line = jnp.sum(found, axis=0, keepdims=True).astype(jnp.int32)
    out_ref[...] = jnp.broadcast_to(line, out_ref.shape)


def rotate_kernel(subs, direct, passages_ref, rotation_ref, codes_ref, after_ref, *refs):
    outs, turned_ref = refs[:-1], refs[-1]
    rows, model = passages_ref.shape
    width = model // subs
    spaces = codes_ref.shape[1] // subs
    halves = width // rows
    tail = spaces // halves
    me = lax.axis_index("sub")
    turned_ref[...] = jnp.transpose(codes_ref[...].astype(F32))
    for step in range(subs):
        at = (me ^ step) if direct else step
        out = outs[step] if direct else outs[0].at[step]
        columns = pl.ds(pl.multiple_of(at * width, width), width)
        out[:rows, :] = jnp.dot(
            passages_ref[...], rotation_ref[:, columns], preferred_element_type=F32
        ).astype(BF16)
        for half in range(halves):
            start = pl.multiple_of(at * spaces + half * tail, tail)
            out[rows:, half * rows : (half + 1) * rows] = turned_ref[pl.ds(start, tail), :].astype(
                BF16
            )


def near_rows(rows_ref, owner, subs):
    me = lax.axis_index("sub")
    return jnp.concatenate(
        [rows_ref[pl.ds(owner * subs + (me ^ step), 1), :] for step in range(subs)], axis=0
    )


def index_slots(held, rows_refs, index_ref, spot_ref, move):
    blocks, cap = index_ref.shape
    rows = rows_refs[0].shape[1]
    group = min(cap, 16)
    me = lax.axis_index("lists")
    local = jnp.concatenate([ref[...] for ref in rows_refs], axis=0) - me * held
    mine = jnp.logical_and(local >= 0, local < held)
    flags = mine.astype(F32)
    rank = jnp.dot(flags.astype(BF16), strict_before(rows), preferred_element_type=F32)
    rank = jnp.where(mine, rank, -1.0)
    local = jnp.where(mine, local, 0)
    pad = max(128 // blocks, 1)
    rank = jnp.transpose(jnp.concatenate([rank] * pad, axis=0))
    local = jnp.transpose(jnp.concatenate([local.astype(F32)] * pad, axis=0))
    slot = lax.broadcasted_iota(jnp.int32, (rows, cap), 1).astype(F32)
    index = []
    for block in range(blocks):
        chosen = slot == rank[:, block : block + 1]
        index.append(
            jnp.sum(jnp.where(chosen, local[:, block : block + 1], 0.0), axis=0, keepdims=True)
        )
    index = jnp.concatenate(index, axis=0).astype(jnp.int32)
    index_ref[...] = index & -16
    move.start()
    within = lax.broadcasted_iota(jnp.int32, (blocks, cap), 1) & (group - 1)
    spot = (within * 16 + (index & 15)).astype(F32)
    spot_ref[...] = jnp.transpose(jnp.concatenate([spot] * pad, axis=0))


def fetch_blocks(first, spot_ref, scalar_ref, centroids_ref, out_ref):
    blocks, cap = out_ref.shape[0], out_ref.shape[1]
    group = min(cap, 16)
    lane = lax.broadcasted_iota(jnp.int32, (cap, group * 16), 1).astype(F32)
    for at in range(blocks):
        block = first + at
        chosen = (lane == spot_ref[:, block : block + 1]).astype(F32).astype(BF16)
        for start in range(0, cap, group):
            tiles = [
                centroids_ref[pl.ds(pl.multiple_of(scalar_ref[block, slot], 16), 16), :]
                for slot in range(start, start + group)
            ]
            out_ref[at, start : start + group, :] = jnp.dot(
                chosen[start : start + group],
                jnp.concatenate(tiles, axis=0),
                preferred_element_type=F32,
            ).astype(BF16)


def fetch_kernel(held, direct, rows_ref, centroids_ref, *refs):
    outs = refs[:-4]
    index_ref, spot_ref, scalar_ref, sem = refs[-4:]
    blocks = index_ref.shape[0]
    me = lax.axis_index("lists")
    if direct:
        lists = rows_ref.shape[0] // outs[0].shape[0]
        near = [near_rows(rows_ref, me ^ step, blocks // lists) for step in range(lists)]
    else:
        near = [rows_ref]
    move = pltpu.make_async_copy(index_ref, scalar_ref, sem)
    index_slots(held, near, index_ref, spot_ref, move)
    move.wait()
    for at, out in enumerate(outs):
        first = (at + 1) * out.shape[0] if direct else 0
        fetch_blocks(first, spot_ref, scalar_ref, centroids_ref, out)


def fetch_rest_kernel(steps, spot_ref, centroids_ref, scalar_ref, *outs):
    for step, out in zip(steps, outs):
        fetch_blocks(step * out.shape[0], spot_ref, scalar_ref, centroids_ref, out)


def lookup_kernel(direct, count, codebook_ref, *refs):
    messages, refs = refs[:count], refs[count:]
    picked_ref, codes_ref, tally_ref, turned_ref, words_ref = refs
    if not direct:
        messages = [messages[0].at[at] for at in range(messages[0].shape[0])]
    subs = len(messages)
    width = messages[0].shape[1]
    spaces = codes_ref.shape[0]
    rows = codes_ref.shape[1] // subs
    depth = width // spaces
    words = words_ref.shape[0] * 128
    halves = width // rows
    tail = spaces // halves
    for at in range(subs):
        for half in range(halves):
            codes_ref[half * tail : (half + 1) * tail, at * rows : (at + 1) * rows] = messages[at][
                rows:, half * rows : (half + 1) * rows
            ].astype(F32)
    for at in range(0, words * depth, 128):
        block = jnp.concatenate(
            [codebook_ref[:, at : at + 128].astype(F32)] * (128 // spaces), axis=0
        )
        turned_ref[at : at + 128, :] = jnp.transpose(block)
    for at in range(depth):
        block = jnp.transpose(turned_ref[pl.ds(at, words, stride=depth), :])
        for piece in range(words // 128):
            words_ref[piece, pl.ds(at, spaces, stride=depth), :] = block[
                :spaces, piece * 128 : (piece + 1) * 128
            ]
    parts = []
    for space in range(spaces):
        line = codes_ref[space : space + 1, :].astype(jnp.int32)
        cells = []
        for at in range(subs):
            index = jnp.broadcast_to(line[:, at * rows : (at + 1) * rows], (depth, rows))
            value = None
            for piece in range(words // 128):
                got = jnp.take_along_axis(
                    words_ref[piece, space * depth : (space + 1) * depth, :], index & 127, axis=1
                )
                value = got if value is None else jnp.where(index >= piece * 128, got, value)
            cells.append(value)
        parts.append(jnp.concatenate(cells, axis=1))
    picked_ref[...] = jnp.transpose(jnp.concatenate(parts, axis=0)).astype(BF16)
    if direct:
        low_words = words * spaces // tally_ref.shape[1]
        codes = codes_ref[...].astype(jnp.int32)
        high, low = codes // low_words, codes % low_words
        highs = [(high == at).astype(F32).astype(BF16) for at in range(words // low_words)]
        lows = [(low == at).astype(F32).astype(BF16) for at in range(low_words)]
        pairs = lax.dot_general(
            jnp.concatenate(lows, axis=0),
            jnp.concatenate(highs, axis=0),
            (((1,), (1,)), ((), ())),
            preferred_element_type=F32,
        )
        first = lax.broadcasted_iota(jnp.int32, pairs.shape, 0) % spaces
        second = lax.broadcasted_iota(jnp.int32, pairs.shape, 1) % spaces
        pairs = jnp.where(first == second, pairs, 0.0)
        tally_ref[...] = jnp.sum(pairs.reshape(low_words, spaces, pairs.shape[1]), axis=1)
        return
    tally = jnp.zeros((words, 128), F32)
    word = lax.broadcasted_iota(jnp.int32, (words, subs * rows), 0).astype(F32)
    lane = lax.broadcasted_iota(jnp.int32, (subs * rows, 128), 1)
    for space in range(spaces):
        hot = (word == codes_ref[space : space + 1, :]).astype(F32).astype(BF16)
        tally = tally + jnp.dot(
            hot, (lane == space).astype(F32).astype(BF16), preferred_element_type=F32
        )
    tally_ref[...] = tally


def in_order(slot_ref, at, start, pieces):
    rows = slot_ref.shape[0]
    total = sum(piece.shape[1] for piece in pieces)
    column = start + lax.broadcasted_iota(jnp.int32, (rows, total), 1).astype(F32)
    chosen = (column == slot_ref[:, at : at + 1]).astype(F32).astype(BF16)
    stacked = jnp.concatenate([piece[at] for piece in pieces], axis=0)
    return jnp.dot(chosen, stacked, preferred_element_type=F32)


def order_kernel(held, lists, direct, cap, rows_ref, *refs):
    pieces, (slot_ref, centre_ref) = refs[:-2], refs[-2:]
    rows = rows_ref.shape[1]
    subs = pieces[0].shape[0]
    me = lax.axis_index("lists")
    if direct:
        tables = near_rows(rows_ref, me, subs)
    else:
        tables = rows_ref[pl.ds(pl.multiple_of(me * subs, subs), subs), :]
    owners = tables // held
    rank = jnp.zeros((subs, rows), F32)
    flags = [(owners == at).astype(F32) for at in range(lists)]
    stacked = jnp.concatenate(flags, axis=0)
    before = jnp.dot(stacked.astype(BF16), strict_before(rows), preferred_element_type=F32)
    for at in range(lists):
        rank = rank + flags[at] * before[at * subs : (at + 1) * subs]
    place = (owners ^ me) if direct else owners
    slot = place.astype(F32) * cap + rank
    slot_ref[...] = jnp.transpose(jnp.concatenate([slot] * (rows // subs), axis=0))
    for at in range(subs):
        centre_ref[at * rows : (at + 1) * rows, :] = in_order(slot_ref, at, 0.0, pieces).astype(BF16)


def order_rest_kernel(start, slot_ref, part_ref, piece_ref, after_ref, centre_ref):
    rows = slot_ref.shape[0]
    for at in range(piece_ref.shape[0]):
        span = slice(at * rows, (at + 1) * rows)
        rest = in_order(slot_ref, at, start, [piece_ref])
        centre_ref[span, :] = (part_ref[span, :].astype(F32) + rest).astype(BF16)


def place_kernel(direct, count, centre_ref, picked_ref, *refs):
    messages, refs = refs[:count], refs[count:]
    if not direct:
        messages = [messages[0].at[at] for at in range(messages[0].shape[0])]
    subs = len(messages)
    rebuilt, residual_ref = (refs, None) if direct else (refs[:-1], refs[-1])
    rows = centre_ref.shape[0] // subs
    for at in range(subs):
        span = slice(at * rows, (at + 1) * rows)
        centre = centre_ref[span, :].astype(F32)
        out = rebuilt[at] if direct else rebuilt[0].at[at]
        out[...] = (centre + picked_ref[span, :].astype(F32)).astype(BF16)
        if not direct:
            residual_ref[span, :] = (messages[at][:rows, :].astype(F32) - centre).astype(BF16)


def add_words(total, codes, residual):
    spaces, rows = codes.shape
    words, width = total.shape
    depth = width // spaces
    word = lax.broadcasted_iota(jnp.int32, (words, rows), 0).astype(F32)
    owner = lax.broadcasted_iota(jnp.int32, (rows, width), 1) // depth
    for space in range(spaces):
        hot = (word == codes[space : space + 1, :]).astype(F32).astype(BF16)
        part = jnp.where(owner == space, residual, jnp.zeros_like(residual))
        total = total + jnp.dot(hot, part, preferred_element_type=F32)
    return total


def early_sums_kernel(limit, codes_ref, slot_ref, centre_ref, *refs):
    messages, out_ref = refs[:-1], refs[-1]
    rows = slot_ref.shape[0]
    residual = []
    for at, message in enumerate(messages):
        centre = centre_ref[at * rows : (at + 1) * rows, :].astype(F32)
        value = message[:rows, :].astype(F32) - centre
        residual.append(jnp.where(slot_ref[:, at : at + 1] < limit, value, 0.0).astype(BF16))
    total = jnp.zeros(out_ref.shape, F32)
    out_ref[...] = add_words(total, codes_ref[...], jnp.concatenate(residual, axis=0))


def late_sums_kernel(limit, codes_ref, slot_ref, piece_ref, early_ref, tally_ref, *refs):
    messages, outs, total_ref = refs[: piece_ref.shape[0]], refs[piece_ref.shape[0] + 1 : -1], refs[-1]
    rows = slot_ref.shape[0]
    subs, cap, width = piece_ref.shape
    column = limit + lax.broadcasted_iota(jnp.int32, (rows, cap), 1).astype(F32)
    residual, codes = [], []
    for at, message in enumerate(messages):
        chosen = (column == slot_ref[:, at : at + 1]).astype(F32)
        turned = jnp.transpose(chosen)
        used = jnp.sum(turned, axis=1, keepdims=True) > 0.0
        rotated = jnp.dot(turned.astype(BF16), message[:rows, :], preferred_element_type=F32)
        value = rotated - piece_ref[at].astype(F32)
        residual.append(jnp.where(used, value, 0.0).astype(BF16))
        own = codes_ref[:, at * rows : (at + 1) * rows].astype(BF16)
        codes.append(jnp.dot(own, chosen.astype(BF16), preferred_element_type=F32))
    residual = jnp.concatenate(residual, axis=0)
    total_ref[...] = add_words(early_ref[...], jnp.concatenate(codes, axis=1), residual)
    send_sums(True, total_ref, tally_ref, outs)


def sums_kernel(codes_ref, residual_ref, tally_ref, *refs):
    outs, total_ref = refs[:-1], refs[-1]
    total = jnp.zeros(total_ref.shape, F32)
    total_ref[...] = add_words(total, codes_ref[...], residual_ref[...])
    send_sums(False, total_ref, tally_ref, outs)


def send_sums(direct, total_ref, tally_ref, outs):
    words, width = total_ref.shape
    lists = lax.axis_size("lists")
    share = words // lists
    me = lax.axis_index("lists")
    for step in range(lists):
        out = outs[step] if direct else outs[0].at[step]
        at = (me ^ step) if direct else step
        span = pl.ds(pl.multiple_of(at * share, share), share)
        if direct:
            halves = width // 128
            for half in range(halves):
                out[half * share : (half + 1) * share, :] = total_ref[
                    span, half * 128 : (half + 1) * 128
                ].astype(BF16)
            lanes = pl.ds(pl.multiple_of(at * 128, 128), 128)
            out[halves * share :, :] = tally_ref[:, lanes].astype(BF16)
        else:
            out[:, :width] = total_ref[span, :].astype(BF16)
            out[:, width:] = tally_ref[span, :].astype(BF16)


def refine_kernel(spaces, direct, codebook_ref, *refs):
    pieces, (out_ref, turned_ref) = refs[:-3], refs[-2:]
    total = None
    for piece in pieces:
        if direct:
            value = piece[...].astype(F32)
        else:
            value = jnp.sum(piece[...].astype(F32), axis=0)
        total = value if total is None else total + value
    share, width = turned_ref.shape[1], turned_ref.shape[0]
    depth = width // spaces
    span = share * depth
    if direct:
        halves = width // 128
        fold = 128 // spaces
        for half in range(halves):
            turned_ref[half * 128 : (half + 1) * 128, :] = jnp.transpose(
                total[half * share : (half + 1) * share]
            )
        packed = jnp.transpose(total[halves * share :])
        tally = jnp.concatenate(
            [packed[at * spaces : (at + 1) * spaces] for at in range(fold)], axis=1
        )
    else:
        turned = jnp.transpose(total)
        turned_ref[...] = turned[:width, :]
        tally = turned[width : width + spaces, :]
    word = lax.broadcasted_iota(jnp.int32, (share, span), 0)
    cell = lax.broadcasted_iota(jnp.int32, (share, span), 1)

    def spread(value, table):
        high = value.astype(BF16)
        rest = value - high.astype(F32)
        low = rest.astype(BF16)
        return jnp.dot(high, table, preferred_element_type=F32) + jnp.dot(
            low, table, preferred_element_type=F32
        )

    sums = jnp.zeros((spaces, span), F32)
    for at in range(depth):
        table = (cell == word * depth + at).astype(F32).astype(BF16)
        sums = sums + spread(turned_ref[pl.ds(at, spaces, stride=depth), :], table)
    counts = spread(tally, (cell // depth == word).astype(F32).astype(BF16))
    me = lax.axis_index("lists")
    if span % 128 == 0:
        prior = codebook_ref[:, pl.ds(pl.multiple_of(me * span, span), span)].astype(F32)
    else:
        prior = jnp.zeros((spaces, span), F32)
        for at in range(codebook_ref.shape[1] // span):
            block = codebook_ref[:, at * span : (at + 1) * span].astype(F32)
            prior = prior + jnp.where(me == at, block, 0.0)
    out_ref[...] = (sums + prior) / (counts + 1.0)


def restore_kernel(direct, passages_ref, rotation_ref, *refs):
    pieces, (out_ref, token_ref) = refs[:-3], refs[-2:]
    token_ref[...] = jnp.zeros(token_ref.shape, F32)
    me = lax.axis_index("sub")
    if direct:
        blocks = [piece[...] for piece in pieces]
    else:
        blocks = [pieces[0][at] for at in range(pieces[0].shape[0])]
    width = blocks[0].shape[1]
    total = None
    for at, block in enumerate(blocks):
        start = (me ^ at) * width if direct else at * width
        if direct:
            start = pl.multiple_of(start, width)
        value = lax.dot_general(
            block,
            rotation_ref[:, pl.ds(start, width)],
            (((1,), (1,)), ((), ())),
            preferred_element_type=F32,
        )
        total = value if total is None else total + value
    out_ref[...] = (passages_ref[...].astype(F32) - total).astype(BF16)


def swap(value, axis, step):
    count = lax.axis_size(axis)
    return lax.ppermute(value, axis, [(at, at ^ step) for at in range(count)])


def exchange(values, axis, order=None):
    came = {0: values[0]}
    for step in order or range(1, len(values)):
        came[step] = swap(values[step], axis, step)
    return [came[step] for step in range(len(values))]


def all_swap(value, axis):
    return lax.all_to_all(value, axis, split_axis=0, concat_axis=0, tiled=True)


def body(passages, rotation, centroids, list_slot, list_ids, codes, codebook):
    lists = lax.axis_size("lists")
    subs = lax.axis_size("sub")
    rows, model = passages.shape
    held, width = centroids.shape
    cap = 2 * rows // lists
    spaces = codebook.shape[0]
    depth = width // spaces
    words = codebook.shape[1] // depth
    share = words // lists
    direct = max(lists, subs) <= DIRECT
    shape = jax.ShapeDtypeStruct

    tables = call(
        tables_kernel,
        shape((lists * subs, rows), jnp.int32),
        TABLES_FLOPS,
        0,
        list_ids.reshape(1, rows),
        list_slot.reshape(-1, 128),
    )
    own_tables = tables
    tables = all_swap(tables.reshape(lists * subs, 1, rows), ("lists", "sub"))
    tables = tables.reshape(lists * subs, rows)

    blocks = lists * subs
    scalars = [pltpu.SMEM((blocks, cap), jnp.int32), pltpu.SemaphoreType.DMA]
    early = lists // 2 if direct else 1
    *pieces, index, spot = call(
        functools.partial(fetch_kernel, held, direct),
        [shape((subs if direct else blocks, cap, width), BF16)] * early
        + [shape((blocks, cap), jnp.int32), shape((cap, max(blocks, 128)), F32)],
        FETCH_FLOPS,
        held * width * 2,
        tables,
        centroids,
        scratch=scalars,
    )
    fetched = pieces[0]
    if direct:
        late = list(range(early + 1, lists)) + [0]
        rest = call(
            functools.partial(fetch_rest_kernel, late),
            [shape((subs, cap, width), BF16)] * len(late),
            0,
            0,
            spot,
            centroids,
            index,
            loose=1,
            space=pltpu.SMEM,
        )
        fetched = rest[-1]
        pieces = exchange([fetched] + list(pieces) + list(rest[:-1]), "lists")
    else:
        found = all_swap(pieces[0].reshape(lists, subs * cap, width), "lists")
        found = found.reshape(lists, subs, cap, width)
        pieces = [jnp.swapaxes(found, 0, 1).reshape(subs, lists * cap, width)]

    long = rows + spaces // (width // rows)
    messages = call(
        functools.partial(rotate_kernel, subs, direct),
        [shape((long, width), BF16)] * subs if direct else [shape((subs, long, width), BF16)],
        0,
        0,
        passages,
        rotation,
        codes,
        fetched,
        loose=1,
        scratch=[pltpu.VMEM((codes.shape[1], rows), F32)],
    )
    messages = exchange(messages, "sub") if direct else [all_swap(messages[0], "sub")]

    picked, codes_t, tally = call(
        functools.partial(lookup_kernel, direct, len(messages)),
        [
            shape((subs * rows, width), BF16),
            shape((spaces, subs * rows), F32),
            shape((share * spaces // 128, lists * 128) if direct else (words, 128), F32),
        ],
        0,
        0,
        codebook,
        *messages,
        scratch=[
            pltpu.VMEM((words * depth, 128), F32),
            pltpu.VMEM((words // 128, width, 128), F32),
        ],
    )
    first = pieces[:-1] if direct else pieces
    slot, part = call(
        functools.partial(order_kernel, held, lists, direct, cap),
        [shape((rows, rows), F32), shape((subs * rows, width), BF16)],
        ORDER_FLOPS,
        0,
        tables,
        *first,
    )
    centre = part
    if direct:
        early_sums = call(
            functools.partial(early_sums_kernel, float((lists - 1) * cap)),
            shape((words, width), F32),
            2_000_000_000,
            0,
            codes_t,
            slot,
            part,
            *messages,
        )
        centre = call(
            functools.partial(order_rest_kernel, float((lists - 1) * cap)),
            shape((subs * rows, width), BF16),
            ORDER_REST_FLOPS,
            0,
            slot,
            part,
            pieces[-1],
            early_sums,
            loose=1,
        )
    rebuilt = call(
        functools.partial(place_kernel, direct, len(messages)),
        [shape((rows, width), BF16)] * subs
        if direct
        else [shape((subs, rows, width), BF16), shape((subs * rows, width), BF16)],
        0,
        0,
        centre,
        picked,
        *messages,
    )
    if not direct:
        rebuilt, residual = rebuilt[:1], rebuilt[1]
    rebuilt = exchange(rebuilt, "sub") if direct else [all_swap(rebuilt[0], "sub")]
    if direct:
        sums = call(
            functools.partial(late_sums_kernel, float((lists - 1) * cap)),
            [shape((width // 128 * share + share * spaces // 128, 128), BF16)] * lists,
            1_000_000_000,
            1_000_000,
            codes_t,
            slot,
            pieces[-1],
            early_sums,
            tally,
            *messages,
            rebuilt[1],
            loose=1,
            scratch=[pltpu.VMEM((words, width), F32)],
        )
    else:
        sums = call(
            sums_kernel,
            [shape((lists, share, width + 128), BF16)],
            2_000_000_000,
            1_000_000,
            codes_t,
            residual,
            tally,
            scratch=[pltpu.VMEM((words, width), F32)],
        )
    sums = exchange(sums, "lists", (3, 2, 1)) if direct else [all_swap(sums[0], "lists")]
    recon_error, token = call(
        functools.partial(restore_kernel, direct),
        [shape((rows, model), BF16), shape((8, 128), F32)],
        1_000,
        1_000,
        passages,
        rotation,
        *rebuilt,
        sums[3] if direct else sums[0],
        loose=1,
    )
    new_codebook = call(
        functools.partial(refine_kernel, spaces, direct),
        shape((spaces, share * depth), F32),
        100_000_000,
        500_000,
        codebook,
        *sums,
        token,
        loose=1,
        scratch=[pltpu.VMEM((width, share), F32)],
    )
    return (recon_error, new_codebook)


def solution(mesh):
    return jax.shard_map(
        body,
        mesh=mesh,
        in_specs=(
            P(("groups", "lists", "sub"), None),
            P(),
            P("lists", "sub"),
            P("groups"),
            P(("groups", "lists", "sub")),
            P(("groups", "lists", "sub"), None),
            P("sub", None),
        ),
        out_specs=(P(("groups", "lists", "sub"), None), P(("groups", "sub"), "lists")),
        check_vma=False,
    )
```

```python
import functools

import jax
import jax.numpy as jnp
from jax import lax
from jax.experimental import pallas as pl
from jax.experimental.pallas import tpu as pltpu
from jax.sharding import PartitionSpec as P

BF16 = jnp.bfloat16
F32 = jnp.float32
VMEM_LIMIT = 32 * 1024 * 1024
FETCH_FLOPS = 600_000_000
ORDER_FLOPS = 3_000_000_000
ORDER_REST_FLOPS = 12_000_000_000
TABLES_FLOPS = 8_000_000_000
DIRECT = 4


def call(kernel, out_shape, flops, nbytes, *args, scratch=(), loose=0, space=pl.ANY):
    whole = lambda: pl.BlockSpec(memory_space=pltpu.VMEM)
    return pl.pallas_call(
        kernel,
        out_shape=out_shape,
        in_specs=[whole() for _ in args[: len(args) - loose]]
        + [pl.BlockSpec(memory_space=space)] * loose,
        out_specs=jax.tree.map(lambda _: whole(), out_shape),
        scratch_shapes=list(scratch),
        compiler_params=pltpu.CompilerParams(vmem_limit_bytes=VMEM_LIMIT),
        cost_estimate=pl.CostEstimate(flops=flops, bytes_accessed=nbytes, transcendentals=0),
    )(*args)


def strict_before(width):
    row = lax.broadcasted_iota(jnp.int32, (width, width), 0)
    col = lax.broadcasted_iota(jnp.int32, (width, width), 1)
    return (row < col).astype(F32).astype(BF16)


def tables_kernel(ids_ref, slots_ref, out_ref):
    rows = ids_ref.shape[1]
    lines = slots_ref.shape[0]
    ids = jnp.transpose(jnp.concatenate([ids_ref[...].astype(F32)] * 128, axis=0))[:, :1]
    ids = ids.astype(jnp.int32)
    line = lax.broadcasted_iota(jnp.int32, (rows, lines), 1)
    chosen = (line == (ids >> 7)).astype(F32).astype(BF16)
    table = slots_ref[...]
    high = (table >> 8).astype(F32).astype(BF16)
    low = (table & 255).astype(F32).astype(BF16)
    found = jnp.dot(chosen, high, preferred_element_type=F32) * 256.0 + jnp.dot(
        chosen, low, preferred_element_type=F32
    )
    lane = lax.broadcasted_iota(jnp.int32, (rows, 128), 1)
    found = jnp.transpose(jnp.where(lane == (ids & 127), found, 0.0))
    line = jnp.sum(found, axis=0, keepdims=True).astype(jnp.int32)
    out_ref[...] = jnp.broadcast_to(line, out_ref.shape)


def rotate_kernel(subs, direct, passages_ref, rotation_ref, codes_ref, after_ref, *refs):
    outs, turned_ref = refs[:-1], refs[-1]
    rows, model = passages_ref.shape
    width = model // subs
    spaces = codes_ref.shape[1] // subs
    halves = width // rows
    tail = spaces // halves
    me = lax.axis_index("sub")
    turned_ref[...] = jnp.transpose(codes_ref[...].astype(F32))
    for step in range(subs):
        at = (me ^ step) if direct else step
        out = outs[step] if direct else outs[0].at[step]
        columns = pl.ds(pl.multiple_of(at * width, width), width)
        out[:rows, :] = jnp.dot(
            passages_ref[...], rotation_ref[:, columns], preferred_element_type=F32
        ).astype(BF16)
        for half in range(halves):
            start = pl.multiple_of(at * spaces + half * tail, tail)
            out[rows:, half * rows : (half + 1) * rows] = turned_ref[pl.ds(start, tail), :].astype(
                BF16
            )


def near_rows(rows_ref, owner, subs):
    me = lax.axis_index("sub")
    return jnp.concatenate(
        [rows_ref[pl.ds(owner * subs + (me ^ step), 1), :] for step in range(subs)], axis=0
    )


def index_slots(held, rows_refs, index_ref, spot_ref, move):
    blocks, cap = index_ref.shape
    rows = rows_refs[0].shape[1]
    group = min(cap, 16)
    me = lax.axis_index("lists")
    local = jnp.concatenate([ref[...] for ref in rows_refs], axis=0) - me * held
    mine = jnp.logical_and(local >= 0, local < held)
    flags = mine.astype(F32)
    rank = jnp.dot(flags.astype(BF16), strict_before(rows), preferred_element_type=F32)
    rank = jnp.where(mine, rank, -1.0)
    local = jnp.where(mine, local, 0)
    pad = max(128 // blocks, 1)
    rank = jnp.transpose(jnp.concatenate([rank] * pad, axis=0))
    local = jnp.transpose(jnp.concatenate([local.astype(F32)] * pad, axis=0))
    slot = lax.broadcasted_iota(jnp.int32, (rows, cap), 1).astype(F32)
    index = []
    for block in range(blocks):
        chosen = slot == rank[:, block : block + 1]
        index.append(
            jnp.sum(jnp.where(chosen, local[:, block : block + 1], 0.0), axis=0, keepdims=True)
        )
    index = jnp.concatenate(index, axis=0).astype(jnp.int32)
    index_ref[...] = index & -16
    move.start()
    within = lax.broadcasted_iota(jnp.int32, (blocks, cap), 1) & (group - 1)
    spot = (within * 16 + (index & 15)).astype(F32)
    spot_ref[...] = jnp.transpose(jnp.concatenate([spot] * pad, axis=0))


def fetch_blocks(first, spot_ref, scalar_ref, centroids_ref, out_ref):
    blocks, cap = out_ref.shape[0], out_ref.shape[1]
    group = min(cap, 16)
    lane = lax.broadcasted_iota(jnp.int32, (cap, group * 16), 1).astype(F32)
    for at in range(blocks):
        block = first + at
        chosen = (lane == spot_ref[:, block : block + 1]).astype(F32).astype(BF16)
        for start in range(0, cap, group):
            tiles = [
                centroids_ref[pl.ds(pl.multiple_of(scalar_ref[block, slot], 16), 16), :]
                for slot in range(start, start + group)
            ]
            out_ref[at, start : start + group, :] = jnp.dot(
                chosen[start : start + group],
                jnp.concatenate(tiles, axis=0),
                preferred_element_type=F32,
            ).astype(BF16)


def fetch_kernel(held, direct, rows_ref, centroids_ref, *refs):
    outs = refs[:-4]
    index_ref, spot_ref, scalar_ref, sem = refs[-4:]
    blocks = index_ref.shape[0]
    me = lax.axis_index("lists")
    if direct:
        lists = rows_ref.shape[0] // outs[0].shape[0]
        near = [near_rows(rows_ref, me ^ step, blocks // lists) for step in range(lists)]
    else:
        near = [rows_ref]
    move = pltpu.make_async_copy(index_ref, scalar_ref, sem)
    index_slots(held, near, index_ref, spot_ref, move)
    move.wait()
    for at, out in enumerate(outs):
        first = (at + 1) * out.shape[0] if direct else 0
        fetch_blocks(first, spot_ref, scalar_ref, centroids_ref, out)


def fetch_rest_kernel(steps, spot_ref, centroids_ref, scalar_ref, *outs):
    for step, out in zip(steps, outs):
        fetch_blocks(step * out.shape[0], spot_ref, scalar_ref, centroids_ref, out)


def lookup_kernel(direct, count, codebook_ref, *refs):
    messages, refs = refs[:count], refs[count:]
    picked_ref, codes_ref, tally_ref, turned_ref, words_ref = refs
    if not direct:
        messages = [messages[0].at[at] for at in range(messages[0].shape[0])]
    subs = len(messages)
    width = messages[0].shape[1]
    spaces = codes_ref.shape[0]
    rows = codes_ref.shape[1] // subs
    depth = width // spaces
    words = words_ref.shape[0] * 128
    halves = width // rows
    tail = spaces // halves
    for at in range(subs):
        for half in range(halves):
            codes_ref[half * tail : (half + 1) * tail, at * rows : (at + 1) * rows] = messages[at][
                rows:, half * rows : (half + 1) * rows
            ].astype(F32)
    for at in range(0, words * depth, 128):
        block = jnp.concatenate(
            [codebook_ref[:, at : at + 128].astype(F32)] * (128 // spaces), axis=0
        )
        turned_ref[at : at + 128, :] = jnp.transpose(block)
    for at in range(depth):
        block = jnp.transpose(turned_ref[pl.ds(at, words, stride=depth), :])
        for piece in range(words // 128):
            words_ref[piece, pl.ds(at, spaces, stride=depth), :] = block[
                :spaces, piece * 128 : (piece + 1) * 128
            ]
    parts = []
    for space in range(spaces):
        line = codes_ref[space : space + 1, :].astype(jnp.int32)
        cells = []
        for at in range(subs):
            index = jnp.broadcast_to(line[:, at * rows : (at + 1) * rows], (depth, rows))
            value = None
            for piece in range(words // 128):
                got = jnp.take_along_axis(
                    words_ref[piece, space * depth : (space + 1) * depth, :], index & 127, axis=1
                )
                value = got if value is None else jnp.where(index >= piece * 128, got, value)
            cells.append(value)
        parts.append(jnp.concatenate(cells, axis=1))
    picked_ref[...] = jnp.transpose(jnp.concatenate(parts, axis=0)).astype(BF16)
    if direct:
        low_words = words * spaces // tally_ref.shape[1]
        codes = codes_ref[...].astype(jnp.int32)
        high, low = codes // low_words, codes % low_words
        highs = [(high == at).astype(F32).astype(BF16) for at in range(words // low_words)]
        lows = [(low == at).astype(F32).astype(BF16) for at in range(low_words)]
        pairs = lax.dot_general(
            jnp.concatenate(lows, axis=0),
            jnp.concatenate(highs, axis=0),
            (((1,), (1,)), ((), ())),
            preferred_element_type=F32,
        )
        first = lax.broadcasted_iota(jnp.int32, pairs.shape, 0) % spaces
        second = lax.broadcasted_iota(jnp.int32, pairs.shape, 1) % spaces
        pairs = jnp.where(first == second, pairs, 0.0)
        tally_ref[...] = jnp.sum(pairs.reshape(low_words, spaces, pairs.shape[1]), axis=1)
        return
    tally = jnp.zeros((words, 128), F32)
    word = lax.broadcasted_iota(jnp.int32, (words, subs * rows), 0).astype(F32)
    lane = lax.broadcasted_iota(jnp.int32, (subs * rows, 128), 1)
    for space in range(spaces):
        hot = (word == codes_ref[space : space + 1, :]).astype(F32).astype(BF16)
        tally = tally + jnp.dot(
            hot, (lane == space).astype(F32).astype(BF16), preferred_element_type=F32
        )
    tally_ref[...] = tally


def in_order(slot_ref, at, start, pieces):
    rows = slot_ref.shape[0]
    total = sum(piece.shape[1] for piece in pieces)
    column = start + lax.broadcasted_iota(jnp.int32, (rows, total), 1).astype(F32)
    chosen = (column == slot_ref[:, at : at + 1]).astype(F32).astype(BF16)
    stacked = jnp.concatenate([piece[at] for piece in pieces], axis=0)
    return jnp.dot(chosen, stacked, preferred_element_type=F32)


def order_kernel(held, lists, direct, cap, rows_ref, *refs):
    pieces, (slot_ref, centre_ref) = refs[:-2], refs[-2:]
    rows = rows_ref.shape[1]
    subs = pieces[0].shape[0]
    me = lax.axis_index("lists")
    if direct:
        tables = near_rows(rows_ref, me, subs)
    else:
        tables = rows_ref[pl.ds(pl.multiple_of(me * subs, subs), subs), :]
    owners = tables // held
    rank = jnp.zeros((subs, rows), F32)
    flags = [(owners == at).astype(F32) for at in range(lists)]
    stacked = jnp.concatenate(flags, axis=0)
    before = jnp.dot(stacked.astype(BF16), strict_before(rows), preferred_element_type=F32)
    for at in range(lists):
        rank = rank + flags[at] * before[at * subs : (at + 1) * subs]
    place = (owners ^ me) if direct else owners
    slot = place.astype(F32) * cap + rank
    slot_ref[...] = jnp.transpose(jnp.concatenate([slot] * (rows // subs), axis=0))
    for at in range(subs):
        centre_ref[at * rows : (at + 1) * rows, :] = in_order(slot_ref, at, 0.0, pieces).astype(BF16)


def order_rest_kernel(start, slot_ref, part_ref, piece_ref, after_ref, centre_ref):
    rows = slot_ref.shape[0]
    for at in range(piece_ref.shape[0]):
        span = slice(at * rows, (at + 1) * rows)
        rest = in_order(slot_ref, at, start, [piece_ref])
        centre_ref[span, :] = (part_ref[span, :].astype(F32) + rest).astype(BF16)


def place_kernel(direct, count, centre_ref, picked_ref, *refs):
    messages, refs = refs[:count], refs[count:]
    if not direct:
        messages = [messages[0].at[at] for at in range(messages[0].shape[0])]
    subs = len(messages)
    rebuilt, residual_ref = (refs, None) if direct else (refs[:-1], refs[-1])
    rows = centre_ref.shape[0] // subs
    for at in range(subs):
        span = slice(at * rows, (at + 1) * rows)
        centre = centre_ref[span, :].astype(F32)
        out = rebuilt[at] if direct else rebuilt[0].at[at]
        out[...] = (centre + picked_ref[span, :].astype(F32)).astype(BF16)
        if not direct:
            residual_ref[span, :] = (messages[at][:rows, :].astype(F32) - centre).astype(BF16)


def add_words(total, codes, residual):
    spaces, rows = codes.shape
    words, width = total.shape
    depth = width // spaces
    word = lax.broadcasted_iota(jnp.int32, (words, rows), 0).astype(F32)
    owner = lax.broadcasted_iota(jnp.int32, (rows, width), 1) // depth
    for space in range(spaces):
        hot = (word == codes[space : space + 1, :]).astype(F32).astype(BF16)
        part = jnp.where(owner == space, residual, jnp.zeros_like(residual))
        total = total + jnp.dot(hot, part, preferred_element_type=F32)
    return total


def early_sums_kernel(limit, codes_ref, slot_ref, centre_ref, *refs):
    messages, (out_ref, rotated_ref, used_ref, picks_ref) = refs[:-4], refs[-4:]
    rows = slot_ref.shape[0]
    cap = rotated_ref.shape[0] // len(messages)
    column = limit + lax.broadcasted_iota(jnp.int32, (rows, cap), 1).astype(F32)
    picks = []
    for at, message in enumerate(messages):
        chosen = (column == slot_ref[:, at : at + 1]).astype(F32)
        turned = jnp.transpose(chosen)
        span = slice(at * cap, (at + 1) * cap)
        used = jnp.sum(turned, axis=1, keepdims=True)
        used_ref[span, :] = jnp.broadcast_to(used, (cap, 128))
        rotated_ref[span, :] = jnp.dot(
            turned.astype(BF16), message[:rows, :], preferred_element_type=F32
        )
        own = codes_ref[:, at * rows : (at + 1) * rows].astype(BF16)
        picks.append(jnp.dot(own, chosen.astype(BF16), preferred_element_type=F32))
    picks_ref[...] = jnp.concatenate(picks, axis=1)
    residual = []
    for at, message in enumerate(messages):
        centre = centre_ref[at * rows : (at + 1) * rows, :].astype(F32)
        value = message[:rows, :].astype(F32) - centre
        residual.append(jnp.where(slot_ref[:, at : at + 1] < limit, value, 0.0).astype(BF16))
    total = jnp.zeros(out_ref.shape, F32)
    out_ref[...] = add_words(total, codes_ref[...], jnp.concatenate(residual, axis=0))


def late_sums_kernel(piece_ref, early_ref, rotated_ref, used_ref, picks_ref, tally_ref, *refs):
    outs, total_ref = refs[1:-1], refs[-1]
    subs, cap, width = piece_ref.shape
    residual = []
    for at in range(subs):
        span = slice(at * cap, (at + 1) * cap)
        value = rotated_ref[span, :] - piece_ref[at].astype(F32)
        residual.append(jnp.where(used_ref[span, :1] > 0.0, value, 0.0).astype(BF16))
    residual = jnp.concatenate(residual, axis=0)
    total_ref[...] = add_words(early_ref[...], picks_ref[...], residual)
    send_sums(True, total_ref, tally_ref, outs)


def sums_kernel(codes_ref, residual_ref, tally_ref, *refs):
    outs, total_ref = refs[:-1], refs[-1]
    total = jnp.zeros(total_ref.shape, F32)
    total_ref[...] = add_words(total, codes_ref[...], residual_ref[...])
    send_sums(False, total_ref, tally_ref, outs)


def send_sums(direct, total_ref, tally_ref, outs):
    words, width = total_ref.shape
    lists = lax.axis_size("lists")
    share = words // lists
    me = lax.axis_index("lists")
    for step in range(lists):
        out = outs[step] if direct else outs[0].at[step]
        at = (me ^ step) if direct else step
        span = pl.ds(pl.multiple_of(at * share, share), share)
        if direct:
            halves = width // 128
            for half in range(halves):
                out[half * share : (half + 1) * share, :] = total_ref[
                    span, half * 128 : (half + 1) * 128
                ].astype(BF16)
            lanes = pl.ds(pl.multiple_of(at * 128, 128), 128)
            out[halves * share :, :] = tally_ref[:, lanes].astype(BF16)
        else:
            out[:, :width] = total_ref[span, :].astype(BF16)
            out[:, width:] = tally_ref[span, :].astype(BF16)


def refine_kernel(spaces, direct, codebook_ref, *refs):
    pieces, (out_ref, turned_ref) = refs[:-3], refs[-2:]
    total = None
    for piece in pieces:
        if direct:
            value = piece[...].astype(F32)
        else:
            value = jnp.sum(piece[...].astype(F32), axis=0)
        total = value if total is None else total + value
    share, width = turned_ref.shape[1], turned_ref.shape[0]
    depth = width // spaces
    span = share * depth
    if direct:
        halves = width // 128
        fold = 128 // spaces
        for half in range(halves):
            turned_ref[half * 128 : (half + 1) * 128, :] = jnp.transpose(
                total[half * share : (half + 1) * share]
            )
        packed = jnp.transpose(total[halves * share :])
        tally = jnp.concatenate(
            [packed[at * spaces : (at + 1) * spaces] for at in range(fold)], axis=1
        )
    else:
        turned = jnp.transpose(total)
        turned_ref[...] = turned[:width, :]
        tally = turned[width : width + spaces, :]
    word = lax.broadcasted_iota(jnp.int32, (share, span), 0)
    cell = lax.broadcasted_iota(jnp.int32, (share, span), 1)

    def spread(value, table):
        high = value.astype(BF16)
        rest = value - high.astype(F32)
        low = rest.astype(BF16)
        return jnp.dot(high, table, preferred_element_type=F32) + jnp.dot(
            low, table, preferred_element_type=F32
        )

    sums = jnp.zeros((spaces, span), F32)
    for at in range(depth):
        table = (cell == word * depth + at).astype(F32).astype(BF16)
        sums = sums + spread(turned_ref[pl.ds(at, spaces, stride=depth), :], table)
    counts = spread(tally, (cell // depth == word).astype(F32).astype(BF16))
    me = lax.axis_index("lists")
    if span % 128 == 0:
        prior = codebook_ref[:, pl.ds(pl.multiple_of(me * span, span), span)].astype(F32)
    else:
        prior = jnp.zeros((spaces, span), F32)
        for at in range(codebook_ref.shape[1] // span):
            block = codebook_ref[:, at * span : (at + 1) * span].astype(F32)
            prior = prior + jnp.where(me == at, block, 0.0)
    out_ref[...] = (sums + prior) / (counts + 1.0)


def restore_kernel(direct, passages_ref, rotation_ref, *refs):
    pieces, (out_ref, token_ref) = refs[:-3], refs[-2:]
    token_ref[...] = jnp.zeros(token_ref.shape, F32)
    me = lax.axis_index("sub")
    if direct:
        blocks = [piece[...] for piece in pieces]
    else:
        blocks = [pieces[0][at] for at in range(pieces[0].shape[0])]
    width = blocks[0].shape[1]
    total = None
    for at, block in enumerate(blocks):
        start = (me ^ at) * width if direct else at * width
        if direct:
            start = pl.multiple_of(start, width)
        value = lax.dot_general(
            block,
            rotation_ref[:, pl.ds(start, width)],
            (((1,), (1,)), ((), ())),
            preferred_element_type=F32,
        )
        total = value if total is None else total + value
    out_ref[...] = (passages_ref[...].astype(F32) - total).astype(BF16)


def swap(value, axis, step):
    count = lax.axis_size(axis)
    return lax.ppermute(value, axis, [(at, at ^ step) for at in range(count)])


def exchange(values, axis, order=None):
    came = {0: values[0]}
    for step in order or range(1, len(values)):
        came[step] = swap(values[step], axis, step)
    return [came[step] for step in range(len(values))]


def all_swap(value, axis):
    return lax.all_to_all(value, axis, split_axis=0, concat_axis=0, tiled=True)


def body(passages, rotation, centroids, list_slot, list_ids, codes, codebook):
    lists = lax.axis_size("lists")
    subs = lax.axis_size("sub")
    rows, model = passages.shape
    held, width = centroids.shape
    cap = 2 * rows // lists
    spaces = codebook.shape[0]
    depth = width // spaces
    words = codebook.shape[1] // depth
    share = words // lists
    direct = max(lists, subs) <= DIRECT
    shape = jax.ShapeDtypeStruct

    tables = call(
        tables_kernel,
        shape((lists * subs, rows), jnp.int32),
        TABLES_FLOPS,
        0,
        list_ids.reshape(1, rows),
        list_slot.reshape(-1, 128),
    )
    own_tables = tables
    tables = all_swap(tables.reshape(lists * subs, 1, rows), ("lists", "sub"))
    tables = tables.reshape(lists * subs, rows)

    blocks = lists * subs
    scalars = [pltpu.SMEM((blocks, cap), jnp.int32), pltpu.SemaphoreType.DMA]
    early = lists // 2 if direct else 1
    *pieces, index, spot = call(
        functools.partial(fetch_kernel, held, direct),
        [shape((subs if direct else blocks, cap, width), BF16)] * early
        + [shape((blocks, cap), jnp.int32), shape((cap, max(blocks, 128)), F32)],
        FETCH_FLOPS,
        held * width * 2,
        tables,
        centroids,
        scratch=scalars,
    )
    fetched = pieces[0]
    if direct:
        late = list(range(early + 1, lists)) + [0]
        rest = call(
            functools.partial(fetch_rest_kernel, late),
            [shape((subs, cap, width), BF16)] * len(late),
            0,
            0,
            spot,
            centroids,
            index,
            loose=1,
            space=pltpu.SMEM,
        )
        fetched = rest[-1]
        pieces = exchange([fetched] + list(pieces) + list(rest[:-1]), "lists")
    else:
        found = all_swap(pieces[0].reshape(lists, subs * cap, width), "lists")
        found = found.reshape(lists, subs, cap, width)
        pieces = [jnp.swapaxes(found, 0, 1).reshape(subs, lists * cap, width)]

    long = rows + spaces // (width // rows)
    messages = call(
        functools.partial(rotate_kernel, subs, direct),
        [shape((long, width), BF16)] * subs if direct else [shape((subs, long, width), BF16)],
        0,
        0,
        passages,
        rotation,
        codes,
        fetched,
        loose=1,
        scratch=[pltpu.VMEM((codes.shape[1], rows), F32)],
    )
    messages = exchange(messages, "sub") if direct else [all_swap(messages[0], "sub")]

    picked, codes_t, tally = call(
        functools.partial(lookup_kernel, direct, len(messages)),
        [
            shape((subs * rows, width), BF16),
            shape((spaces, subs * rows), F32),
            shape((share * spaces // 128, lists * 128) if direct else (words, 128), F32),
        ],
        0,
        0,
        codebook,
        *messages,
        scratch=[
            pltpu.VMEM((words * depth, 128), F32),
            pltpu.VMEM((words // 128, width, 128), F32),
        ],
    )
    first = pieces[:-1] if direct else pieces
    slot, part = call(
        functools.partial(order_kernel, held, lists, direct, cap),
        [shape((rows, rows), F32), shape((subs * rows, width), BF16)],
        ORDER_FLOPS,
        0,
        tables,
        *first,
    )
    centre = part
    if direct:
        early_sums, *far = call(
            functools.partial(early_sums_kernel, float((lists - 1) * cap)),
            [
                shape((words, width), F32),
                shape((subs * cap, width), F32),
                shape((subs * cap, 128), F32),
                shape((spaces, subs * cap), F32),
            ],
            2_000_000_000,
            0,
            codes_t,
            slot,
            part,
            *messages,
        )
        centre = call(
            functools.partial(order_rest_kernel, float((lists - 1) * cap)),
            shape((subs * rows, width), BF16),
            ORDER_REST_FLOPS,
            0,
            slot,
            part,
            pieces[-1],
            early_sums,
            loose=1,
        )
    rebuilt = call(
        functools.partial(place_kernel, direct, len(messages)),
        [shape((rows, width), BF16)] * subs
        if direct
        else [shape((subs, rows, width), BF16), shape((subs * rows, width), BF16)],
        0,
        0,
        centre,
        picked,
        *messages,
    )
    if not direct:
        rebuilt, residual = rebuilt[:1], rebuilt[1]
    rebuilt = exchange(rebuilt, "sub") if direct else [all_swap(rebuilt[0], "sub")]
    if direct:
        sums = call(
            late_sums_kernel,
            [shape((width // 128 * share + share * spaces // 128, 128), BF16)] * lists,
            1_000_000_000,
            1_000_000,
            pieces[-1],
            early_sums,
            *far,
            tally,
            rebuilt[1],
            loose=1,
            scratch=[pltpu.VMEM((words, width), F32)],
        )
    else:
        sums = call(
            sums_kernel,
            [shape((lists, share, width + 128), BF16)],
            2_000_000_000,
            1_000_000,
            codes_t,
            residual,
            tally,
            scratch=[pltpu.VMEM((words, width), F32)],
        )
    sums = exchange(sums, "lists", (3, 2, 1)) if direct else [all_swap(sums[0], "lists")]
    recon_error, token = call(
        functools.partial(restore_kernel, direct),
        [shape((rows, model), BF16), shape((8, 128), F32)],
        1_000,
        1_000,
        passages,
        rotation,
        *rebuilt,
        sums[3] if direct else sums[0],
        loose=1,
    )
    new_codebook = call(
        functools.partial(refine_kernel, spaces, direct),
        shape((spaces, share * depth), F32),
        100_000_000,
        500_000,
        codebook,
        *sums,
        token,
        loose=1,
        scratch=[pltpu.VMEM((width, share), F32)],
    )
    return (recon_error, new_codebook)


def solution(mesh):
    return jax.shard_map(
        body,
        mesh=mesh,
        in_specs=(
            P(("groups", "lists", "sub"), None),
            P(),
            P("lists", "sub"),
            P("groups"),
            P(("groups", "lists", "sub")),
            P(("groups", "lists", "sub"), None),
            P("sub", None),
        ),
        out_specs=(P(("groups", "lists", "sub"), None), P(("groups", "sub"), "lists")),
        check_vma=False,
    )
```
